32 devices in a mesh: dp: 2 (over core), fsdp: 16 (over z, y, x).
Axes of the slice: x: 2, y: 2, z: 4, core: 2. Of those that a mesh axis runs over, the one named last changes fastest.
Arguments:
- tokens: bfloat16 [32768, 768], P(('dp', 'fsdp')), may hold values from -6 to 6
- cotangent: bfloat16 [32768, 768], P(('dp', 'fsdp')), may hold values from -6 to 6
- master_slots: float32 [18432, 768], P('fsdp'), as said below
- first_slots: float32 [18432, 768], P('fsdp')
- second_slots: float32 [18432, 768], P('fsdp')
- norm_gains: float32 [2, 768], replicated, may hold values from 0.5 to 1.5
- gains_first: float32 [2, 768], replicated, may hold values from -1086.116 to 1086.116
- gains_second: float32 [2, 768], replicated, may hold values from 10922 to 43690
- bias_table: float32 [32, 12], replicated, may hold values from -4 to 4
- table_first: float32 [32, 12], replicated, may hold values from -1086.116 to 1086.116
- table_second: float32 [32, 12], replicated, may hold values from 10922 to 43690
- bucket_ids: int32 [1023], replicated, may hold values from 0 to 31
- valid_len: int32 [64], P(('dp', 'fsdp')), may hold values from 128 to 512, as said below
- task_sizes: int32 [40], replicated, may hold values from 1 to 4, 64 in all
- owner_list: int32 [1152], replicated, may hold values from 0 to 15, as said below
Outputs:
- block_out: bfloat16 [32768, 768], P(('dp', 'fsdp'))
- grad_input: float32 [32768, 768], P(('dp', 'fsdp'))
- grad_slots: float32 [18432, 768], P('fsdp')
- grad_gains: float32 [2, 768], replicated
- grad_table: float32 [32, 12], replicated
- first_new: float32 [18432, 768], P('fsdp')
- second_new: float32 [18432, 768], P('fsdp')
- master_new: float32 [18432, 768], P('fsdp')
- master_copy: bfloat16 [18432, 768], P('fsdp')
- gains_first_new: float32 [2, 768], replicated
- gains_second_new: float32 [2, 768], replicated
- gains_new: float32 [2, 768], replicated
- table_first_new: float32 [32, 12], replicated
- table_second_new: float32 [32, 12], replicated
- table_new: float32 [32, 12], replicated
The draws below stay inside these ranges and needn't reach their ends.
Inputs may be any that keep to these rules, and one draw needn't show every extreme that they name: `owner_list`: each block's owner along fsdp; no device owns more than 144 blocks, and one device owns exactly 144. Range r is blocks r * 72 to r * 72 + 71; no owner holds more than 9 blocks of one range, and some owner holds exactly 9 of some range. `valid_len`: some sequence is unpadded. `task_sizes`: they add up to 64. `bucket_ids`: entry j - i + 511 is the bucket of key j seen from query i. `master_slots`: unoccupied slots hold values too.
All inputs are finite; a program needn't handle non-finite values.
Results may differ from the reference program's by a relative error of at most 0.014.
The reference program's roundings to bfloat16 on the way count: a program that leaves them out, or rounds other values in their place, can miss the bound.
Values may be sent and summed in bfloat16 or wider, within the bound.
A program may use at most 320 MiB of HBM per device.

```python
import math
from functools import partial
import jax
import jax.numpy as jnp
import numpy as np
from jax import lax

D = 768
HEADS = 12
HEAD_DIM = 64
FF = 3072
BUCKETS = 32
LEN = 512
BROWS = 8
OPT_STEP = 3
NB = 1152
CAP = 144
SEQS = 64
TASKS = 40
TOKENS = 32768
N_FSDP = 16


def owner_blocks(key):
    inner_key = jax.random.fold_in(key, 7)
    key_full, key_rest, key_range, key_inner = jax.random.split(inner_key, 4)
    full_owner = jax.random.randint(key_full, (), 0, N_FSDP)
    others = jax.random.permutation(key_rest, N_FSDP * CAP - CAP)[:NB - CAP]
    others = others + jnp.where(others >= full_owner * CAP, CAP, 0)
    chosen = jnp.concatenate([full_owner * CAP + jnp.arange(CAP, dtype=jnp.int32), others.astype(jnp.int32)])
    owners_sorted = jnp.sort(chosen // CAP).astype(jnp.int32)
    positions = jnp.arange(NB, dtype=jnp.int32)
    range_order = jax.random.permutation(key_range, N_FSDP).astype(jnp.int32)
    inner_order = jax.random.permutation(key_inner, NB // N_FSDP).astype(jnp.int32)
    block_of = range_order[positions % N_FSDP] * (NB // N_FSDP) + inner_order[positions // N_FSDP]
    return jnp.zeros((NB,), jnp.int32).at[block_of].set(owners_sorted)


def slot_factor(key, factors):
    owner_list = owner_blocks(key)
    onehot = (owner_list[:, None] == jnp.arange(N_FSDP, dtype=jnp.int32)[None, :]).astype(jnp.int32)
    rank_in = jnp.sum((jnp.cumsum(onehot, axis=0) - onehot) * onehot, axis=1)
    slot_of = owner_list * CAP + rank_in
    bounds = jnp.array([D, 2 * D, 3 * D, 4 * D, 4 * D + FF], jnp.int32)
    block_rows = jnp.arange(NB, dtype=jnp.int32) * BROWS
    kind_of = jnp.sum((block_rows[:, None] >= bounds[None, :]).astype(jnp.int32), axis=1)
    per_block = jnp.array(factors, jnp.float32)[kind_of]
    per_slot = jnp.full((N_FSDP * CAP,), factors[0], jnp.float32).at[slot_of].set(per_block)
    return jnp.repeat(per_slot, BROWS)[:, None]


def base_values(key):
    return jax.random.normal(key, (N_FSDP * CAP * BROWS, D), jnp.float32)


def draw_owner_list(key, part):
    return owner_blocks(key)


def draw_master_slots(key, part):
    query_std = math.sqrt(1.2) * HEAD_DIM ** (-0.25) / math.sqrt(D)
    drawn_std = 1.0 / math.sqrt(D)
    factors = [query_std, query_std, drawn_std, math.sqrt(LEN / 8.0) * drawn_std, drawn_std, math.sqrt(2.0 / FF)]
    return base_values(jax.random.fold_in(key, 11)) * slot_factor(key, factors)


def grad_factors():
    typical = math.sqrt(TOKENS)
    return [4.0 * typical, 4.0 * typical, 1.5 * typical, 0.2 * typical, typical, 0.7 * typical]


def draw_first_slots(key, part):
    return base_values(jax.random.fold_in(key, 13)) * slot_factor(key, grad_factors())


def draw_second_slots(key, part):
    squares = [value * value / 3.0 for value in grad_factors()]
    spread_key = jax.random.fold_in(key, 17)
    spread = jnp.exp(jax.random.uniform(spread_key, (N_FSDP * CAP * BROWS, D), jnp.float32, 0.0, math.log(4.0)))
    return spread * slot_factor(key, squares)


def draw_valid_len(key, part):
    key_len, key_pick = jax.random.split(jax.random.fold_in(key, 3))
    lengths = jax.random.randint(key_len, (SEQS,), LEN // 4, LEN + 1)
    pick_index = jax.random.randint(key_pick, (), 0, SEQS)
    return lengths.at[pick_index].set(LEN).astype(jnp.int32)


def touch_ends(values, key, smallest, top_value):
    longest = values.shape.index(max(values.shape))
    spots = []
    for shift in (0, 1):
        where = [jax.random.randint(jax.random.fold_in(key, axis), (), 0, length) for axis, length in enumerate(values.shape)]
        where[longest] = (where[longest] + shift) % values.shape[longest]
        spots.append(tuple(where))
    return values.at[spots[0]].set(smallest).at[spots[1]].set(top_value)


def shard_levels(rng, shape, shards, smallest, largest):
    gain, own = 1.0, jax.random.fold_in(rng, 6)
    for dim, parts in shards:
        draws = jnp.exp(jax.random.uniform(jax.random.fold_in(own, dim), (parts,), jnp.float32, smallest / len(shards), largest / len(shards)))
        gain = gain * jnp.repeat(draws, shape[dim] // parts).reshape([-1 if axis == dim else 1 for axis in range(len(shape))])
    return gain


def length_profile(number_of, total, bound, lean):
    loads = [(1 << 20) // math.isqrt(rank ** lean) + 1 for rank in range(2, number_of + 1)]
    rest, counts = total - bound - (number_of - 1), [1] * (number_of - 1)
    while rest > 0:
        movable = [i for i in range(number_of - 1) if counts[i] < bound]
        mass, remaining = sum([loads[i] for i in movable]), rest
        for i in movable:
            extra = min(bound - counts[i], max(1, remaining * loads[i] // mass), rest)
            counts[i] = counts[i] + extra
            rest = rest - extra
    return np.array([bound] + counts)


def ragged(stream_key, amount, total, reach, lean):
    if amount == 2:
        one = jax.random.randint(stream_key, (), max(1, total - reach), min(reach, total - 1) + 1)
        return jnp.stack([one, total - one])
    sizes = jnp.asarray(length_profile(amount, total, reach, lean), jnp.int32)
    pairs = (amount - 1) // 2
    donor, receiver = sizes[1:1 + 2 * pairs:2], sizes[2:2 + 2 * pairs:2]
    slack = jnp.minimum(donor - 1, reach - receiver)
    shifted = jax.random.randint(jax.random.fold_in(stream_key, 1), (pairs,), 0, 1 << 20) % (slack + 1)
    sizes = sizes.at[1:1 + 2 * pairs:2].set(donor - shifted).at[2:2 + 2 * pairs:2].set(receiver + shifted)
    return sizes[jax.random.permutation(jax.random.fold_in(stream_key, 2), amount)]


def noise(own_key, extent, scale, limit, cuts=(), kind=jnp.bfloat16):
    values = scale * jax.random.normal(own_key, extent, jnp.float32)
    if cuts:
        values = values * shard_levels(own_key, extent, cuts, -0.22, 0.18)
    return jnp.clip(values, -limit, limit).astype(kind)


def setup_inputs(seed: int = 0) -> dict:
    keys = jax.random.split(jax.random.key(seed), 16)
    return {
        "tokens": noise(keys[0], (TOKENS, D), 1.0, 6.0, ((0, 32),)),
        "cotangent": noise(keys[1], (TOKENS, D), 1.0, 6.0, ((0, 32),)),
        "master_slots": draw_master_slots(jax.random.fold_in(keys[15], 71), 0),
        "first_slots": draw_first_slots(jax.random.fold_in(keys[15], 71), 0),
        "second_slots": draw_second_slots(jax.random.fold_in(keys[15], 71), 0),
        "norm_gains": jnp.clip(1.0 + 0.1 * jax.random.normal(keys[5], (2, D), jnp.float32), 0.5, 1.5),
        "gains_first": noise(keys[6], (2, D), (TOKENS ** 0.5), 1086.116, (), jnp.float32),
        "gains_second": jnp.clip(jnp.exp(jax.random.uniform(keys[7], (2, D), jnp.float32, math.log(10922.0), math.log(43690.0))), 10922.0, 43690.0),
        "bias_table": noise(keys[8], (BUCKETS, HEADS), 0.8, 4.0, (), jnp.float32),
        "table_first": noise(keys[9], (BUCKETS, HEADS), (TOKENS ** 0.5), 1086.116, (), jnp.float32),
        "table_second": jnp.clip(jnp.exp(jax.random.uniform(keys[10], (BUCKETS, HEADS), jnp.float32, math.log(10922.0), math.log(43690.0))), 10922.0, 43690.0),
        "bucket_ids": touch_ends(jax.random.randint(keys[11], (2 * LEN - 1,), 0, BUCKETS), jax.random.fold_in(keys[11], 1), 0, BUCKETS - 1).astype(jnp.int32),
        "valid_len": draw_valid_len(jax.random.fold_in(keys[15], 71), 0),
        "task_sizes": ragged(keys[13], TASKS, SEQS, 4, 2).astype(jnp.int32),
        "owner_list": draw_owner_list(jax.random.fold_in(keys[15], 71), 0),
    }


EPS_NORM = 1e-06
BETA_ONE = 0.5
BETA_TWO = 0.75
LEARN_RATE = 0.06
SMALL_RATE = 0.4
WEIGHT_DECAY = 0.01
EPS_ADAM = 1e-08
NEG_FILL = -1e+30
HIGHEST = lax.Precision.HIGHEST

@jax.custom_vjp
def low(v):
    return lax.optimization_barrier(v.astype(jnp.bfloat16)).astype(jnp.float32)

@jax.custom_vjp
def low_back(v):
    return v

def low_keep(v):
    return (low(v), None)

def low_pass(kept, grad):
    return (grad,)

def back_keep(v):
    return (v, None)

def back_low(kept, grad):
    return (low(grad),)
low.defvjp(low_keep, low_pass)
low_back.defvjp(back_keep, back_low)

def matmul(left_side, right_side):
    return jnp.dot(left_side, right_side, precision=HIGHEST)

def slot_layout(owner_list):
    onehot = (owner_list[:, None] == jnp.arange(N_FSDP, dtype=jnp.int32)[None, :]).astype(jnp.int32)
    rank_in = lax.optimization_barrier(jnp.sum((jnp.cumsum(onehot, axis=0) - onehot) * onehot, axis=1))
    slot_of = owner_list * CAP + rank_in
    source = jnp.zeros((N_FSDP * CAP,), jnp.int32).at[slot_of].set(jnp.arange(NB, dtype=jnp.int32))
    filled = jnp.zeros((N_FSDP * CAP,), jnp.int32).at[slot_of].set(jnp.ones((NB,), jnp.int32))
    return (slot_of, source, filled)

def normed(values, gain_row):
    inv_rms = lax.rsqrt(lax.optimization_barrier(jnp.mean(values * values, axis=-1, keepdims=True)) + EPS_NORM)
    return low(values * inv_rms * gain_row)

def relative_bias(bias_table, bucket_ids):
    onehot = jax.nn.one_hot(bucket_ids, BUCKETS, dtype=jnp.float32)
    rel_rows = matmul(onehot, bias_table)
    offsets = jnp.arange(LEN, dtype=jnp.int32)[None, :] - jnp.arange(LEN, dtype=jnp.int32)[:, None] + LEN - 1
    return jnp.transpose(rel_rows[offsets], (2, 0, 1))

def attend(packed, rel_bias):
    queries, keys_in, values_in, lengths = packed
    scores = jnp.einsum('sqhd,skhd->shqk', queries, keys_in, precision=HIGHEST) + rel_bias[None]
    scores = low_back(scores)
    live = jnp.arange(LEN, dtype=jnp.int32)[None, None, None, :] < lengths[:, None, None, None]
    scores = jnp.where(live, scores, NEG_FILL)
    attn_probs = jax.nn.softmax(scores, axis=-1)
    return jnp.einsum('shqk,skhd->sqhd', low(attn_probs), values_in, precision=HIGHEST)

def layer(inputs, w_query, w_key, w_value, w_out, w_in, w_down, gains_in, table_in, bucket_ids, valid_len):
    rel_bias = relative_bias(table_in, bucket_ids)
    hidden_one = normed(inputs, gains_in[0])
    queries = low(low_back(matmul(hidden_one, w_query)))
    keys_in = low(low_back(matmul(hidden_one, w_key)))
    values_in = low(low_back(matmul(hidden_one, w_value)))
    group_size = math.gcd(SEQS, max(1, 4096 // LEN))

    def shaped(array_in):
        return array_in.reshape(SEQS // group_size, group_size, LEN, HEADS, HEAD_DIM)
    packed = (shaped(queries), shaped(keys_in), shaped(values_in), valid_len.reshape(SEQS // group_size, group_size))
    context = lax.map(jax.checkpoint(partial(attend, rel_bias=rel_bias)), packed)
    context = low(low_back(context.reshape(SEQS * LEN, D)))
    resid = inputs + low_back(matmul(context, w_out))
    hidden_two = normed(resid, gains_in[1])
    pre_act = low_back(matmul(hidden_two, w_in.T))
    active = low(jax.nn.gelu(pre_act, approximate=True))
    return resid + low_back(matmul(active, w_down))

def adamw(weight, gradient, first_in, second, step_value, rate):
    first_out = BETA_ONE * first_in + (1.0 - BETA_ONE) * gradient
    second_out = BETA_TWO * second + (1.0 - BETA_TWO) * gradient * gradient
    fix_first = 1.0 - jnp.power(jnp.float32(BETA_ONE), step_value)
    fix_second = 1.0 - jnp.power(jnp.float32(BETA_TWO), step_value)
    update = first_out / fix_first / (jnp.sqrt(second_out / fix_second) + EPS_ADAM)
    return (first_out, second_out, weight - rate * (update + WEIGHT_DECAY * weight))

def reference(tokens, cotangent, master_slots, first_slots, second_slots, norm_gains, gains_first, gains_second, bias_table, table_first, table_second, bucket_ids, valid_len, task_sizes, owner_list):
    slot_of, source, filled = slot_layout(owner_list)
    all_rows = low(master_slots.reshape(N_FSDP * CAP, BROWS, D)[slot_of].reshape(NB * BROWS, D))
    bounds = [0, D, 2 * D, 3 * D, 4 * D, 4 * D + FF, 4 * D + 2 * FF]
    matrices = [all_rows[bounds[piece_index]:bounds[piece_index + 1]] for piece_index in range(6)]
    task_ends = jnp.cumsum(task_sizes)
    seq_ids = jnp.arange(SEQS, dtype=jnp.int32)
    task_of = lax.optimization_barrier(jnp.sum((task_ends[None, :] <= seq_ids[:, None]).astype(jnp.int32), axis=1))
    size_of = lax.optimization_barrier(jnp.sum(jnp.where(task_of[:, None] == jnp.arange(TASKS, dtype=jnp.int32)[None, :], task_sizes[None, :], 0), axis=1))
    seq_weight = jnp.float32(SEQS) / (jnp.float32(TASKS) * size_of.astype(jnp.float32))
    back_out = (cotangent.astype(jnp.float32).reshape(SEQS, LEN, D) * seq_weight[:, None, None]).reshape(SEQS * LEN, D)

    def forward(inputs, w_query, w_key, w_value, w_out, w_in, w_down, gains_in, table_in):
        return layer(inputs, w_query, w_key, w_value, w_out, w_in, w_down, gains_in, table_in, bucket_ids, valid_len)
    block_out, pull_back = jax.vjp(forward, tokens.astype(jnp.float32), *matrices, norm_gains, bias_table)
    gradients = pull_back(back_out)
    grad_rows = jnp.concatenate(gradients[1:7], axis=0).reshape(NB, BROWS, D)
    grad_slots = jnp.where(filled[:, None, None] > 0, grad_rows[source], 0.0).reshape(N_FSDP * CAP * BROWS, D)
    step_value = jnp.float32(OPT_STEP)
    first_new, second_new, master_new = adamw(master_slots, grad_slots, first_slots, second_slots, step_value, LEARN_RATE)
    gains_first_new, gains_second_new, gains_new = adamw(norm_gains, gradients[7], gains_first, gains_second, step_value, SMALL_RATE)
    table_first_new, table_second_new, table_new = adamw(bias_table, gradients[8], table_first, table_second, step_value, SMALL_RATE)
    return (block_out.astype(jnp.bfloat16), gradients[0], grad_slots, gradients[7], gradients[8], first_new, second_new, master_new, master_new.astype(jnp.bfloat16), gains_first_new, gains_second_new, gains_new, table_first_new, table_second_new, table_new)
```

```python
import functools
import jax
import jax.numpy as jnp
from jax import lax
from jax.experimental import pallas as pl
from jax.experimental.pallas import tpu as pltpu
from jax.sharding import PartitionSpec as P

HEADS = 12
HEAD_DIM = 64
LEN = 512
BROWS = 8
EPS_NORM = 1e-06
NEG_FILL = -1e30
HIGHEST = lax.Precision.HIGHEST
MESH = pl.DeviceIdType.MESH
BF = jnp.bfloat16
F32 = jnp.float32

CHIPS = 16
RANGE_BLOCKS = 72
RANGE_ROWS = 576
PAIR_ROWS = 80
PACK_ROWS = CHIPS * PAIR_ROWS
ROUNDS = 3
TILE = 128
HALF = 3 * TILE
NT = (((1,), (1,)), ((), ()))
NN = (((1,), (0,)), ((), ()))


def dotf(a, b, dims=NN):
    return lax.dot_general(a, b, dims, preferred_element_type=F32)


def unit_place(v):
    return v // 3, v % 3


def unit_slice(v, core):
    rng, til = unit_place(v)
    return (
        pl.ds(pl.multiple_of(rng * RANGE_ROWS, 64), RANGE_ROWS),
        pl.ds(pl.multiple_of(core * HALF + til * TILE, TILE), TILE),
    )


def half_slice(v, core, half):
    rng, til = unit_place(v)
    return (
        pl.ds(pl.multiple_of(rng * RANGE_ROWS + half * (RANGE_ROWS // 2), 32), RANGE_ROWS // 2),
        pl.ds(pl.multiple_of(core * HALF + til * TILE, TILE), TILE),
    )


def place():
    core = lax.axis_index("dp")
    chip = lax.axis_index("fsdp")
    xpos = chip % 2
    ypos = (chip // 2) % 2
    zpos = chip // 4
    xnbr = chip + 1 - 2 * xpos
    ynbr = chip + 2 - 4 * ypos
    return core, chip, xpos, ypos, zpos, xnbr, ynbr


def enter(core, chip):
    barrier = pltpu.get_barrier_semaphore()
    for step in range(1, CHIPS):
        pl.semaphore_signal(
            barrier, inc=1, device_id=(core, lax.rem(chip + step, CHIPS)), device_id_type=MESH
        )
    pl.semaphore_signal(barrier, inc=1, device_id=(1 - core, chip), device_id_type=MESH)
    pl.semaphore_wait(barrier, CHIPS)


def gather_kernel(
    master_ref, idx_pack_ref, idx_unit_ref, tokens_ref, gains_ref, rel_ref, len_ref,
    w_hbm, q_ref, k_ref, v_ref, ctx_ref, p_hbm,
    weights, sendbuf, recvbuf, hidden, base, s_scr, p_scr,
    a2a_send, a2a_recv, z_send, z_recv, x_send, x_recv, y_send, y_recv,
    da_send, da_recv, db_send, db_recv, s_send, s_recv, w_sem, p_sem,
):
    core, chip, xpos, ypos, zpos, xnbr, ynbr = place()
    col = ypos * 2 + xpos
    xcol = ypos * 2 + (1 - xpos)
    ycol = (1 - ypos) * 2 + xpos
    dcol = (1 - ypos) * 2 + (1 - xpos)

    def remote(src, dst, ssem, rsem, device):
        return pltpu.make_async_remote_copy(
            src_ref=src, dst_ref=dst, send_sem=ssem, recv_sem=rsem, device_id=device, device_id_type=MESH
        )

    for part in range(4):
        rows = PACK_ROWS // 4
        onehot = (
            lax.broadcasted_iota(jnp.int32, (rows, master_ref.shape[0]), 1)
            == idx_pack_ref[part * rows : (part + 1) * rows, :]
        ).astype(F32).astype(BF)
        own_half = master_ref[:, pl.ds(pl.multiple_of(core * HALF, TILE), HALF)].astype(BF)
        packed = dotf(onehot, own_half).astype(BF)
        for til in range(3):
            sendbuf[til, part * rows : (part + 1) * rows, :] = packed[:, til * TILE : (til + 1) * TILE]

    enter(core, chip)

    def a2a_copy(rnd, step):
        dest = lax.rem(chip + step, CHIPS)
        rng, til = unit_place(rnd * CHIPS + dest)
        return remote(
            sendbuf.at[til, pl.ds(pl.multiple_of(rng * PAIR_ROWS, 16), PAIR_ROWS), :],
            recvbuf.at[rnd, pl.ds(pl.multiple_of(chip * PAIR_ROWS, 16), PAIR_ROWS), :],
            a2a_send.at[rnd, step], a2a_recv.at[rnd, step], (core, dest),
        )

    for rnd in range(ROUNDS):
        for step in range(1, CHIPS):
            a2a_copy(rnd, step).start()
        rng, til = unit_place(rnd * CHIPS + chip)
        recvbuf[rnd, pl.ds(pl.multiple_of(chip * PAIR_ROWS, 16), PAIR_ROWS), :] = sendbuf[
            til, pl.ds(pl.multiple_of(rng * PAIR_ROWS, 16), PAIR_ROWS), :
        ]

    for part in range(tokens_ref.shape[0] // 128):
        rows = slice(part * 128, (part + 1) * 128)
        values = tokens_ref[rows, :].astype(F32)
        inv_rms = lax.rsqrt(jnp.mean(values * values, axis=-1, keepdims=True) + EPS_NORM)
        hidden[rows, :] = (values * inv_rms * gains_ref[0:1, :]).astype(BF)

    def bands(h, _):
        wide = jnp.broadcast_to(rel_ref[pl.ds(h, 1), :], (128, 1024))
        base[pl.ds(h, 1)] = pltpu.roll(wide, 0, 1, stride=1, stride_axis=0)[:, :896][None]
        return 0

    lax.fori_loop(0, HEADS, bands, 0)

    def own_unit(rnd):
        for step in range(1, CHIPS):
            a2a_copy(rnd, step).wait_recv()
        v = rnd * CHIPS + chip
        for part in range(2):
            rows = RANGE_ROWS // 2
            onehot = (
                lax.broadcasted_iota(jnp.int32, (rows, PACK_ROWS), 1)
                == idx_unit_ref[rnd, part * rows : (part + 1) * rows, :]
            ).astype(F32).astype(BF)
            weights[half_slice(v, core, part)] = dotf(onehot, recvbuf[rnd]).astype(BF)

    def z_copy(rnd, off):
        v = rnd * CHIPS + chip
        dest = lax.rem(zpos + off, 4) * 4 + col
        place_at = unit_slice(v, core)
        return remote(
            weights.at[place_at], weights.at[place_at],
            z_send.at[rnd, off], z_recv.at[rnd, off], (core, dest),
        )

    def plane(off):
        return lax.rem(zpos + 4 - off, 4)

    def unit_at(rnd, off, column):
        return rnd * CHIPS + plane(off) * 4 + column

    def x_copy(rnd, off):
        at = unit_slice(unit_at(rnd, off, col), core)
        return remote(weights.at[at], weights.at[at], x_send.at[rnd, off], x_recv.at[rnd, off], (core, xnbr))

    def y_copy(rnd, off):
        at = unit_slice(unit_at(rnd, off, col), core)
        return remote(weights.at[at], weights.at[at], y_send.at[rnd, off], y_recv.at[rnd, off], (core, ynbr))

    def da_copy(rnd, off):
        at = half_slice(unit_at(rnd, off, xcol), core, 0)
        return remote(weights.at[at], weights.at[at], da_send.at[rnd, off], da_recv.at[rnd, off], (core, ynbr))

    def db_copy(rnd, off):
        at = half_slice(unit_at(rnd, off, ycol), core, 1)
        return remote(weights.at[at], weights.at[at], db_send.at[rnd, off], db_recv.at[rnd, off], (core, xnbr))

    def s_copy(rnd, off, kind):
        at = unit_slice(unit_at(rnd, off, (col, xcol, ycol, dcol)[kind]), core)
        return remote(
            weights.at[at], weights.at[at], s_send.at[kind, rnd, off], s_recv.at[kind, rnd, off], (1 - core, chip)
        )

    def z_start(rnd):
        for off in (1, 2, 3):
            z_copy(rnd, off).start()

    def stage_a(rnd, off):
        x_copy(rnd, off).start()
        y_copy(rnd, off).start()
        s_copy(rnd, off, 0).start()

    def stage_b(rnd, off):
        x_copy(rnd, off).wait_recv()
        da_copy(rnd, off).start()
        s_copy(rnd, off, 1).start()
        y_copy(rnd, off).wait_recv()
        db_copy(rnd, off).start()
        s_copy(rnd, off, 2).start()

    def stage_c(rnd, off):
        da_copy(rnd, off).wait_recv()
        db_copy(rnd, off).wait_recv()
        s_copy(rnd, off, 3).start()

    def z_wait(rnd, off):
        z_copy(rnd, off).wait_recv()

    def s_wait(rnd):
        for off in range(4):
            for kind in range(4):
                s_copy(rnd, off, kind).wait_recv()

    own_unit(0)
    z_start(0)
    stage_a(0, 0)
    for rnd in (1, 2):
        own_unit(rnd)
        z_start(rnd)
    z_wait(0, 1)
    stage_a(0, 1)
    stage_b(0, 0)
    z_wait(0, 2)
    stage_a(0, 2)
    stage_b(0, 1)
    stage_c(0, 0)
    z_wait(0, 3)
    stage_a(0, 3)
    stage_a(1, 0)
    stage_b(0, 2)
    stage_c(0, 1)
    z_wait(1, 1)
    stage_a(1, 1)
    stage_b(0, 3)
    stage_c(0, 2)
    stage_b(1, 0)
    stage_c(0, 3)
    s_wait(0)

    model = hidden.shape[1]
    for mat, out_ref in enumerate((q_ref, k_ref, v_ref)):
        for til in range(model // 256):
            cols = slice(til * 256, (til + 1) * 256)
            out_ref[:, cols] = dotf(hidden[...], weights[mat * model : (mat + 1) * model, cols]).astype(BF)

    row_id = lax.broadcasted_iota(jnp.int32, (128, LEN), 0)
    lane_head = lax.broadcasted_iota(jnp.int32, (LEN, 128), 1) // HEAD_DIM

    def p_copy(step, head):
        seq, pair = step // 6, step % 6
        return pltpu.make_async_copy(
            p_scr.at[step % 2, head], p_hbm.at[seq * HEADS + pair * 2 + head], p_sem.at[step % 2, head]
        )

    def attend(step, _):
        seq, pair = step // 6, step % 6
        rows = pl.ds(pl.multiple_of(seq * LEN, LEN), LEN)
        lanes = pl.ds(pl.multiple_of(pair * 128, 128), 128)
        length = len_ref[seq]

        @pl.when(step >= 2)
        def _():
            for head in range(2):
                p_copy(step - 2, head).wait()

        q_two = q_ref[rows, lanes]
        k_two = k_ref[rows, lanes]
        v_two = v_ref[rows, lanes].T
        outs = []
        for head in range(2):
            k_one = jnp.where(lane_head == head, k_two, jnp.zeros_like(k_two))
            top = jnp.full((8, LEN), NEG_FILL, F32)
            for blk in range(4):
                score = dotf(k_one[blk * 128 : (blk + 1) * 128], q_two, NT)
                score = score + base[pair * 2 + head, :, 384 - 128 * blk : 896 - 128 * blk]
                score = jnp.where(row_id + blk * 128 < length, score, NEG_FILL)
                s_scr[head, blk * 128 : (blk + 1) * 128, :] = score
                top = jnp.maximum(top, jnp.max(score.reshape(16, 8, LEN), axis=0))
            top = jnp.max(top, axis=0, keepdims=True)
            total = jnp.zeros((8, LEN), F32)
            for blk in range(4):
                part = jnp.exp(s_scr[head, blk * 128 : (blk + 1) * 128, :] - top)
                s_scr[head, blk * 128 : (blk + 1) * 128, :] = part
                total = total + jnp.sum(part.reshape(16, 8, LEN), axis=0)
            inverse = 1.0 / jnp.sum(total, axis=0, keepdims=True)
            for blk in range(4):
                p_scr[step % 2, head, blk * 128 : (blk + 1) * 128, :] = (
                    s_scr[head, blk * 128 : (blk + 1) * 128, :] * inverse
                ).astype(BF)
            outs.append(dotf(v_two[head * HEAD_DIM : (head + 1) * HEAD_DIM], p_scr[step % 2, head]))
            p_copy(step, head).start()
        ctx_ref[rows, lanes] = jnp.concatenate(outs, axis=0).T.astype(BF)
        return 0

    def w_copy(rnd):
        at = slice(rnd * 3072, (rnd + 1) * 3072)
        return pltpu.make_async_copy(weights.at[at], w_hbm.at[at], w_sem.at[rnd])

    lax.fori_loop(0, 4, attend, 0)
    z_wait(1, 2)
    stage_a(1, 2)
    stage_b(1, 1)
    stage_c(1, 0)
    z_wait(1, 3)
    stage_a(1, 3)
    stage_a(2, 0)
    stage_b(1, 2)
    stage_c(1, 1)
    lax.fori_loop(4, 8, attend, 0)
    z_wait(2, 1)
    stage_a(2, 1)
    stage_b(1, 3)
    stage_c(1, 2)
    stage_b(2, 0)
    stage_c(1, 3)
    z_wait(2, 2)
    stage_a(2, 2)
    lax.fori_loop(8, 12, attend, 0)
    stage_b(2, 1)
    stage_c(2, 0)
    z_wait(2, 3)
    stage_a(2, 3)
    stage_b(2, 2)
    stage_c(2, 1)
    stage_b(2, 3)
    stage_c(2, 2)
    stage_c(2, 3)
    s_wait(1)
    s_wait(2)
    for rnd in range(ROUNDS):
        w_copy(rnd).start()
    for step in (10, 11):
        for head in range(2):
            p_copy(step, head).wait()
    for rnd in range(ROUNDS):
        w_copy(rnd).wait()
        for step in range(1, CHIPS):
            a2a_copy(rnd, step).wait_send()
        for off in (1, 2, 3):
            z_copy(rnd, off).wait_send()
        for off in range(4):
            x_copy(rnd, off).wait_send()
            y_copy(rnd, off).wait_send()
            da_copy(rnd, off).wait_send()
            db_copy(rnd, off).wait_send()
            for kind in range(4):
                s_copy(rnd, off, kind).wait_send()


VM = pl.BlockSpec(memory_space=pltpu.VMEM)
SM = pl.BlockSpec(memory_space=pltpu.SMEM)
ANY = pl.BlockSpec(memory_space=pl.ANY)


def gather_forward(master, idx_pack, idx_unit, tokens, gains, rel, lens):
    ntok, model = tokens.shape
    rows = 4 * model + 2 * 3072
    dma = pltpu.SemaphoreType.DMA
    return pl.pallas_call(
        gather_kernel,
        name="gather_forward",
        out_shape=(
            jax.ShapeDtypeStruct((rows, model), BF),
            jax.ShapeDtypeStruct((ntok, model), BF),
            jax.ShapeDtypeStruct((ntok, model), BF),
            jax.ShapeDtypeStruct((ntok, model), BF),
            jax.ShapeDtypeStruct((ntok, model), BF),
            jax.ShapeDtypeStruct((2 * HEADS, LEN, LEN), BF),
        ),
        in_specs=[VM, VM, VM, VM, VM, VM, SM],
        out_specs=(ANY, VM, VM, VM, VM, ANY),
        scratch_shapes=[
            pltpu.VMEM((rows, model), BF),
            pltpu.VMEM((3, PACK_ROWS, TILE), BF),
            pltpu.VMEM((ROUNDS, PACK_ROWS, TILE), BF),
            pltpu.VMEM((ntok, model), BF),
            pltpu.VMEM((HEADS, 128, 896), F32),
            pltpu.VMEM((2, LEN, LEN), F32),
            pltpu.VMEM((2, 2, LEN, LEN), BF),
            dma((ROUNDS, CHIPS)), dma((ROUNDS, CHIPS)),
            dma((ROUNDS, 4)), dma((ROUNDS, 4)),
            dma((ROUNDS, 4)), dma((ROUNDS, 4)),
            dma((ROUNDS, 4)), dma((ROUNDS, 4)),
            dma((ROUNDS, 4)), dma((ROUNDS, 4)),
            dma((ROUNDS, 4)), dma((ROUNDS, 4)),
            dma((4, ROUNDS, 4)), dma((4, ROUNDS, 4)),
            dma((ROUNDS,)), dma((2, 2)),
        ],
        compiler_params=pltpu.CompilerParams(
            collective_id=0, has_side_effects=True, vmem_limit_bytes=60 * 2**20
        ),
    )(master, idx_pack, idx_unit, tokens, gains, rel, lens)


def slot_tables(owner_list, chip):
    owners = owner_list.reshape(CHIPS, RANGE_BLOCKS)
    counts = jnp.sum((owners == chip).astype(jnp.int32), axis=1)
    tri = jnp.arange(CHIPS)[:, None] > jnp.arange(CHIPS)[None, :]
    starts = jnp.sum(jnp.where(tri, counts[None, :], 0), axis=1)
    blk = jnp.arange(PAIR_ROWS // BROWS, dtype=jnp.int32)[None, :, None]
    sub = jnp.arange(BROWS, dtype=jnp.int32)[None, None, :]
    pack = jnp.where(
        blk < counts[:, None, None], (starts[:, None, None] + blk) * BROWS + sub, -1
    ).reshape(PACK_ROWS)
    v = jnp.arange(ROUNDS, dtype=jnp.int32) * CHIPS + chip
    rng, _ = unit_place(v)
    mine = jnp.stack([lax.dynamic_slice(owners, (rng[i], 0), (1, RANGE_BLOCKS))[0] for i in range(ROUNDS)])
    before = jnp.arange(RANGE_BLOCKS)[:, None] > jnp.arange(RANGE_BLOCKS)[None, :]
    rank = jnp.sum(
        ((mine[:, :, None] == mine[:, None, :]) & before[None]).astype(jnp.int32), axis=2
    )
    unit = (
        (mine * PAIR_ROWS + rank * BROWS)[:, :, None] + jnp.arange(BROWS, dtype=jnp.int32)[None, None, :]
    ).reshape(ROUNDS, RANGE_ROWS)
    return pack, unit


def rel_values(bias_table, bucket_ids):
    length = (bucket_ids.shape[0] + 1) // 2
    onehot = jax.nn.one_hot(bucket_ids, bias_table.shape[0], dtype=F32)
    rel = jnp.dot(onehot, bias_table, precision=HIGHEST)[::-1].T
    rel = jnp.concatenate([rel, jnp.zeros((HEADS, 1), F32)], axis=1)
    rel = jnp.concatenate([rel[:, 127:], rel[:, :127]], axis=1)
    return jnp.concatenate([rel, jnp.zeros((4, 2 * length), F32)], axis=0)


FF_CHUNK = 512
GELU_A = 0.7978845608028654
GELU_B = 0.044715 * GELU_A


def gelu_pair(v):
    sq = v * v
    half = 0.5 + 0.5 * jnp.tanh(v * (GELU_A + GELU_B * sq))
    act = v * half
    return act, half + act * (1.0 - half) * (2.0 * GELU_A + 6.0 * GELU_B * sq)


TN = (((0,), (0,)), ((), ()))


def ffn_kernel(
    tokens_ref, cot_ref, ctx_ref, gains_ref, weight_ref, w_hbm,
    out_ref, rb_ref, cb_ref, gain_ref, grad_hbm,
    weights, hidden, down, resid, out_acc, u_acc, act_s, pb_s, gbuf, w_sem, g_sem,
):
    ntok, model = tokens_ref.shape
    hid = (weights.shape[0] - 4 * model) // 2
    nchunk = hid // FF_CHUNK
    first_in, first_down = 4 * model, 4 * model + hid
    seq_len = LEN

    def w_copy(start, rows, sem):
        at = pl.ds(start, rows)
        return pltpu.make_async_copy(w_hbm.at[at], weights.at[at], sem)

    w_copy(3 * model, model, w_sem.at[0]).start()
    for c in range(nchunk):
        w_copy(first_in + c * FF_CHUNK, FF_CHUNK, w_sem.at[1 + c]).start()
        w_copy(first_down + c * FF_CHUNK, FF_CHUNK, w_sem.at[1 + nchunk + c]).start()
    w_copy(3 * model, model, w_sem.at[0]).wait()

    tile = 256
    ntile = ntok // tile

    def head(i, _):
        rows = pl.ds(pl.multiple_of(i * tile, tile), tile)
        value = tokens_ref[rows, :].astype(F32) + dotf(
            ctx_ref[rows, :], weights[3 * model : 4 * model, :]
        )
        resid[rows, :] = value
        inv_rms = lax.rsqrt(jnp.mean(value * value, axis=-1, keepdims=True) + EPS_NORM)
        hidden[rows, :] = (value * inv_rms * gains_ref[1:2, :]).astype(BF)
        down[rows, :] = (cot_ref[rows, :].astype(F32) * weight_ref[i * tile // seq_len]).astype(BF)
        out_acc[rows, :] = jnp.zeros((tile, model), F32)
        u_acc[rows, :] = jnp.zeros((tile, model), F32)
        return 0

    lax.fori_loop(0, ntile, head, 0)

    def g_copy(c, which):
        start = (first_in, first_down)[which] + c * FF_CHUNK
        return pltpu.make_async_copy(
            gbuf.at[c % 2, which], grad_hbm.at[pl.ds(pl.multiple_of(start, FF_CHUNK), FF_CHUNK)],
            g_sem.at[c % 2, which],
        )

    def chunk(c, _):
        rows_in = pl.ds(pl.multiple_of(first_in + c * FF_CHUNK, FF_CHUNK), FF_CHUNK)
        rows_down = pl.ds(pl.multiple_of(first_down + c * FF_CHUNK, FF_CHUNK), FF_CHUNK)
        pltpu.make_async_copy(w_hbm.at[rows_in], weights.at[rows_in], w_sem.at[1 + c]).wait()
        pltpu.make_async_copy(w_hbm.at[rows_down], weights.at[rows_down], w_sem.at[1 + nchunk + c]).wait()
        for i in range(ntile):
            rows = slice(i * tile, (i + 1) * tile)
            pre = dotf(hidden[rows, :], weights[rows_in, :], NT)
            back = dotf(down[rows, :], weights[rows_down, :], NT)
            act, slope = gelu_pair(pre)
            act = act.astype(BF)
            pre_back = (back * slope).astype(BF)
            act_s[rows, :] = act
            pb_s[rows, :] = pre_back
            out_acc[rows, :] += dotf(act, weights[rows_down, :])
            u_acc[rows, :] += dotf(pre_back, weights[rows_in, :])

        @pl.when(c >= 2)
        def _():
            g_copy(c - 2, 0).wait()
            g_copy(c - 2, 1).wait()

        gbuf[c % 2, 1] = dotf(act_s[...], down[...], TN).astype(BF)
        g_copy(c, 1).start()
        gbuf[c % 2, 0] = dotf(pb_s[...], hidden[...], TN).astype(BF)
        g_copy(c, 0).start()
        return 0

    lax.fori_loop(0, nchunk, chunk, 0)

    def tail(i, gain):
        rows = pl.ds(pl.multiple_of(i * tile, tile), tile)
        value = resid[rows, :]
        out_ref[rows, :] = (value + out_acc[rows, :]).astype(BF)
        inv_rms = lax.rsqrt(jnp.mean(value * value, axis=-1, keepdims=True) + EPS_NORM)
        u = u_acc[rows, :]
        gu = u * gains_ref[1:2, :]
        normal = value * inv_rms
        mean = jnp.mean(gu * normal, axis=-1, keepdims=True)
        back = cot_ref[rows, :].astype(F32) * weight_ref[i * tile // seq_len] + inv_rms * (gu - normal * mean)
        rb_ref[rows, :] = back
        low = back.astype(BF)
        hidden[rows, :] = low
        cb_ref[rows, :] = dotf(low, weights[3 * model : 4 * model, :], NT).astype(BF)
        return gain + jnp.sum((u * normal).reshape(tile // 8, 8, model), axis=0)

    gain = lax.fori_loop(0, ntile, tail, jnp.zeros((8, model), F32))
    gain_ref[...] = gain
    for c in (nchunk - 2, nchunk - 1):
        g_copy(c, 0).wait()
        g_copy(c, 1).wait()
    for part in range(2):
        cols = slice(part * model // 2, (part + 1) * model // 2)
        gbuf[part, 0, : model // 2, :] = dotf(ctx_ref[:, cols], hidden[...], TN).astype(BF)
        pltpu.make_async_copy(
            gbuf.at[part, 0, pl.ds(0, model // 2)],
            grad_hbm.at[pl.ds(3 * model + part * model // 2, model // 2)], g_sem.at[part, 0],
        ).start()
    for part in range(2):
        pltpu.make_async_copy(
            gbuf.at[part, 0, pl.ds(0, model // 2)],
            grad_hbm.at[pl.ds(3 * model + part * model // 2, model // 2)], g_sem.at[part, 0],
        ).wait()


def ffn_pass(tokens, cot, ctx, gains, seq_weight, w_all):
    ntok, model = tokens.shape
    rows = w_all.shape[0]
    nchunk = (rows - 4 * model) // 2 // FF_CHUNK
    dma = pltpu.SemaphoreType.DMA
    return pl.pallas_call(
        ffn_kernel,
        name="ffn_pass",
        out_shape=(
            jax.ShapeDtypeStruct((ntok, model), BF),
            jax.ShapeDtypeStruct((ntok, model), F32),
            jax.ShapeDtypeStruct((ntok, model), BF),
            jax.ShapeDtypeStruct((8, model), F32),
            jax.ShapeDtypeStruct((rows, model), BF),
        ),
        in_specs=[VM, VM, VM, VM, SM, ANY],
        out_specs=(VM, VM, VM, VM, ANY),
        scratch_shapes=[
            pltpu.VMEM((rows, model), BF),
            pltpu.VMEM((ntok, model), BF),
            pltpu.VMEM((ntok, model), BF),
            pltpu.VMEM((ntok, model), F32),
            pltpu.VMEM((ntok, model), F32),
            pltpu.VMEM((ntok, model), F32),
            pltpu.VMEM((ntok, FF_CHUNK), BF),
            pltpu.VMEM((ntok, FF_CHUNK), BF),
            pltpu.VMEM((2, 2, FF_CHUNK, model), BF),
            dma((1 + 2 * nchunk,)), dma((2, 2)),
        ],
        compiler_params=pltpu.CompilerParams(vmem_limit_bytes=60 * 2**20),
    )(tokens, cot, ctx, gains, seq_weight, w_all)


def reduce_kernel(
    tokens_ref, gains_ref, q_ref, k_ref, v_ref, ctx_ref, cb_ref, bucket_ref, gain_two_ref, idx_unit_ref,
    rb_hbm, w_hbm, p_hbm, grad_hbm,
    gin_ref, slot_ref, small_ref,
    weights, gown, gsend, sib, xin, yin, dain, dbin, zin, expand,
    hid_t, dq, dk, dv, diag, drow, p_scr, ds_scr, small,
    w_sem, l_sem, p_sem, r_sem, h_send, h_recv, da_send, da_recv, db_send, db_recv,
    x_send, x_recv, y_send, y_recv, z_send, z_recv, a2a_send, a2a_recv, half_send, half_recv,
    sm_send, sm_recv,
):
    core, chip, xpos, ypos, zpos, xnbr, ynbr = place()
    ntok, model = tokens_ref.shape
    col = ypos * 2 + xpos
    xcol = ypos * 2 + (1 - xpos)
    ycol = (1 - ypos) * 2 + xpos
    dcol = (1 - ypos) * 2 + (1 - xpos)
    other = 1 - core
    own_cols = pl.ds(pl.multiple_of(core * HALF, TILE), HALF)
    other_cols = pl.ds(pl.multiple_of(other * HALF, TILE), HALF)
    qkv_rows = 3 * model
    nrange = gown.shape[0] // RANGE_ROWS
    qkv_ranges = qkv_rows // RANGE_ROWS

    def remote(src, dst, ssem, rsem, device):
        return pltpu.make_async_remote_copy(
            src_ref=src, dst_ref=dst, send_sem=ssem, recv_sem=rsem, device_id=device, device_id_type=MESH
        )

    def range_rows(rng):
        return pl.ds(pl.multiple_of(rng * RANGE_ROWS, 64), RANGE_ROWS)

    def load_copy(rng):
        return pltpu.make_async_copy(
            grad_hbm.at[range_rows(rng), own_cols], gown.at[range_rows(rng)], l_sem.at[rng]
        )

    def sib_copy(rng):
        src = grad_hbm.at[range_rows(rng), other_cols] if rng >= qkv_ranges else gsend.at[range_rows(rng)]
        return remote(src, sib.at[range_rows(rng)], h_send.at[rng], h_recv.at[rng], (other, chip))

    def sib_wait(rng):
        remote(
            gown.at[range_rows(rng)], sib.at[range_rows(rng)], h_send.at[rng], h_recv.at[rng], (other, chip)
        ).wait_recv()

    w_all = pltpu.make_async_copy(w_hbm.at[pl.ds(0, qkv_rows)], weights, w_sem)
    w_all.start()
    enter(core, chip)
    for rng in reversed(range(qkv_ranges, nrange)):
        load_copy(rng).start()
        sib_copy(rng).start()

    def gslice(v):
        rng, til = unit_place(v)
        return (range_rows(rng), pl.ds(pl.multiple_of(til * TILE, TILE), TILE))

    def ghalf(v, half):
        rng, til = unit_place(v)
        return (
            pl.ds(pl.multiple_of(rng * RANGE_ROWS + half * (RANGE_ROWS // 2), 32), RANGE_ROWS // 2),
            pl.ds(pl.multiple_of(til * TILE, TILE), TILE),
        )

    def plane(off):
        return lax.rem(zpos + off, 4)

    def unit_at(rnd, off, column):
        return rnd * CHIPS + plane(off) * 4 + column

    def da_copy(rnd, off):
        at = ghalf(unit_at(rnd, off, dcol), 0)
        return remote(gown.at[at], dain.at[rnd, off], da_send.at[rnd, off], da_recv.at[rnd, off], (core, ynbr))

    def db_copy(rnd, off):
        at = ghalf(unit_at(rnd, off, dcol), 1)
        return remote(gown.at[at], dbin.at[rnd, off], db_send.at[rnd, off], db_recv.at[rnd, off], (core, xnbr))

    def x_copy(rnd, off):
        at = gslice(unit_at(rnd, off, xcol))
        return remote(gown.at[at], xin.at[rnd, off], x_send.at[rnd, off], x_recv.at[rnd, off], (core, xnbr))

    def y_copy(rnd, off):
        at = gslice(unit_at(rnd, off, ycol))
        return remote(gown.at[at], yin.at[rnd, off], y_send.at[rnd, off], y_recv.at[rnd, off], (core, ynbr))

    def z_copy(rnd, off):
        at = gslice(unit_at(rnd, off, col))
        return remote(
            gown.at[at], zin.at[rnd, off], z_send.at[rnd, off], z_recv.at[rnd, off], (core, plane(off) * 4 + col)
        )

    def add(at, other_ref):
        gown[at] = (gown[at].astype(F32) + other_ref[...].astype(F32)).astype(BF)

    def stage_zero(rnd, off):
        for column in (dcol, xcol, ycol, col):
            at = gslice(unit_at(rnd, off, column))
            add(at, sib.at[at])
        da_copy(rnd, off).start()
        db_copy(rnd, off).start()

    def stage_one(rnd, off):
        da_copy(rnd, off).wait_recv()
        add(ghalf(unit_at(rnd, off, xcol), 0), dain.at[rnd, off])
        x_copy(rnd, off).start()
        db_copy(rnd, off).wait_recv()
        add(ghalf(unit_at(rnd, off, ycol), 1), dbin.at[rnd, off])
        y_copy(rnd, off).start()

    def stage_two(rnd, off):
        x_copy(rnd, off).wait_recv()
        y_copy(rnd, off).wait_recv()
        at = gslice(unit_at(rnd, off, col))
        gown[at] = (
            gown[at].astype(F32) + xin[rnd, off].astype(F32) + yin[rnd, off].astype(F32)
        ).astype(BF)

    def a2a_copy(rnd, step):
        dest = lax.rem(chip + step, CHIPS)
        rng, til = unit_place(rnd * CHIPS + chip)
        return remote(
            expand.at[rnd, pl.ds(pl.multiple_of(dest * PAIR_ROWS, 16), PAIR_ROWS), :],
            slot_ref.at[
                pl.ds(pl.multiple_of(rng * PAIR_ROWS, 16), PAIR_ROWS),
                pl.ds(pl.multiple_of(core * HALF + til * TILE, TILE), TILE),
            ],
            a2a_send.at[rnd, step], a2a_recv.at[rnd, step], (core, dest),
        )

    def stage_three(rnd):
        for off in (1, 2, 3):
            z_copy(rnd, off).wait_recv()
        at = gslice(unit_at(rnd, 0, col))
        total = gown[at].astype(F32)
        for off in (1, 2, 3):
            total = total + zin[rnd, off].astype(F32)
        total = total.astype(BF)
        for part in range(4):
            rows = PACK_ROWS // 4
            onehot = (
                lax.broadcasted_iota(jnp.int32, (rows, RANGE_ROWS), 0) + part * rows
                == idx_unit_ref[rnd : rnd + 1, :]
            ).astype(F32).astype(BF)
            expand[rnd, part * rows : (part + 1) * rows, :] = dotf(onehot, total).astype(BF)
        for step in range(1, CHIPS):
            a2a_copy(rnd, step).start()
        rng, til = unit_place(rnd * CHIPS + chip)
        slot_ref[
            pl.ds(pl.multiple_of(rng * PAIR_ROWS, 16), PAIR_ROWS),
            pl.ds(pl.multiple_of(core * HALF + til * TILE, TILE), TILE),
        ] = expand[rnd, pl.ds(pl.multiple_of(chip * PAIR_ROWS, 16), PAIR_ROWS), :]

    offsets = (1, 2, 3, 0)

    def pump(p):
        @pl.when(p < 8)
        def _():
            stage_zero(2 - p // 4, lax.rem(p % 4 + 1, 4))

        @pl.when(jnp.logical_and(p >= 1, p < 9))
        def _():
            stage_one(2 - (p - 1) // 4, lax.rem((p - 1) % 4 + 1, 4))

        @pl.when(jnp.logical_and(p >= 2, p < 10))
        def _():
            stage_two(2 - (p - 2) // 4, lax.rem((p - 2) % 4 + 1, 4))

            @pl.when((p - 2) % 4 < 3)
            def _():
                z_copy(2 - (p - 2) // 4, (p - 2) % 4 + 1).start()

    def p_copy(step, head):
        seq, pair = step // 6, step % 6
        return pltpu.make_async_copy(
            p_hbm.at[seq * HEADS + pair * 2 + head], p_scr.at[step % 2, head], p_sem.at[step % 2, head]
        )

    rb_all = pltpu.make_async_copy(rb_hbm, gin_ref, r_sem)
    rb_all.start()
    for head in range(2):
        p_copy(0, head).start()
    diag[...] = jnp.zeros_like(diag)
    for part in range(ntok // 128):
        rows = slice(part * 128, (part + 1) * 128)
        values = tokens_ref[rows, :].astype(F32)
        inv_rms = lax.rsqrt(jnp.mean(values * values, axis=-1, keepdims=True) + EPS_NORM)
        hid_t[:, rows] = (values * inv_rms * gains_ref[0:1, :]).astype(BF).T
    lane_head = lax.broadcasted_iota(jnp.int32, (LEN, 128), 1) // HEAD_DIM

    def attend_back(step, _):
        seq, pair = step // 6, step % 6
        rows = pl.ds(pl.multiple_of(seq * LEN, LEN), LEN)
        lanes = pl.ds(pl.multiple_of(pair * 128, 128), 128)

        @pl.when(step + 1 < 12)
        def _():
            for head in range(2):
                p_copy(step + 1, head).start()

        q_two, k_two, v_two, do_two = q_ref[rows, lanes], k_ref[rows, lanes], v_ref[rows, lanes], cb_ref[rows, lanes]
        k_turn = k_two.T
        inner = (do_two.astype(F32) * ctx_ref[rows, lanes].astype(F32)).T
        dv_parts, dk_parts, dq_parts = [], [], []
        for head in range(2):
            p_copy(step, head).wait()
            delta = jnp.sum(inner[head * HEAD_DIM : (head + 1) * HEAD_DIM], axis=0, keepdims=True)
            v_one = jnp.where(lane_head == head, v_two, jnp.zeros_like(v_two))
            for blk in range(4):
                sub = slice(blk * 128, (blk + 1) * 128)
                prob_back = dotf(v_one[sub], do_two, NT)
                score = p_scr[step % 2, head, sub, :].astype(F32) * (prob_back - delta)
                diag[pair * 2 + head, :, 384 - 128 * blk : 896 - 128 * blk] += score
                ds_scr[head, sub, :] = score.astype(BF)
            dv_parts.append(dotf(p_scr[step % 2, head], do_two))
            dk_parts.append(dotf(ds_scr[head], q_two))
            dq_parts.append(dotf(k_turn[head * HEAD_DIM : (head + 1) * HEAD_DIM], ds_scr[head]))
        dv[rows, lanes] = jnp.where(lane_head == 0, dv_parts[0], dv_parts[1]).astype(BF)
        dk[rows, lanes] = jnp.where(lane_head == 0, dk_parts[0], dk_parts[1]).astype(BF)
        dq[rows, lanes] = jnp.concatenate(dq_parts, axis=0).T.astype(BF)
        return 0

    for rng in reversed(range(qkv_ranges, nrange)):
        load_copy(rng).wait()
        sib_wait(rng)

    def step_both(step, _):
        pump(step)
        attend_back(step, 0)
        return 0

    lax.fori_loop(0, 12, step_both, 0)

    w_all.wait()
    for mat, grad in enumerate((dq, dk, dv)):
        mat_rows = slice(mat * model, (mat + 1) * model)
        for part in range(2):
            value = dotf(hid_t[...], grad[:, part * HALF : (part + 1) * HALF]).astype(BF)

            @pl.when(core == part)
            def _():
                gown[mat_rows, :] = value

            @pl.when(core != part)
            def _():
                gsend[mat_rows, :] = value

    for rng in range(qkv_ranges):
        sib_copy(rng).start()

    rb_all.wait()
    tile = 256

    def tail(i, gain):
        rows = pl.ds(pl.multiple_of(i * tile, tile), tile)
        u = (
            dotf(dq[rows, :], weights[:model, :], NT)
            + dotf(dk[rows, :], weights[model : 2 * model, :], NT)
            + dotf(dv[rows, :], weights[2 * model :, :], NT)
        )
        value = tokens_ref[rows, :].astype(F32)
        inv_rms = lax.rsqrt(jnp.mean(value * value, axis=-1, keepdims=True) + EPS_NORM)
        gu = u * gains_ref[0:1, :]
        normal = value * inv_rms
        mean = jnp.mean(gu * normal, axis=-1, keepdims=True)
        gin_ref[rows, :] += inv_rms * (gu - normal * mean)
        return gain + jnp.sum((u * normal).reshape(tile // 8, 8, model), axis=0)

    gain = lax.fori_loop(0, ntok // tile, tail, jnp.zeros((8, model), F32))

    for rng in range(qkv_ranges):
        sib_wait(rng)
    stage_three(2)
    stage_three(1)
    for off in offsets:
        stage_zero(0, off)
    for off in offsets:
        stage_one(0, off)

    def unskew(h, _):
        acc = jnp.concatenate([diag[h], jnp.zeros((128, 128), F32)], axis=1)
        size = 64
        while size >= 1:
            acc = acc[:size] + pltpu.roll(acc[size:], 1024 - size, 1)
            size //= 2
        drow[pl.ds(h, 1), :] = acc
        return 0

    drow[...] = jnp.zeros_like(drow)
    lax.fori_loop(0, HEADS, unskew, 0)
    onehot = (lax.broadcasted_iota(jnp.int32, (128, 1024), 0) == bucket_ref[...]).astype(F32)
    table = lax.dot_general(drow[...], onehot, NT, precision=HIGHEST, preferred_element_type=F32)
    small[0, :, :model] = jnp.zeros((16, model), F32)
    small[0, 0:1, :model] = jnp.sum(gain, axis=0, keepdims=True)
    small[0, 1:2, :model] = jnp.sum(gain_two_ref[...], axis=0, keepdims=True)
    small[0, :, model:] = table

    for off in offsets:
        stage_two(0, off)
        if off:
            z_copy(0, off).start()

    def sm_copy(slot, src, dst, device):
        return remote(small.at[src], small.at[dst], sm_send.at[slot], sm_recv.at[slot], device)

    for slot, device in enumerate(((other, chip), (core, xnbr), (core, ynbr))):
        cp = sm_copy(slot, 2 * slot, 2 * slot + 1, device)
        cp.start()
        cp.wait()
        small[2 * slot + 2] = small[2 * slot] + small[2 * slot + 1]
    for off in (1, 2, 3):
        sm_copy(2 + off, 6, 7 + zpos, (core, plane(off) * 4 + col)).start()
    small[7 + zpos] = small[6]

    stage_three(0)

    for off in (1, 2, 3):
        sm_copy(2 + off, 6, 7 + zpos, (core, plane(off) * 4 + col)).wait()
    small_ref[...] = small[7] + small[8] + small[9] + small[10]

    for rnd in range(ROUNDS):
        for step in range(1, CHIPS):
            a2a_copy(rnd, step).wait_recv()
    half = remote(
        slot_ref.at[:, own_cols], slot_ref.at[:, own_cols], half_send, half_recv, (other, chip)
    )
    half.start()
    for rng in range(nrange):
        sib_copy(rng).wait_send()
    for rnd in range(ROUNDS):
        for step in range(1, CHIPS):
            a2a_copy(rnd, step).wait_send()
        for off in range(4):
            x_copy(rnd, off).wait_send()
            y_copy(rnd, off).wait_send()
            da_copy(rnd, off).wait_send()
            db_copy(rnd, off).wait_send()
            if off:
                z_copy(rnd, off).wait_send()
    half.wait()


def reduce_backward(
    tokens, gains, q, k, v, ctx, cb, bucket_row, gain_two, idx_unit, rb, w_all, probs, grads
):
    ntok, model = tokens.shape
    rows = w_all.shape[0]
    dma = pltpu.SemaphoreType.DMA
    unit_half = RANGE_ROWS // 2
    return pl.pallas_call(
        reduce_kernel,
        name="reduce_backward",
        out_shape=(
            jax.ShapeDtypeStruct((ntok, model), F32),
            jax.ShapeDtypeStruct((PACK_ROWS, model), BF),
            jax.ShapeDtypeStruct((16, model + 128), F32),
        ),
        in_specs=[VM] * 10 + [ANY] * 4,
        out_specs=(VM, VM, VM),
        scratch_shapes=[
            pltpu.VMEM((3 * model, model), BF),
            pltpu.VMEM((rows, HALF), BF),
            pltpu.VMEM((3 * model, HALF), BF),
            pltpu.VMEM((rows, HALF), BF),
            pltpu.VMEM((ROUNDS, 4, RANGE_ROWS, TILE), BF),
            pltpu.VMEM((ROUNDS, 4, RANGE_ROWS, TILE), BF),
            pltpu.VMEM((ROUNDS, 4, unit_half, TILE), BF),
            pltpu.VMEM((ROUNDS, 4, unit_half, TILE), BF),
            pltpu.VMEM((ROUNDS, 4, RANGE_ROWS, TILE), BF),
            pltpu.VMEM((ROUNDS, PACK_ROWS, TILE), BF),
            pltpu.VMEM((model, ntok), BF),
            pltpu.VMEM((ntok, model), BF),
            pltpu.VMEM((ntok, model), BF),
            pltpu.VMEM((ntok, model), BF),
            pltpu.VMEM((HEADS, 128, 896), F32),
            pltpu.VMEM((16, 1024), F32),
            pltpu.VMEM((2, 2, LEN, LEN), BF),
            pltpu.VMEM((2, LEN, LEN), BF),
            pltpu.VMEM((11, 16, model + 128), F32),
            dma, dma((CHIPS,)), dma((2, 2)), dma, dma((CHIPS,)), dma((CHIPS,)),
            dma((ROUNDS, 4)), dma((ROUNDS, 4)), dma((ROUNDS, 4)), dma((ROUNDS, 4)),
            dma((ROUNDS, 4)), dma((ROUNDS, 4)), dma((ROUNDS, 4)), dma((ROUNDS, 4)),
            dma((ROUNDS, 4)), dma((ROUNDS, 4)),
            dma((ROUNDS, CHIPS)), dma((ROUNDS, CHIPS)), dma, dma,
            dma((6,)), dma((6,)),
        ],
        compiler_params=pltpu.CompilerParams(
            collective_id=1, has_side_effects=True, vmem_limit_bytes=62 * 2**20
        ),
    )(tokens, gains, q, k, v, ctx, cb, bucket_row, gain_two, idx_unit, rb, w_all, probs, grads)


BETA_ONE = 0.5
BETA_TWO = 0.75
LEARN_RATE = 0.06
SMALL_RATE = 0.4
WEIGHT_DECAY = 0.01
EPS_ADAM = 1e-08
OPT_STEP = 3


def adamw(weight, gradient, first_in, second, rate):
    first_out = BETA_ONE * first_in + (1.0 - BETA_ONE) * gradient
    second_out = BETA_TWO * second + (1.0 - BETA_TWO) * gradient * gradient
    fix_first = 1.0 - BETA_ONE**OPT_STEP
    fix_second = 1.0 - BETA_TWO**OPT_STEP
    update = first_out / fix_first / (jnp.sqrt(second_out / fix_second) + EPS_ADAM)
    return (first_out, second_out, weight - rate * (update + WEIGHT_DECAY * weight))


def adam_kernel(idx_ref, packed_ref, master_ref, first_ref, second_ref, grad_ref, fnew_ref, snew_ref, mnew_ref, copy_ref):
    rows = master_ref.shape[0]
    onehot = (
        lax.broadcasted_iota(jnp.int32, (rows, PACK_ROWS), 0) + pl.program_id(0) * rows == idx_ref[...]
    ).astype(F32).astype(BF)
    grad = dotf(onehot, packed_ref[...])
    first_new, second_new, master_new = adamw(
        master_ref[...], grad, first_ref[...], second_ref[...], LEARN_RATE
    )
    grad_ref[...] = grad
    fnew_ref[...] = first_new
    snew_ref[...] = second_new
    mnew_ref[...] = master_new
    copy_ref[...] = master_new.astype(BF)


def adam_slots(idx_row, packed, master, first, second):
    rows, model = master.shape
    tile = 144
    blk = pl.BlockSpec((tile, model), lambda i: (i, 0))
    full = lambda a: pl.BlockSpec(a.shape, lambda i: (0, 0))
    wide = jax.ShapeDtypeStruct((rows, model), F32)
    return pl.pallas_call(
        adam_kernel,
        name="adam_slots",
        grid=(rows // tile,),
        out_shape=(wide, wide, wide, wide, jax.ShapeDtypeStruct((rows, model), BF)),
        in_specs=[full(idx_row), full(packed), blk, blk, blk],
        out_specs=(blk,) * 5,
        compiler_params=pltpu.CompilerParams(vmem_limit_bytes=48 * 2**20),
    )(idx_row, packed, master, first, second)


def fast_body(
    tokens, cotangent, master_slots, first_slots, second_slots, norm_gains, gains_first, gains_second,
    bias_table, table_first, table_second, bucket_ids, valid_len, task_sizes, owner_list,
):
    chip = lax.axis_index("fsdp")
    model = tokens.shape[1]
    pack, unit = slot_tables(owner_list, chip)
    rel = rel_values(bias_table, bucket_ids)
    turned = jnp.concatenate([bucket_ids[::-1], jnp.full((1,), -1, jnp.int32)])
    bucket_row = jnp.concatenate([turned[127:], turned[:127]])[None, :]
    seq_weight = sequence_weights(valid_len.shape[0], task_sizes)
    w_all, q, k, v, ctx, probs = gather_forward(
        master_slots, pack[:, None], unit[:, :, None], tokens, norm_gains, rel, valid_len
    )
    block_out, rb, cb, gain_two, grads = ffn_pass(tokens, cotangent, ctx, norm_gains, seq_weight, w_all)
    grad_input, packed, small = reduce_backward(
        tokens, norm_gains, q, k, v, ctx, cb, bucket_row, gain_two, unit, rb, w_all, probs, grads
    )
    grad_gains = small[:2, :model]
    grad_table = small[: bias_table.shape[1], model : model + bias_table.shape[0]].T
    grad_slots, first_new, second_new, master_new, master_copy = adam_slots(
        pack[None, :], packed, master_slots, first_slots, second_slots
    )
    gains_first_new, gains_second_new, gains_new = adamw(
        norm_gains, grad_gains, gains_first, gains_second, SMALL_RATE
    )
    table_first_new, table_second_new, table_new = adamw(
        bias_table, grad_table, table_first, table_second, SMALL_RATE
    )
    return (
        block_out, grad_input, grad_slots, grad_gains, grad_table, first_new, second_new, master_new, master_copy,
        gains_first_new, gains_second_new, gains_new, table_first_new, table_second_new, table_new,
    )


def sequence_weights(seq_dev, task_sizes):
    first_seq = (lax.axis_index("dp") * lax.axis_size("fsdp") + lax.axis_index("fsdp")) * seq_dev
    seq_ids = first_seq + jnp.arange(seq_dev, dtype=jnp.int32)
    task_ends = jnp.cumsum(task_sizes)
    task_count = task_sizes.shape[0]
    task_of = jnp.sum((task_ends[None, :] <= seq_ids[:, None]).astype(jnp.int32), axis=1)
    size_of = jnp.sum(
        jnp.where(
            task_of[:, None] == jnp.arange(task_count, dtype=jnp.int32)[None, :], task_sizes[None, :], 0
        ),
        axis=1,
    )
    total = seq_dev * lax.axis_size("dp") * lax.axis_size("fsdp")
    return jnp.float32(total) / (jnp.float32(task_count) * size_of.astype(F32))


def product(left_side, right_side):
    return jnp.dot(left_side, right_side, preferred_element_type=jnp.float32)


def contract_rows(left_side, right_side):
    return lax.dot_general(
        left_side, right_side, (((0,), (0,)), ((), ())), preferred_element_type=jnp.float32
    )


def contract_cols(left_side, right_side):
    return lax.dot_general(
        left_side, right_side, (((1,), (1,)), ((), ())), preferred_element_type=jnp.float32
    )


def smooth_act(values):
    return jax.nn.gelu(values, approximate=True)


def slot_layout(owner_list, devices, capacity):
    block_count = owner_list.shape[0]
    onehot = (owner_list[:, None] == jnp.arange(devices, dtype=jnp.int32)[None, :]).astype(
        jnp.int32
    )
    rank_in = jnp.sum((jnp.cumsum(onehot, axis=0) - onehot) * onehot, axis=1)
    slot_of = owner_list * capacity + rank_in
    source = (
        jnp.zeros((devices * capacity,), jnp.int32)
        .at[slot_of]
        .set(jnp.arange(block_count, dtype=jnp.int32))
    )
    filled = (
        jnp.zeros((devices * capacity,), jnp.int32)
        .at[slot_of]
        .set(jnp.ones((block_count,), jnp.int32))
    )
    return (slot_of, source, filled, rank_in)


def split_rows(all_rows):
    model_width = all_rows.shape[1]
    hidden = (all_rows.shape[0] - 4 * model_width) // 2
    return (
        all_rows[:model_width],
        all_rows[model_width : 2 * model_width],
        all_rows[2 * model_width : 3 * model_width],
        all_rows[3 * model_width : 4 * model_width],
        all_rows[4 * model_width : 4 * model_width + hidden],
        all_rows[4 * model_width + hidden :],
    )


def norm_raw(values, gain_row):
    inv_rms = lax.rsqrt(jnp.mean(values * values, axis=-1, keepdims=True) + EPS_NORM)
    return values * inv_rms * gain_row


def expand_bias(bias_table, bucket_ids):
    length = (bucket_ids.shape[0] + 1) // 2
    onehot = jax.nn.one_hot(bucket_ids, bias_table.shape[0], dtype=jnp.float32)
    rel_rows = jnp.dot(onehot, bias_table, precision=HIGHEST)
    reverse = rel_rows[::-1].T
    tiled_rows = jnp.tile(reverse, (1, length + 1))[:, : 2 * length * length]
    return tiled_rows.reshape(reverse.shape[0], length, 2 * length)[:, :, :length][:, :, ::-1]


def masked_scores(seq_query, seq_key, rel_bias, length):
    scores = (
        jnp.einsum("qhd,khd->hqk", seq_query, seq_key, preferred_element_type=jnp.float32)
        + rel_bias
    )
    live = jnp.arange(seq_key.shape[0], dtype=jnp.int32)[None, None, :] < length
    return jnp.where(live, scores, NEG_FILL)


def adamw_step(weight, gradient, first_in, second, step_value, rate):
    first_out = BETA_ONE * first_in + (1.0 - BETA_ONE) * gradient
    second_out = BETA_TWO * second + (1.0 - BETA_TWO) * gradient * gradient
    fix_first = 1.0 - jnp.power(jnp.float32(BETA_ONE), step_value)
    fix_second = 1.0 - jnp.power(jnp.float32(BETA_TWO), step_value)
    update = first_out / fix_first / (jnp.sqrt(second_out / fix_second) + EPS_ADAM)
    return (first_out, second_out, weight - rate * (update + WEIGHT_DECAY * weight))


def plain_body(
    tokens,
    cotangent,
    master_slots,
    first_slots,
    second_slots,
    norm_gains,
    gains_first,
    gains_second,
    bias_table,
    table_first,
    table_second,
    bucket_ids,
    valid_len,
    task_sizes,
    owner_list,
):
    devices = lax.axis_size("fsdp")
    replicas = lax.axis_size("dp")
    my_index = lax.axis_index("fsdp")
    capacity = master_slots.shape[0] // BROWS
    model_width = master_slots.shape[1]
    seq_dev = valid_len.shape[0]
    slot_of, source, filled, rank_in = slot_layout(owner_list, devices, capacity)
    sent_shard = master_slots.astype(jnp.bfloat16)

    def rebuild(gathered):
        blocks = gathered.reshape(devices * capacity, BROWS, model_width)[slot_of]
        return split_rows(blocks.reshape(-1, model_width))

    def by_seq(array_in):
        return array_in.reshape(seq_dev, LEN, HEADS, HEAD_DIM)

    def to_rows(array_in):
        return array_in.reshape(-1, model_width).astype(jnp.bfloat16)

    w_query, w_key, w_value, w_out, w_in, w_down = rebuild(
        lax.all_gather(sent_shard, "fsdp", axis=0, tiled=True)
    )
    rel_bias, bias_pull = jax.vjp(lambda table_in: expand_bias(table_in, bucket_ids), bias_table)
    inputs = tokens.astype(jnp.float32)
    hidden_one, norm_one_pull = jax.vjp(norm_raw, inputs, norm_gains[0])
    hidden_one = hidden_one.astype(jnp.bfloat16)
    queries = product(hidden_one, w_query).astype(jnp.bfloat16)
    keys_in = product(hidden_one, w_key).astype(jnp.bfloat16)
    values_in = product(hidden_one, w_value).astype(jnp.bfloat16)

    def attend_one(packed):
        seq_query, seq_key, seq_value, length = packed
        scores = masked_scores(seq_query, seq_key, rel_bias, length)
        row_max = jnp.max(scores, axis=-1, keepdims=True)
        exp_scores = jnp.exp(scores - row_max)
        totals = jnp.sum(exp_scores, axis=-1, keepdims=True)
        attn_probs = (exp_scores / totals).astype(jnp.bfloat16)
        context = jnp.einsum(
            "hqk,khd->qhd", attn_probs, seq_value, preferred_element_type=jnp.float32
        )
        return (context, row_max + jnp.log(totals))

    context, log_sums = lax.map(
        attend_one, (by_seq(queries), by_seq(keys_in), by_seq(values_in), valid_len)
    )
    context = to_rows(context)
    resid = inputs + product(context, w_out)
    hidden_two, norm_two_pull = jax.vjp(norm_raw, resid, norm_gains[1])
    hidden_two = hidden_two.astype(jnp.bfloat16)
    pre_act = contract_cols(hidden_two, w_in)
    active_full, act_pull = jax.vjp(smooth_act, pre_act)
    active = active_full.astype(jnp.bfloat16)
    block_out = (resid + product(active, w_down)).astype(jnp.bfloat16)
    first_seq = (lax.axis_index("dp") * devices + my_index) * seq_dev
    seq_ids = first_seq + jnp.arange(seq_dev, dtype=jnp.int32)
    task_ends = jnp.cumsum(task_sizes)
    task_count = task_sizes.shape[0]
    task_of = jnp.sum((task_ends[None, :] <= seq_ids[:, None]).astype(jnp.int32), axis=1)
    size_of = jnp.sum(
        jnp.where(
            task_of[:, None] == jnp.arange(task_count, dtype=jnp.int32)[None, :],
            task_sizes[None, :],
            0,
        ),
        axis=1,
    )
    seq_weight = jnp.float32(seq_dev * replicas * devices) / (
        jnp.float32(task_count) * size_of.astype(jnp.float32)
    )
    back_out = (
        cotangent.astype(jnp.float32).reshape(seq_dev, LEN, model_width) * seq_weight[:, None, None]
    ).reshape(-1, model_width)
    w_query, w_key, w_value, w_out, w_in, w_down = rebuild(
        lax.all_gather(sent_shard, "fsdp", axis=0, tiled=True)
    )
    down_back = back_out.astype(jnp.bfloat16)
    grad_down = contract_rows(active, down_back)
    act_back = contract_cols(down_back, w_down)
    (pre_full,) = act_pull(act_back)
    pre_back = pre_full.astype(jnp.bfloat16)
    grad_in = contract_rows(pre_back, hidden_two)
    resid_part, gain_two = norm_two_pull(product(pre_back, w_in))
    resid_back = back_out + resid_part
    out_back = resid_back.astype(jnp.bfloat16)
    grad_out = contract_rows(context, out_back)
    context_back = contract_cols(out_back, w_out).astype(jnp.bfloat16)

    def attend_back(score_sum, packed):
        seq_query, seq_key, seq_value, seq_back, length, log_sum = packed
        scores = masked_scores(seq_query, seq_key, rel_bias, length)
        attn_probs = jnp.exp(scores - log_sum)
        value_grad = jnp.einsum(
            "hqk,qhd->khd",
            attn_probs.astype(jnp.bfloat16),
            seq_back,
            preferred_element_type=jnp.float32,
        )
        prob_grad = jnp.einsum(
            "qhd,khd->hqk", seq_back, seq_value, preferred_element_type=jnp.float32
        )
        score_back = (
            attn_probs * (prob_grad - jnp.sum(attn_probs * prob_grad, axis=-1, keepdims=True))
        ).astype(jnp.bfloat16)
        query_grad = jnp.einsum(
            "hqk,khd->qhd", score_back, seq_key, preferred_element_type=jnp.float32
        )
        key_grad = jnp.einsum(
            "hqk,qhd->khd", score_back, seq_query, preferred_element_type=jnp.float32
        )
        return (score_sum + score_back.astype(jnp.float32), (query_grad, key_grad, value_grad))

    score_sum, (query_grad, key_grad, value_grad) = lax.scan(
        attend_back,
        jnp.zeros_like(rel_bias),
        (
            by_seq(queries),
            by_seq(keys_in),
            by_seq(values_in),
            by_seq(context_back),
            valid_len,
            log_sums,
        ),
    )
    query_back = to_rows(query_grad)
    key_back = to_rows(key_grad)
    value_back = to_rows(value_grad)
    grad_query = contract_rows(hidden_one, query_back)
    grad_key = contract_rows(hidden_one, key_back)
    grad_value = contract_rows(hidden_one, value_back)
    hidden_back = (
        contract_cols(query_back, w_query)
        + contract_cols(key_back, w_key)
        + contract_cols(value_back, w_value)
    )
    input_part, gain_one = norm_one_pull(hidden_back)
    grad_input = resid_back + input_part
    (table_grad,) = bias_pull(score_sum)
    grad_rows = jnp.concatenate(
        [grad_query, grad_key, grad_value, grad_out, grad_in, grad_down], axis=0
    )
    slotted = jnp.where(
        filled[:, None, None] > 0, grad_rows.reshape(-1, BROWS, model_width)[source], 0.0
    ).reshape(-1, model_width)
    owned_grads = lax.psum_scatter(slotted, "fsdp", scatter_dimension=0, tiled=True)
    grad_slots = lax.psum(owned_grads, "dp")
    grad_gains, grad_table = lax.psum((jnp.stack([gain_one, gain_two]), table_grad), ("dp", "fsdp"))
    step_value = jnp.float32(OPT_STEP)
    first_new, second_new, master_new = adamw_step(
        master_slots, grad_slots, first_slots, second_slots, step_value, LEARN_RATE
    )
    gains_first_new, gains_second_new, gains_new = adamw_step(
        norm_gains, grad_gains, gains_first, gains_second, step_value, SMALL_RATE
    )
    table_first_new, table_second_new, table_new = adamw_step(
        bias_table, grad_table, table_first, table_second, step_value, SMALL_RATE
    )
    return (
        block_out,
        grad_input,
        grad_slots,
        grad_gains,
        grad_table,
        first_new,
        second_new,
        master_new,
        master_new.astype(jnp.bfloat16),
        gains_first_new,
        gains_second_new,
        gains_new,
        table_first_new,
        table_second_new,
        table_new,
    )


def solution(mesh):
    in_specs = (
        P(("dp", "fsdp"), None),
        P(("dp", "fsdp"), None),
        P("fsdp", None),
        P("fsdp", None),
        P("fsdp", None),
        P(),
        P(),
        P(),
        P(),
        P(),
        P(),
        P(),
        P(("dp", "fsdp")),
        P(),
        P(),
    )
    out_specs = (
        P(("dp", "fsdp"), None),
        P(("dp", "fsdp"), None),
        P("fsdp", None),
        P(),
        P(),
        P("fsdp", None),
        P("fsdp", None),
        P("fsdp", None),
        P("fsdp", None),
        P(),
        P(),
        P(),
        P(),
        P(),
        P(),
    )
    fast = dict(mesh.shape) == {"dp": 2, "fsdp": CHIPS}
    body = fast_body if fast else plain_body
    return jax.shard_map(
        body, mesh=mesh, in_specs=in_specs, out_specs=out_specs, check_vma=False)
```

```python
import functools
import jax
import jax.numpy as jnp
from jax import lax
from jax.experimental import pallas as pl
from jax.experimental.pallas import tpu as pltpu
from jax.sharding import PartitionSpec as P

HEADS = 12
HEAD_DIM = 64
LEN = 512
BROWS = 8
EPS_NORM = 1e-06
NEG_FILL = -1e30
HIGHEST = lax.Precision.HIGHEST
MESH = pl.DeviceIdType.MESH
BF = jnp.bfloat16
F32 = jnp.float32

CHIPS = 16
RANGE_BLOCKS = 72
RANGE_ROWS = 576
PAIR_ROWS = 80
PACK_ROWS = CHIPS * PAIR_ROWS
ROUNDS = 3
TILE = 128
HALF = 3 * TILE
FF_CHUNK = 512
GELU_A = 0.7978845608028654
GELU_B = 0.044715 * GELU_A
NN = (((1,), (0,)), ((), ()))
NT = (((1,), (1,)), ((), ()))
TN = (((0,), (0,)), ((), ()))
VM = pl.BlockSpec(memory_space=pltpu.VMEM)
SM = pl.BlockSpec(memory_space=pltpu.SMEM)
ANY = pl.BlockSpec(memory_space=pl.ANY)


def dotf(a, b, dims=NN):
    return lax.dot_general(a, b, dims, preferred_element_type=F32)


def unit_place(v):
    first = 1 - (v + 36) // 48
    last = (v + 30) // 48
    i = last * (v // 3 - 6)
    more = (i + 6) // 8
    rng = (
        first * (v % 4)
        + (1 - first - last) * (v // 3)
        + last * ((1 - more) * (10 + 5 * i) + more * (5 + i // 2 + 5 * (i % 2)))
    )
    return rng, first * (v // 4) + (1 - first) * (v % 3)


def unit_slice(v, core):
    rng, til = unit_place(v)
    return (
        pl.ds(pl.multiple_of(rng * RANGE_ROWS, 64), RANGE_ROWS),
        pl.ds(pl.multiple_of(core * HALF + til * TILE, TILE), TILE),
    )


def half_slice(v, core, half):
    rng, til = unit_place(v)
    return (
        pl.ds(pl.multiple_of(rng * RANGE_ROWS + half * (RANGE_ROWS // 2), 32), RANGE_ROWS // 2),
        pl.ds(pl.multiple_of(core * HALF + til * TILE, TILE), TILE),
    )


def piece_rows(i):
    return pl.ds(pl.multiple_of(i * PAIR_ROWS, 16), PAIR_ROWS)


def place():
    core = lax.axis_index("dp")
    chip = lax.axis_index("fsdp")
    xpos = chip % 2
    ypos = (chip // 2) % 2
    zpos = chip // 4
    return core, chip, xpos, ypos, zpos, chip + 1 - 2 * xpos, chip + 2 - 4 * ypos


def remote(src, dst, ssem, rsem, device):
    return pltpu.make_async_remote_copy(
        src_ref=src, dst_ref=dst, send_sem=ssem, recv_sem=rsem, device_id=device, device_id_type=MESH
    )


def as_column(row):
    return jnp.broadcast_to(row, (8, row.shape[1])).astype(F32).T[:, :1].astype(jnp.int32)


def gelu_pair(v):
    sq = v * v
    half = 0.5 + 0.5 * jnp.tanh(v * (GELU_A + GELU_B * sq))
    act = v * half
    return act, half + act * (1.0 - half) * (2.0 * GELU_A + 6.0 * GELU_B * sq)


def layer_kernel(
    idx_pack_ref, idx_row_ref, gains_ref, rel_ref, bucket_ref, len_ref, weight_ref,
    master_hbm, tokens_hbm, cot_hbm,
    out_hbm, gin_hbm, p_hbm, slot_ref, small_ref,
    weights, sib, xin, yin, dain, dbin, zin, ubuf, sendbuf, recvbuf,
    q_ref, k_ref, v_ref, ctx_ref, tokens, hidden, cb_ref, rb_ref, small, gacc,
    load_sem, out_sem, p_sem,
    fa_send, fa_recv, fz_send, fz_recv, fx_send, fx_recv, fy_send, fy_recv,
    fda_send, fda_recv, fdb_send, fdb_recv, fs_send, fs_recv,
    h_send, h_recv, da_send, da_recv, db_send, db_recv,
    x_send, x_recv, y_send, y_recv, z_send, z_recv, a2a_send, a2a_recv, half_send, half_recv,
    sm_send, sm_recv,
):
    core, chip, xpos, ypos, zpos, xnbr, ynbr = place()
    other = 1 - core
    ntok, model = tokens.shape
    hid = (weights.shape[0] - 4 * model) // 2
    nchunk = hid // FF_CHUNK
    first_in, first_down = 4 * model, 4 * model + hid
    col = ypos * 2 + xpos
    xcol = ypos * 2 + (1 - xpos)
    ycol = (1 - ypos) * 2 + xpos
    dcol = (1 - ypos) * 2 + (1 - xpos)
    own_cols = pl.ds(pl.multiple_of(core * HALF, TILE), HALF)
    tile = 256
    ntile = ntok // tile

    load_tokens = pltpu.make_async_copy(tokens_hbm, tokens, load_sem.at[0])
    load_tokens.start()

    barrier = pltpu.get_barrier_semaphore()
    for step in range(1, CHIPS):
        pl.semaphore_signal(
            barrier, inc=1, device_id=(core, lax.rem(chip + step, CHIPS)), device_id_type=MESH
        )
    pl.semaphore_signal(barrier, inc=1, device_id=(other, chip), device_id_type=MESH)

    def pack(mbuf):
        load = pltpu.make_async_copy(master_hbm.at[:, own_cols], mbuf, load_sem.at[1])
        load.start()
        load.wait()
        own_half = mbuf[...].astype(BF)
        index = as_column(idx_pack_ref[...])
        for part in range(4):
            rows = PACK_ROWS // 4
            onehot = (
                lax.broadcasted_iota(jnp.int32, (rows, mbuf.shape[0]), 1)
                == index[part * rows : (part + 1) * rows, :]
            ).astype(F32).astype(BF)
            packed = dotf(onehot, own_half).astype(BF)
            for til in range(3):
                sendbuf[til, part * rows : (part + 1) * rows, :] = packed[:, til * TILE : (til + 1) * TILE]

    pl.run_scoped(pack, pltpu.VMEM((master_hbm.shape[0], HALF), F32))
    pl.semaphore_wait(barrier, CHIPS)

    def fa_copy(rnd, step):
        dest = lax.rem(chip + step, CHIPS)
        rng, til = unit_place(rnd * CHIPS + dest)
        return remote(
            sendbuf.at[til, piece_rows(rng), :], recvbuf.at[rnd, piece_rows(chip), :],
            fa_send.at[rnd, step], fa_recv.at[rnd, step], (core, dest),
        )

    def fa_start(rnd):
        for step in range(1, CHIPS):
            fa_copy(rnd, step).start()
        rng, til = unit_place(rnd * CHIPS + chip)
        recvbuf[rnd, piece_rows(chip), :] = sendbuf[til, piece_rows(rng), :]

    def own_unit(rnd):
        for step in range(1, CHIPS):
            fa_copy(rnd, step).wait_recv()
        v = rnd * CHIPS + chip
        index = as_column(idx_row_ref[rnd : rnd + 1, :])
        for part in range(2):
            rows = RANGE_ROWS // 2
            onehot = (
                lax.broadcasted_iota(jnp.int32, (rows, PACK_ROWS), 1)
                == index[part * rows : (part + 1) * rows, :]
            ).astype(F32).astype(BF)
            weights[half_slice(v, core, part)] = dotf(onehot, recvbuf[rnd]).astype(BF)

    def behind(p, column):
        return p // 4 * CHIPS + lax.rem(zpos + 4 - p % 4, 4) * 4 + column

    def fz_copy(rnd, off):
        at = unit_slice(rnd * CHIPS + chip, core)
        dest = lax.rem(zpos + off, 4) * 4 + col
        return remote(
            weights.at[at], weights.at[at], fz_send.at[rnd, off], fz_recv.at[rnd, off], (core, dest)
        )

    def fx_copy(p):
        at = unit_slice(behind(p, col), core)
        return remote(weights.at[at], weights.at[at], fx_send.at[p], fx_recv.at[p], (core, xnbr))

    def fy_copy(p):
        at = unit_slice(behind(p, col), core)
        return remote(weights.at[at], weights.at[at], fy_send.at[p], fy_recv.at[p], (core, ynbr))

    def fda_copy(p):
        at = half_slice(behind(p, xcol), core, 0)
        return remote(weights.at[at], weights.at[at], fda_send.at[p], fda_recv.at[p], (core, ynbr))

    def fdb_copy(p):
        at = half_slice(behind(p, ycol), core, 1)
        return remote(weights.at[at], weights.at[at], fdb_send.at[p], fdb_recv.at[p], (core, xnbr))

    def fs_copy(p, kind):
        at = unit_slice(behind(p, (col, xcol, ycol, dcol)[kind]), core)
        return remote(
            weights.at[at], weights.at[at], fs_send.at[kind, p], fs_recv.at[kind, p], (other, chip)
        )

    def fz_start(rnd):
        for off in (1, 2, 3):
            fz_copy(rnd, off).start()

    def fwd_a(p):
        if p % 4:
            fz_copy(p // 4, p % 4).wait_recv()
        fx_copy(p).start()
        fy_copy(p).start()
        fs_copy(p, 0).start()

    def fwd_b(p):
        fx_copy(p).wait_recv()
        fda_copy(p).start()
        fs_copy(p, 1).start()
        fy_copy(p).wait_recv()
        fdb_copy(p).start()
        fs_copy(p, 2).start()

    def fwd_c(p):
        fda_copy(p).wait_recv()
        fdb_copy(p).wait_recv()
        fs_copy(p, 3).start()

    def fwd_done(rnd):
        for p in range(4 * rnd, 4 * rnd + 4):
            for kind in range(4):
                fs_copy(p, kind).wait_recv()

    def fwd_sent(rnd):
        for step in range(1, CHIPS):
            fa_copy(rnd, step).wait_send()
        for off in (1, 2, 3):
            fz_copy(rnd, off).wait_send()
        for p in range(4 * rnd, 4 * rnd + 4):
            fx_copy(p).wait_send()
            fy_copy(p).wait_send()
            fda_copy(p).wait_send()
            fdb_copy(p).wait_send()
            for kind in range(4):
                fs_copy(p, kind).wait_send()

    lane_head = lax.broadcasted_iota(jnp.int32, (LEN, 128), 1) // HEAD_DIM

    def forward(base, s_scr, p_scr):
        fa_start(0)
        load_tokens.wait()
        for part in range(ntok // 128):
            rows = slice(part * 128, (part + 1) * 128)
            values = tokens[rows, :].astype(F32)
            inv_rms = lax.rsqrt(jnp.mean(values * values, axis=-1, keepdims=True) + EPS_NORM)
            hidden[rows, :] = (values * inv_rms * gains_ref[0:1, :]).astype(BF)

        def bands(h, _):
            wide = jnp.broadcast_to(rel_ref[pl.ds(h, 1), :], (128, 1024))
            base[pl.ds(h, 1)] = pltpu.roll(wide, 0, 1, stride=1, stride_axis=0)[:, :896][None]
            return 0

        lax.fori_loop(0, HEADS, bands, 0)
        own_unit(0)
        fz_start(0)
        fwd_a(0)
        fa_start(1)
        fwd_a(1)
        fwd_b(0)
        fwd_a(2)
        fa_start(2)
        fwd_b(1)
        fwd_a(3)
        own_unit(1)
        fz_start(1)
        fwd_b(2)
        fwd_c(0)
        fwd_a(4)
        fwd_b(3)
        fwd_c(1)
        own_unit(2)
        fz_start(2)
        fwd_c(2)
        fwd_a(5)
        fwd_c(3)
        fwd_done(0)

        for mat, out_ref in enumerate((q_ref, k_ref, v_ref)):
            for til in range(model // 256):
                cols = slice(til * 256, (til + 1) * 256)
                out_ref[:, cols] = dotf(hidden[...], weights[mat * model : (mat + 1) * model, cols]).astype(BF)

        row_id = lax.broadcasted_iota(jnp.int32, (128, LEN), 0)

        def p_copy(step, head):
            seq, pair = step // 6, step % 6
            return pltpu.make_async_copy(
                p_scr.at[step % 2, head], p_hbm.at[seq * HEADS + pair * 2 + head], p_sem.at[step % 2, head]
            )

        def attend(step):
            seq, pair = step // 6, step % 6
            rows = pl.ds(pl.multiple_of(seq * LEN, LEN), LEN)
            lanes = pl.ds(pl.multiple_of(pair * 128, 128), 128)
            length = len_ref[seq]

            @pl.when(step >= 2)
            def _():
                for head in range(2):
                    p_copy(step - 2, head).wait()

            q_two = q_ref[rows, lanes]
            k_two = k_ref[rows, lanes]
            v_two = v_ref[rows, lanes].T
            outs = []
            for head in range(2):
                k_one = jnp.where(lane_head == head, k_two, jnp.zeros_like(k_two))
                top = jnp.full((8, LEN), NEG_FILL, F32)
                for blk in range(4):
                    score = dotf(k_one[blk * 128 : (blk + 1) * 128], q_two, NT)
                    score = score + base[pair * 2 + head, :, 384 - 128 * blk : 896 - 128 * blk]
                    score = jnp.where(row_id + blk * 128 < length, score, NEG_FILL)
                    s_scr[head, blk * 128 : (blk + 1) * 128, :] = score
                    top = jnp.maximum(top, jnp.max(score.reshape(16, 8, LEN), axis=0))
                top = jnp.max(top, axis=0, keepdims=True)
                total = jnp.zeros((8, LEN), F32)
                for blk in range(4):
                    part = jnp.exp(s_scr[head, blk * 128 : (blk + 1) * 128, :] - top)
                    s_scr[head, blk * 128 : (blk + 1) * 128, :] = part
                    total = total + jnp.sum(part.reshape(16, 8, LEN), axis=0)
                inverse = 1.0 / jnp.sum(total, axis=0, keepdims=True)
                for blk in range(4):
                    p_scr[step % 2, head, blk * 128 : (blk + 1) * 128, :] = (
                        s_scr[head, blk * 128 : (blk + 1) * 128, :] * inverse
                    ).astype(BF)
                outs.append(dotf(v_two[head * HEAD_DIM : (head + 1) * HEAD_DIM], p_scr[step % 2, head]))
                p_copy(step, head).start()
            ctx_ref[rows, lanes] = jnp.concatenate(outs, axis=0).T.astype(BF)

        plan = {
            0: (lambda: fwd_b(4),),
            1: (lambda: fwd_a(6), lambda: fwd_b(5)),
            3: (lambda: fwd_c(4), lambda: fwd_a(7), lambda: fwd_b(6)),
            5: (lambda: fwd_c(5), lambda: fwd_a(8), lambda: fwd_b(7)),
            7: (lambda: fwd_c(6), lambda: fwd_a(9), lambda: fwd_b(8)),
            9: (lambda: fwd_c(7), lambda: fwd_a(10), lambda: fwd_b(9)),
            11: (lambda: fwd_c(8), lambda: fwd_a(11), lambda: fwd_b(10)),
        }

        def attend_step(step, _):
            attend(step)
            for at, todo in plan.items():
                @pl.when(step == at)
                def _():
                    for act in todo:
                        act()
            return 0

        lax.fori_loop(0, 12, attend_step, 0)
        for step in (10, 11):
            for head in range(2):
                p_copy(step, head).wait()

    pl.run_scoped(
        forward,
        pltpu.VMEM((HEADS, 128, 896), F32),
        pltpu.VMEM((2, LEN, LEN), F32),
        pltpu.VMEM((2, 2, LEN, LEN), BF),
    )

    def src_of(p, gq):
        return gq if p < 3 else weights

    def unit(p, column):
        return p * 4 + column

    def sib_copy(p, column, gq=None):
        v = unit(p, column)
        rng, til = unit_place(v)
        return remote(
            src_of(p, gq).at[unit_slice(v, other)], sib.at[unit_slice(v, 0)],
            h_send.at[p, column], h_recv.at[p, column], (other, chip),
        )

    def da_copy(p, gq=None):
        at = half_slice(unit(p, dcol), core, 0)
        return remote(src_of(p, gq).at[at], dain.at[p], da_send.at[p], da_recv.at[p], (core, ynbr))

    def db_copy(p, gq=None):
        at = half_slice(unit(p, dcol), core, 1)
        return remote(src_of(p, gq).at[at], dbin.at[p], db_send.at[p], db_recv.at[p], (core, xnbr))

    def x_copy(p, gq=None):
        at = unit_slice(unit(p, xcol), core)
        return remote(src_of(p, gq).at[at], xin.at[p], x_send.at[p], x_recv.at[p], (core, xnbr))

    def y_copy(p, gq=None):
        at = unit_slice(unit(p, ycol), core)
        return remote(src_of(p, gq).at[at], yin.at[p], y_send.at[p], y_recv.at[p], (core, ynbr))

    def z_copy(p, gq=None):
        rnd, zt = p // 4, p % 4
        at = unit_slice(unit(p, col), core)
        return remote(
            src_of(p, gq).at[at], zin.at[rnd, zpos], z_send.at[p], z_recv.at[rnd, zpos], (core, zt * 4 + col)
        )

    def z_arrived(rnd, src):
        return remote(zin.at[rnd, src], zin.at[rnd, src], z_send.at[rnd * 4], z_recv.at[rnd, src], (core, xnbr))

    def add(ref, at, incoming):
        ref[at] = (ref[at].astype(F32) + incoming.astype(F32)).astype(BF)

    def red_s(p, gq=None):
        for column in range(4):
            sib_copy(p, column, gq).start()

    def red_0(p, gq=None):
        for column in range(4):
            sib_copy(p, column, gq).wait_recv()
            add(src_of(p, gq), unit_slice(unit(p, column), core), sib[unit_slice(unit(p, column), 0)])
        da_copy(p, gq).start()
        db_copy(p, gq).start()

    def red_1(p, gq=None):
        da_copy(p, gq).wait_recv()
        add(src_of(p, gq), half_slice(unit(p, xcol), core, 0), dain[p])
        x_copy(p, gq).start()
        db_copy(p, gq).wait_recv()
        add(src_of(p, gq), half_slice(unit(p, ycol), core, 1), dbin[p])
        y_copy(p, gq).start()

    def red_2(p, gq=None):
        x_copy(p, gq).wait_recv()
        y_copy(p, gq).wait_recv()
        at = unit_slice(unit(p, col), core)
        total = (src_of(p, gq)[at].astype(F32) + xin[p].astype(F32) + yin[p].astype(F32)).astype(BF)

        @pl.when(zpos == p % 4)
        def _():
            ubuf[p // 4] = total

        @pl.when(zpos != p % 4)
        def _():
            src_of(p, gq)[at] = total
            z_copy(p, gq).start()

    def a2a_copy(rnd, step):
        dest = lax.rem(chip + step, CHIPS)
        rng, til = unit_place(rnd * CHIPS + chip)
        return remote(
            recvbuf.at[rnd, piece_rows(dest), :],
            slot_ref.at[piece_rows(rng), pl.ds(pl.multiple_of(core * HALF + til * TILE, TILE), TILE)],
            a2a_send.at[rnd, step], a2a_recv.at[rnd, step], (core, dest),
        )

    def keep_copy(rnd):
        rng, til = unit_place(rnd * CHIPS + chip)
        return pltpu.make_async_copy(
            recvbuf.at[rnd, piece_rows(chip), :],
            slot_ref.at[piece_rows(rng), pl.ds(pl.multiple_of(core * HALF + til * TILE, TILE), TILE)],
            load_sem.at[rnd],
        )

    def red_3(rnd):
        total = ubuf[rnd].astype(F32)
        for off in (1, 2, 3):
            src = lax.rem(zpos + off, 4)
            z_arrived(rnd, src).wait_recv()
            total = total + zin[rnd, src].astype(F32)
        total = total.astype(BF)
        for part in range(4):
            rows = PACK_ROWS // 4
            onehot = (
                lax.broadcasted_iota(jnp.int32, (rows, RANGE_ROWS), 0) + part * rows
                == idx_row_ref[rnd : rnd + 1, :]
            ).astype(F32).astype(BF)
            recvbuf[rnd, part * rows : (part + 1) * rows, :] = dotf(onehot, total).astype(BF)
        for step in range(1, CHIPS):
            a2a_copy(rnd, step).start()
        keep_copy(rnd).start()

    def out_copy(i):
        rows = pl.ds(pl.multiple_of(i * tile, tile), tile)
        return pltpu.make_async_copy(hidden.at[rows], out_hbm.at[rows], out_sem.at[i])

    def feed(cot, down, out_acc, u_acc, act_s, pb_s):
        load_cot = pltpu.make_async_copy(cot_hbm, cot, load_sem.at[2])
        load_cot.start()
        load_cot.wait()
        fwd_done(1)

        def head(i, _):
            rows = pl.ds(pl.multiple_of(i * tile, tile), tile)
            value = tokens[rows, :].astype(F32) + dotf(ctx_ref[rows, :], weights[3 * model : 4 * model, :])
            rb_ref[rows, :] = value
            inv_rms = lax.rsqrt(jnp.mean(value * value, axis=-1, keepdims=True) + EPS_NORM)
            hidden[rows, :] = (value * inv_rms * gains_ref[1:2, :]).astype(BF)
            down[rows, :] = (cot[rows, :].astype(F32) * weight_ref[i * tile // LEN]).astype(BF)
            out_acc[rows, :] = jnp.zeros((tile, model), F32)
            u_acc[rows, :] = jnp.zeros((tile, model), F32)
            return 0

        lax.fori_loop(0, ntile, head, 0)
        fwd_c(9)
        fwd_b(11)
        fwd_sent(0)
        fwd_sent(1)

        plan = {
            0: (lambda: fwd_c(10), lambda: fwd_c(11), lambda: fwd_done(2), lambda: fwd_sent(2)),
            1: (lambda: red_s(6),),
            2: (lambda: red_s(7), lambda: red_s(8), lambda: red_0(6)),
            3: (lambda: red_0(7), lambda: red_1(6)),
            4: (lambda: red_s(9), lambda: red_0(8), lambda: red_1(7), lambda: red_2(6)),
            5: (
                lambda: red_s(5), lambda: red_s(10), lambda: red_s(11),
                lambda: red_0(9), lambda: red_1(8), lambda: red_2(7),
            ),
        }

        def chunk(c, _):
            rows_in = pl.ds(pl.multiple_of(first_in + c * FF_CHUNK, FF_CHUNK), FF_CHUNK)
            rows_down = pl.ds(pl.multiple_of(first_down + c * FF_CHUNK, FF_CHUNK), FF_CHUNK)
            for i in range(ntile):
                rows = slice(i * tile, (i + 1) * tile)
                pre = dotf(hidden[rows, :], weights[rows_in, :], NT)
                back = dotf(down[rows, :], weights[rows_down, :], NT)
                act, slope = gelu_pair(pre)
                act = act.astype(BF)
                pre_back = (back * slope).astype(BF)
                act_s[rows, :] = act
                pb_s[rows, :] = pre_back
                out_acc[rows, :] += dotf(act, weights[rows_down, :])
                u_acc[rows, :] += dotf(pre_back, weights[rows_in, :])
            weights[rows_down, :] = dotf(act_s[...], down[...], TN).astype(BF)
            weights[rows_in, :] = dotf(pb_s[...], hidden[...], TN).astype(BF)
            for at, todo in plan.items():
                @pl.when(c == at)
                def _():
                    for act in todo:
                        act()
            return 0

        lax.fori_loop(0, nchunk, chunk, 0)

        tail_plan = {
            1: (lambda: red_0(5), lambda: red_1(9), lambda: red_2(8)),
            3: (lambda: red_0(10), lambda: red_1(5), lambda: red_2(9)),
        }
        gacc[1] = jnp.zeros((8, model), F32)

        def tail(i, _):
            rows = pl.ds(pl.multiple_of(i * tile, tile), tile)
            value = rb_ref[rows, :]
            out = (value + out_acc[rows, :]).astype(BF)
            inv_rms = lax.rsqrt(jnp.mean(value * value, axis=-1, keepdims=True) + EPS_NORM)
            u = u_acc[rows, :]
            gu = u * gains_ref[1:2, :]
            normal = value * inv_rms
            mean = jnp.mean(gu * normal, axis=-1, keepdims=True)
            back = cot[rows, :].astype(F32) * weight_ref[i * tile // LEN] + inv_rms * (gu - normal * mean)
            rb_ref[rows, :] = back
            low = back.astype(BF)
            down[rows, :] = low
            hidden[rows, :] = out
            out_copy(i).start()
            cb_ref[rows, :] = dotf(low, weights[3 * model : 4 * model, :], NT).astype(BF)
            gacc[1] += jnp.sum((u * normal).reshape(tile // 8, 8, model), axis=0)
            for at, todo in tail_plan.items():
                @pl.when(i == at)
                def _():
                    for act in todo:
                        act()
            return 0

        lax.fori_loop(0, ntile, tail, 0)
        weights[3 * model : 4 * model, :] = dotf(ctx_ref[...], down[...], TN).astype(BF)
        red_s(4)
        red_s(3)
        red_0(11)
        red_1(10)
        red_2(5)
        for i in range(ntile):
            out_copy(i).wait()

    pl.run_scoped(
        feed,
        pltpu.VMEM((ntok, model), BF),
        pltpu.VMEM((ntok, model), BF),
        pltpu.VMEM((ntok, model), F32),
        pltpu.VMEM((ntok, model), F32),
        pltpu.VMEM((ntok, FF_CHUNK), BF),
        pltpu.VMEM((ntok, FF_CHUNK), BF),
    )

    def backward(gq, hid_t, diag, drow, p_scr, ds_scr):
        def split(step):
            turn = step // 2
            return step % 2, turn // 2 + 3 * (turn % 2)

        def p_copy(step, head):
            seq, pair = split(step)
            return pltpu.make_async_copy(
                p_hbm.at[seq * HEADS + pair * 2 + head], p_scr.at[step % 2, head], p_sem.at[step % 2, head]
            )

        for head in range(2):
            p_copy(0, head).start()
        diag[...] = jnp.zeros_like(diag)
        for part in range(ntok // 128):
            rows = slice(part * 128, (part + 1) * 128)
            values = tokens[rows, :].astype(F32)
            inv_rms = lax.rsqrt(jnp.mean(values * values, axis=-1, keepdims=True) + EPS_NORM)
            hid_t[:, rows] = (values * inv_rms * gains_ref[0:1, :]).astype(BF).T

        def attend_back(step):
            seq, pair = split(step)
            rows = pl.ds(pl.multiple_of(seq * LEN, LEN), LEN)
            lanes = pl.ds(pl.multiple_of(pair * 128, 128), 128)

            @pl.when(step + 1 < 12)
            def _():
                for head in range(2):
                    p_copy(step + 1, head).start()

            q_two, k_two, v_two, do_two = (
                q_ref[rows, lanes], k_ref[rows, lanes], v_ref[rows, lanes], cb_ref[rows, lanes]
            )
            k_turn = k_two.T
            inner = (do_two.astype(F32) * ctx_ref[rows, lanes].astype(F32)).T
            dv_parts, dk_parts, dq_parts = [], [], []
            for head in range(2):
                p_copy(step, head).wait()
                delta = jnp.sum(inner[head * HEAD_DIM : (head + 1) * HEAD_DIM], axis=0, keepdims=True)
                v_one = jnp.where(lane_head == head, v_two, jnp.zeros_like(v_two))
                for blk in range(4):
                    sub = slice(blk * 128, (blk + 1) * 128)
                    prob_back = dotf(v_one[sub], do_two, NT)
                    score = p_scr[step % 2, head, sub, :].astype(F32) * (prob_back - delta)
                    diag[pair * 2 + head, :, 384 - 128 * blk : 896 - 128 * blk] += score
                    ds_scr[head, sub, :] = score.astype(BF)
                dv_parts.append(dotf(p_scr[step % 2, head], do_two))
                dk_parts.append(dotf(ds_scr[head], q_two))
                dq_parts.append(dotf(k_turn[head * HEAD_DIM : (head + 1) * HEAD_DIM], ds_scr[head]))
            v_ref[rows, lanes] = jnp.where(lane_head == 0, dv_parts[0], dv_parts[1]).astype(BF)
            k_ref[rows, lanes] = jnp.where(lane_head == 0, dk_parts[0], dk_parts[1]).astype(BF)
            q_ref[rows, lanes] = jnp.concatenate(dq_parts, axis=0).T.astype(BF)

        def project(third):
            near = slice(third * TILE, (third + 1) * TILE)
            far = slice(HALF + third * TILE, HALF + (third + 1) * TILE)
            for mat, grad in enumerate((q_ref, k_ref, v_ref)):
                mat_rows = slice(mat * model, (mat + 1) * model)
                both = jnp.concatenate([grad[:, near], grad[:, far]], axis=1)
                value = dotf(hid_t[...], both).astype(BF)
                gq[mat_rows, near] = value[:, :TILE]
                gq[mat_rows, far] = value[:, TILE:]

        plan = {
            1: (lambda: red_0(4), lambda: red_1(11), lambda: red_2(10)),
            3: (
                lambda: project(0), lambda: red_s(0, gq), lambda: red_0(3), lambda: red_1(4), lambda: red_2(11),
            ),
            5: (lambda: red_0(0, gq), lambda: red_1(3), lambda: red_2(4)),
            7: (
                lambda: project(1), lambda: red_s(1, gq), lambda: red_1(0, gq), lambda: red_2(3), lambda: red_3(2),
            ),
            9: (lambda: red_0(1, gq), lambda: red_2(0, gq), lambda: red_3(1)),
            11: (lambda: project(2), lambda: red_s(2, gq), lambda: red_1(1, gq)),
        }

        def back_step(step, _):
            attend_back(step)
            for at, todo in plan.items():
                @pl.when(step == at)
                def _():
                    for act in todo:
                        act()
            return 0

        lax.fori_loop(0, 12, back_step, 0)

        gacc[0] = jnp.zeros((8, model), F32)

        def gin_copy(i):
            rows = slice(i * tile, (i + 1) * tile)
            return pltpu.make_async_copy(rb_ref.at[rows], gin_hbm.at[rows], out_sem.at[i])

        def tail(i):
            rows = slice(i * tile, (i + 1) * tile)
            u = (
                dotf(q_ref[rows, :], weights[:model, :], NT)
                + dotf(k_ref[rows, :], weights[model : 2 * model, :], NT)
                + dotf(v_ref[rows, :], weights[2 * model : 3 * model, :], NT)
            )
            value = tokens[rows, :].astype(F32)
            inv_rms = lax.rsqrt(jnp.mean(value * value, axis=-1, keepdims=True) + EPS_NORM)
            gu = u * gains_ref[0:1, :]
            normal = value * inv_rms
            mean = jnp.mean(gu * normal, axis=-1, keepdims=True)
            rb_ref[rows, :] += inv_rms * (gu - normal * mean)
            gin_copy(i).start()
            gacc[0] += jnp.sum((u * normal).reshape(tile // 8, 8, model), axis=0)

        def unskew(g, _):
            accs = [
                jnp.concatenate([diag[g * 4 + h], jnp.zeros((128, 128), F32)], axis=1) for h in range(4)
            ]
            size = 64
            while size >= 1:
                accs = [acc[:size] + pltpu.roll(acc[size:], 1024 - size, 1) for acc in accs]
                size //= 2
            for h in range(4):
                drow[pl.ds(g * 4 + h, 1), :] = accs[h]
            return 0

        tail(0)
        red_0(2, gq)
        tail(1)
        red_2(1, gq)
        tail(2)
        red_1(2, gq)
        tail(3)
        drow[...] = jnp.zeros_like(drow)
        lax.fori_loop(0, HEADS // 4, unskew, 0)
        onehot = (lax.broadcasted_iota(jnp.int32, (128, 1024), 0) == bucket_ref[...]).astype(F32)
        table = lax.dot_general(drow[...], onehot, NT, precision=HIGHEST, preferred_element_type=F32)
        small[0, :, :model] = jnp.zeros((16, model), F32)
        small[0, 0:1, :model] = jnp.sum(gacc[0], axis=0, keepdims=True)
        small[0, 1:2, :model] = jnp.sum(gacc[1], axis=0, keepdims=True)
        small[0, :, model:] = table
        sm_copy(0).start()
        red_2(2, gq)
        sm_next(0)
        sm_copy(1).start()
        red_3(0)
        for i in range(ntile):
            gin_copy(i).wait()
        for p in range(3):
            for column in range(4):
                sib_copy(p, column, gq).wait_send()
            da_copy(p, gq).wait_send()
            db_copy(p, gq).wait_send()
            x_copy(p, gq).wait_send()
            y_copy(p, gq).wait_send()

            @pl.when(zpos != p)
            def _():
                z_copy(p, gq).wait_send()

    def sm_copy(step):
        device = ((other, chip), (core, xnbr), (core, ynbr))[step]
        return remote(small.at[2 * step], small.at[2 * step + 1], sm_send.at[step], sm_recv.at[step], device)

    def sm_plane(off):
        return remote(
            small.at[6], small.at[7 + zpos], sm_send.at[2 + off], sm_recv.at[2 + off],
            (core, lax.rem(zpos + off, 4) * 4 + col),
        )

    def sm_next(step):
        sm_copy(step).wait_recv()
        small[2 * step + 2] = small[2 * step] + small[2 * step + 1]

    pl.run_scoped(
        backward,
        pltpu.VMEM((3 * model, model), BF),
        pltpu.VMEM((model, ntok), BF),
        pltpu.VMEM((HEADS, 128, 896), F32),
        pltpu.VMEM((16, 1024), F32),
        pltpu.VMEM((2, 2, LEN, LEN), BF),
        pltpu.VMEM((2, LEN, LEN), BF),
    )

    early = 6 * PAIR_ROWS

    def half_copy(part):
        at = (slice(0, early), slice(early, PACK_ROWS))[part]
        return remote(
            slot_ref.at[at, own_cols], slot_ref.at[at, own_cols], half_send.at[part], half_recv.at[part],
            (other, chip),
        )

    for rnd in (2, 1):
        keep_copy(rnd).wait()
        for step in range(1, CHIPS):
            a2a_copy(rnd, step).wait_recv()
    half_copy(1).start()
    sm_next(1)
    sm_copy(2).start()
    sm_next(2)
    for off in (1, 2, 3):
        sm_plane(off).start()
    small[7 + zpos] = small[6]
    keep_copy(0).wait()
    for step in range(1, CHIPS):
        a2a_copy(0, step).wait_recv()
    half_copy(0).start()
    for off in (1, 2, 3):
        sm_plane(off).wait_recv()
    small_ref[...] = small[7] + small[8] + small[9] + small[10]
    for step in range(3):
        sm_copy(step).wait_send()
    for off in (1, 2, 3):
        sm_plane(off).wait_send()
    for rnd in range(ROUNDS):
        for step in range(1, CHIPS):
            a2a_copy(rnd, step).wait_send()
    for p in range(3, 4 * ROUNDS):
        for column in range(4):
            sib_copy(p, column).wait_send()
        x_copy(p).wait_send()
        y_copy(p).wait_send()
        da_copy(p).wait_send()
        db_copy(p).wait_send()

        @pl.when(zpos != p % 4)
        def _():
            z_copy(p).wait_send()

    half_copy(1).wait()
    half_copy(0).wait()


def layer_pass(idx_pack, idx_unit, gains, rel, bucket_row, lens, seq_weight, master, tokens, cot):
    ntok, model = tokens.shape
    rows = 8 * master.shape[0]
    dma = pltpu.SemaphoreType.DMA
    half = RANGE_ROWS // 2
    pairs = 4 * ROUNDS
    act = pltpu.VMEM((ntok, model), BF)
    return pl.pallas_call(
        layer_kernel,
        name="layer_pass",
        out_shape=(
            jax.ShapeDtypeStruct((ntok, model), BF),
            jax.ShapeDtypeStruct((ntok, model), F32),
            jax.ShapeDtypeStruct((2 * HEADS, LEN, LEN), BF),
            jax.ShapeDtypeStruct((PACK_ROWS, model), BF),
            jax.ShapeDtypeStruct((16, model + 128), F32),
        ),
        in_specs=[VM] * 5 + [SM] * 2 + [ANY] * 3,
        out_specs=(ANY, ANY, ANY, ANY, VM),
        scratch_shapes=[
            pltpu.VMEM((rows, model), BF),
            pltpu.VMEM((rows, HALF), BF),
            pltpu.VMEM((pairs, RANGE_ROWS, TILE), BF),
            pltpu.VMEM((pairs, RANGE_ROWS, TILE), BF),
            pltpu.VMEM((pairs, half, TILE), BF),
            pltpu.VMEM((pairs, half, TILE), BF),
            pltpu.VMEM((ROUNDS, 4, RANGE_ROWS, TILE), BF),
            pltpu.VMEM((ROUNDS, RANGE_ROWS, TILE), BF),
            pltpu.VMEM((3, PACK_ROWS, TILE), BF),
            pltpu.VMEM((ROUNDS, PACK_ROWS, TILE), BF),
            act, act, act, act, act, act, act,
            pltpu.VMEM((ntok, model), F32),
            pltpu.VMEM((11, 16, model + 128), F32),
            pltpu.VMEM((2, 8, model), F32),
            dma((3,)), dma((4,)), dma((2, 2)),
            dma((ROUNDS, CHIPS)), dma((ROUNDS, CHIPS)), dma((ROUNDS, 4)), dma((ROUNDS, 4)),
            dma((pairs,)), dma((pairs,)), dma((pairs,)), dma((pairs,)),
            dma((pairs,)), dma((pairs,)), dma((pairs,)), dma((pairs,)),
            dma((4, pairs)), dma((4, pairs)),
            dma((pairs, 4)), dma((pairs, 4)), dma((pairs,)), dma((pairs,)), dma((pairs,)), dma((pairs,)),
            dma((pairs,)), dma((pairs,)), dma((pairs,)), dma((pairs,)), dma((pairs,)), dma((ROUNDS, 4)),
            dma((ROUNDS, CHIPS)), dma((ROUNDS, CHIPS)), dma((2,)), dma((2,)),
            dma((6,)), dma((6,)),
        ],
        compiler_params=pltpu.CompilerParams(
            collective_id=0, has_side_effects=True, vmem_limit_bytes=62 * 2**20
        ),
    )(idx_pack, idx_unit, gains, rel, bucket_row, lens, seq_weight, master, tokens, cot)


def slot_tables(owner_list, chip):
    owners = owner_list.reshape(CHIPS, RANGE_BLOCKS)
    counts = jnp.sum((owners == chip).astype(jnp.int32), axis=1)
    tri = jnp.arange(CHIPS)[:, None] > jnp.arange(CHIPS)[None, :]
    starts = jnp.sum(jnp.where(tri, counts[None, :], 0), axis=1)
    blk = jnp.arange(PAIR_ROWS // BROWS, dtype=jnp.int32)[None, :, None]
    sub = jnp.arange(BROWS, dtype=jnp.int32)[None, None, :]
    pack = jnp.where(
        blk < counts[:, None, None], (starts[:, None, None] + blk) * BROWS + sub, -1
    ).reshape(PACK_ROWS)
    v = jnp.arange(ROUNDS, dtype=jnp.int32) * CHIPS + chip
    rng, _ = unit_place(v)
    mine = jnp.stack([lax.dynamic_slice(owners, (rng[i], 0), (1, RANGE_BLOCKS))[0] for i in range(ROUNDS)])
    before = jnp.arange(RANGE_BLOCKS)[:, None] > jnp.arange(RANGE_BLOCKS)[None, :]
    rank = jnp.sum(
        ((mine[:, :, None] == mine[:, None, :]) & before[None]).astype(jnp.int32), axis=2
    )
    unit = (
        (mine * PAIR_ROWS + rank * BROWS)[:, :, None] + jnp.arange(BROWS, dtype=jnp.int32)[None, None, :]
    ).reshape(ROUNDS, RANGE_ROWS)
    return pack, unit


def rel_values(bias_table, bucket_ids):
    length = (bucket_ids.shape[0] + 1) // 2
    onehot = jax.nn.one_hot(bucket_ids, bias_table.shape[0], dtype=F32)
    rel = jnp.dot(onehot, bias_table, precision=HIGHEST)[::-1].T
    rel = jnp.concatenate([rel, jnp.zeros((HEADS, 1), F32)], axis=1)
    rel = jnp.concatenate([rel[:, 127:], rel[:, :127]], axis=1)
    return jnp.concatenate([rel, jnp.zeros((4, 2 * length), F32)], axis=0)


BETA_ONE = 0.5
BETA_TWO = 0.75
LEARN_RATE = 0.06
SMALL_RATE = 0.4
WEIGHT_DECAY = 0.01
EPS_ADAM = 1e-08
OPT_STEP = 3


def adamw(weight, gradient, first_in, second, rate):
    first_out = BETA_ONE * first_in + (1.0 - BETA_ONE) * gradient
    second_out = BETA_TWO * second + (1.0 - BETA_TWO) * gradient * gradient
    fix_first = 1.0 - BETA_ONE**OPT_STEP
    fix_second = 1.0 - BETA_TWO**OPT_STEP
    update = first_out / fix_first / (jnp.sqrt(second_out / fix_second) + EPS_ADAM)
    return (first_out, second_out, weight - rate * (update + WEIGHT_DECAY * weight))


def adam_kernel(idx_ref, packed_ref, master_ref, first_ref, second_ref, grad_ref, fnew_ref, snew_ref, mnew_ref, copy_ref):
    rows = master_ref.shape[0]
    onehot = (
        lax.broadcasted_iota(jnp.int32, (rows, PACK_ROWS), 0) + pl.program_id(0) * rows == idx_ref[...]
    ).astype(F32).astype(BF)
    grad = dotf(onehot, packed_ref[...])
    first_new, second_new, master_new = adamw(
        master_ref[...], grad, first_ref[...], second_ref[...], LEARN_RATE
    )
    grad_ref[...] = grad
    fnew_ref[...] = first_new
    snew_ref[...] = second_new
    mnew_ref[...] = master_new
    copy_ref[...] = master_new.astype(BF)


def adam_slots(idx_row, packed, master, first, second):
    rows, model = master.shape
    tile = 144
    blk = pl.BlockSpec((tile, model), lambda i: (i, 0))
    full = lambda a: pl.BlockSpec(a.shape, lambda i: (0, 0))
    wide = jax.ShapeDtypeStruct((rows, model), F32)
    return pl.pallas_call(
        adam_kernel,
        name="adam_slots",
        grid=(rows // tile,),
        out_shape=(wide, wide, wide, wide, jax.ShapeDtypeStruct((rows, model), BF)),
        in_specs=[full(idx_row), full(packed), blk, blk, blk],
        out_specs=(blk,) * 5,
        compiler_params=pltpu.CompilerParams(vmem_limit_bytes=48 * 2**20),
    )(idx_row, packed, master, first, second)


def fast_body(
    tokens, cotangent, master_slots, first_slots, second_slots, norm_gains, gains_first, gains_second,
    bias_table, table_first, table_second, bucket_ids, valid_len, task_sizes, owner_list,
):
    chip = lax.axis_index("fsdp")
    model = tokens.shape[1]
    pack, unit = slot_tables(owner_list, chip)
    rel = rel_values(bias_table, bucket_ids)
    turned = jnp.concatenate([bucket_ids[::-1], jnp.full((1,), -1, jnp.int32)])
    bucket_row = jnp.concatenate([turned[127:], turned[:127]])[None, :]
    seq_weight = sequence_weights(valid_len.shape[0], task_sizes)
    block_out, grad_input, _, packed, small = layer_pass(
        pack[None, :], unit, norm_gains, rel, bucket_row, valid_len, seq_weight, master_slots, tokens, cotangent
    )
    grad_gains = small[:2, :model]
    grad_table = small[: bias_table.shape[1], model : model + bias_table.shape[0]].T
    grad_slots, first_new, second_new, master_new, master_copy = adam_slots(
        pack[None, :], packed, master_slots, first_slots, second_slots
    )
    gains_first_new, gains_second_new, gains_new = adamw(
        norm_gains, grad_gains, gains_first, gains_second, SMALL_RATE
    )
    table_first_new, table_second_new, table_new = adamw(
        bias_table, grad_table, table_first, table_second, SMALL_RATE
    )
    return (
        block_out, grad_input, grad_slots, grad_gains, grad_table, first_new, second_new, master_new, master_copy,
        gains_first_new, gains_second_new, gains_new, table_first_new, table_second_new, table_new,
    )


def sequence_weights(seq_dev, task_sizes):
    first_seq = (lax.axis_index("dp") * lax.axis_size("fsdp") + lax.axis_index("fsdp")) * seq_dev
    seq_ids = first_seq + jnp.arange(seq_dev, dtype=jnp.int32)
    task_ends = jnp.cumsum(task_sizes)
    task_count = task_sizes.shape[0]
    task_of = jnp.sum((task_ends[None, :] <= seq_ids[:, None]).astype(jnp.int32), axis=1)
    size_of = jnp.sum(
        jnp.where(
            task_of[:, None] == jnp.arange(task_count, dtype=jnp.int32)[None, :], task_sizes[None, :], 0
        ),
        axis=1,
    )
    total = seq_dev * lax.axis_size("dp") * lax.axis_size("fsdp")
    return jnp.float32(total) / (jnp.float32(task_count) * size_of.astype(F32))


def product(left_side, right_side):
    return jnp.dot(left_side, right_side, preferred_element_type=jnp.float32)


def contract_rows(left_side, right_side):
    return lax.dot_general(
        left_side, right_side, (((0,), (0,)), ((), ())), preferred_element_type=jnp.float32
    )


def contract_cols(left_side, right_side):
    return lax.dot_general(
        left_side, right_side, (((1,), (1,)), ((), ())), preferred_element_type=jnp.float32
    )


def smooth_act(values):
    return jax.nn.gelu(values, approximate=True)


def slot_layout(owner_list, devices, capacity):
    block_count = owner_list.shape[0]
    onehot = (owner_list[:, None] == jnp.arange(devices, dtype=jnp.int32)[None, :]).astype(
        jnp.int32
    )
    rank_in = jnp.sum((jnp.cumsum(onehot, axis=0) - onehot) * onehot, axis=1)
    slot_of = owner_list * capacity + rank_in
    source = (
        jnp.zeros((devices * capacity,), jnp.int32)
        .at[slot_of]
        .set(jnp.arange(block_count, dtype=jnp.int32))
    )
    filled = (
        jnp.zeros((devices * capacity,), jnp.int32)
        .at[slot_of]
        .set(jnp.ones((block_count,), jnp.int32))
    )
    return (slot_of, source, filled, rank_in)


def split_rows(all_rows):
    model_width = all_rows.shape[1]
    hidden = (all_rows.shape[0] - 4 * model_width) // 2
    return (
        all_rows[:model_width],
        all_rows[model_width : 2 * model_width],
        all_rows[2 * model_width : 3 * model_width],
        all_rows[3 * model_width : 4 * model_width],
        all_rows[4 * model_width : 4 * model_width + hidden],
        all_rows[4 * model_width + hidden :],
    )


def norm_raw(values, gain_row):
    inv_rms = lax.rsqrt(jnp.mean(values * values, axis=-1, keepdims=True) + EPS_NORM)
    return values * inv_rms * gain_row


def expand_bias(bias_table, bucket_ids):
    length = (bucket_ids.shape[0] + 1) // 2
    onehot = jax.nn.one_hot(bucket_ids, bias_table.shape[0], dtype=jnp.float32)
    rel_rows = jnp.dot(onehot, bias_table, precision=HIGHEST)
    reverse = rel_rows[::-1].T
    tiled_rows = jnp.tile(reverse, (1, length + 1))[:, : 2 * length * length]
    return tiled_rows.reshape(reverse.shape[0], length, 2 * length)[:, :, :length][:, :, ::-1]


def masked_scores(seq_query, seq_key, rel_bias, length):
    scores = (
        jnp.einsum("qhd,khd->hqk", seq_query, seq_key, preferred_element_type=jnp.float32)
        + rel_bias
    )
    live = jnp.arange(seq_key.shape[0], dtype=jnp.int32)[None, None, :] < length
    return jnp.where(live, scores, NEG_FILL)


def adamw_step(weight, gradient, first_in, second, step_value, rate):
    first_out = BETA_ONE * first_in + (1.0 - BETA_ONE) * gradient
    second_out = BETA_TWO * second + (1.0 - BETA_TWO) * gradient * gradient
    fix_first = 1.0 - jnp.power(jnp.float32(BETA_ONE), step_value)
    fix_second = 1.0 - jnp.power(jnp.float32(BETA_TWO), step_value)
    update = first_out / fix_first / (jnp.sqrt(second_out / fix_second) + EPS_ADAM)
    return (first_out, second_out, weight - rate * (update + WEIGHT_DECAY * weight))


def plain_body(
    tokens,
    cotangent,
    master_slots,
    first_slots,
    second_slots,
    norm_gains,
    gains_first,
    gains_second,
    bias_table,
    table_first,
    table_second,
    bucket_ids,
    valid_len,
    task_sizes,
    owner_list,
):
    devices = lax.axis_size("fsdp")
    replicas = lax.axis_size("dp")
    my_index = lax.axis_index("fsdp")
    capacity = master_slots.shape[0] // BROWS
    model_width = master_slots.shape[1]
    seq_dev = valid_len.shape[0]
    slot_of, source, filled, rank_in = slot_layout(owner_list, devices, capacity)
    sent_shard = master_slots.astype(jnp.bfloat16)

    def rebuild(gathered):
        blocks = gathered.reshape(devices * capacity, BROWS, model_width)[slot_of]
        return split_rows(blocks.reshape(-1, model_width))

    def by_seq(array_in):
        return array_in.reshape(seq_dev, LEN, HEADS, HEAD_DIM)

    def to_rows(array_in):
        return array_in.reshape(-1, model_width).astype(jnp.bfloat16)

    w_query, w_key, w_value, w_out, w_in, w_down = rebuild(
        lax.all_gather(sent_shard, "fsdp", axis=0, tiled=True)
    )
    rel_bias, bias_pull = jax.vjp(lambda table_in: expand_bias(table_in, bucket_ids), bias_table)
    inputs = tokens.astype(jnp.float32)
    hidden_one, norm_one_pull = jax.vjp(norm_raw, inputs, norm_gains[0])
    hidden_one = hidden_one.astype(jnp.bfloat16)
    queries = product(hidden_one, w_query).astype(jnp.bfloat16)
    keys_in = product(hidden_one, w_key).astype(jnp.bfloat16)
    values_in = product(hidden_one, w_value).astype(jnp.bfloat16)

    def attend_one(packed):
        seq_query, seq_key, seq_value, length = packed
        scores = masked_scores(seq_query, seq_key, rel_bias, length)
        row_max = jnp.max(scores, axis=-1, keepdims=True)
        exp_scores = jnp.exp(scores - row_max)
        totals = jnp.sum(exp_scores, axis=-1, keepdims=True)
        attn_probs = (exp_scores / totals).astype(jnp.bfloat16)
        context = jnp.einsum(
            "hqk,khd->qhd", attn_probs, seq_value, preferred_element_type=jnp.float32
        )
        return (context, row_max + jnp.log(totals))

    context, log_sums = lax.map(
        attend_one, (by_seq(queries), by_seq(keys_in), by_seq(values_in), valid_len)
    )
    context = to_rows(context)
    resid = inputs + product(context, w_out)
    hidden_two, norm_two_pull = jax.vjp(norm_raw, resid, norm_gains[1])
    hidden_two = hidden_two.astype(jnp.bfloat16)
    pre_act = contract_cols(hidden_two, w_in)
    active_full, act_pull = jax.vjp(smooth_act, pre_act)
    active = active_full.astype(jnp.bfloat16)
    block_out = (resid + product(active, w_down)).astype(jnp.bfloat16)
    first_seq = (lax.axis_index("dp") * devices + my_index) * seq_dev
    seq_ids = first_seq + jnp.arange(seq_dev, dtype=jnp.int32)
    task_ends = jnp.cumsum(task_sizes)
    task_count = task_sizes.shape[0]
    task_of = jnp.sum((task_ends[None, :] <= seq_ids[:, None]).astype(jnp.int32), axis=1)
    size_of = jnp.sum(
        jnp.where(
            task_of[:, None] == jnp.arange(task_count, dtype=jnp.int32)[None, :],
            task_sizes[None, :],
            0,
        ),
        axis=1,
    )
    seq_weight = jnp.float32(seq_dev * replicas * devices) / (
        jnp.float32(task_count) * size_of.astype(jnp.float32)
    )
    back_out = (
        cotangent.astype(jnp.float32).reshape(seq_dev, LEN, model_width) * seq_weight[:, None, None]
    ).reshape(-1, model_width)
    w_query, w_key, w_value, w_out, w_in, w_down = rebuild(
        lax.all_gather(sent_shard, "fsdp", axis=0, tiled=True)
    )
    down_back = back_out.astype(jnp.bfloat16)
    grad_down = contract_rows(active, down_back)
    act_back = contract_cols(down_back, w_down)
    (pre_full,) = act_pull(act_back)
    pre_back = pre_full.astype(jnp.bfloat16)
    grad_in = contract_rows(pre_back, hidden_two)
    resid_part, gain_two = norm_two_pull(product(pre_back, w_in))
    resid_back = back_out + resid_part
    out_back = resid_back.astype(jnp.bfloat16)
    grad_out = contract_rows(context, out_back)
    context_back = contract_cols(out_back, w_out).astype(jnp.bfloat16)

    def attend_back(score_sum, packed):
        seq_query, seq_key, seq_value, seq_back, length, log_sum = packed
        scores = masked_scores(seq_query, seq_key, rel_bias, length)
        attn_probs = jnp.exp(scores - log_sum)
        value_grad = jnp.einsum(
            "hqk,qhd->khd",
            attn_probs.astype(jnp.bfloat16),
            seq_back,
            preferred_element_type=jnp.float32,
        )
        prob_grad = jnp.einsum(
            "qhd,khd->hqk", seq_back, seq_value, preferred_element_type=jnp.float32
        )
        score_back = (
            attn_probs * (prob_grad - jnp.sum(attn_probs * prob_grad, axis=-1, keepdims=True))
        ).astype(jnp.bfloat16)
        query_grad = jnp.einsum(
            "hqk,khd->qhd", score_back, seq_key, preferred_element_type=jnp.float32
        )
        key_grad = jnp.einsum(
            "hqk,qhd->khd", score_back, seq_query, preferred_element_type=jnp.float32
        )
        return (score_sum + score_back.astype(jnp.float32), (query_grad, key_grad, value_grad))

    score_sum, (query_grad, key_grad, value_grad) = lax.scan(
        attend_back,
        jnp.zeros_like(rel_bias),
        (
            by_seq(queries),
            by_seq(keys_in),
            by_seq(values_in),
            by_seq(context_back),
            valid_len,
            log_sums,
        ),
    )
    query_back = to_rows(query_grad)
    key_back = to_rows(key_grad)
    value_back = to_rows(value_grad)
    grad_query = contract_rows(hidden_one, query_back)
    grad_key = contract_rows(hidden_one, key_back)
    grad_value = contract_rows(hidden_one, value_back)
    hidden_back = (
        contract_cols(query_back, w_query)
        + contract_cols(key_back, w_key)
        + contract_cols(value_back, w_value)
    )
    input_part, gain_one = norm_one_pull(hidden_back)
    grad_input = resid_back + input_part
    (table_grad,) = bias_pull(score_sum)
    grad_rows = jnp.concatenate(
        [grad_query, grad_key, grad_value, grad_out, grad_in, grad_down], axis=0
    )
    slotted = jnp.where(
        filled[:, None, None] > 0, grad_rows.reshape(-1, BROWS, model_width)[source], 0.0
    ).reshape(-1, model_width)
    owned_grads = lax.psum_scatter(slotted, "fsdp", scatter_dimension=0, tiled=True)
    grad_slots = lax.psum(owned_grads, "dp")
    grad_gains, grad_table = lax.psum((jnp.stack([gain_one, gain_two]), table_grad), ("dp", "fsdp"))
    step_value = jnp.float32(OPT_STEP)
    first_new, second_new, master_new = adamw_step(
        master_slots, grad_slots, first_slots, second_slots, step_value, LEARN_RATE
    )
    gains_first_new, gains_second_new, gains_new = adamw_step(
        norm_gains, grad_gains, gains_first, gains_second, step_value, SMALL_RATE
    )
    table_first_new, table_second_new, table_new = adamw_step(
        bias_table, grad_table, table_first, table_second, step_value, SMALL_RATE
    )
    return (
        block_out,
        grad_input,
        grad_slots,
        grad_gains,
        grad_table,
        first_new,
        second_new,
        master_new,
        master_new.astype(jnp.bfloat16),
        gains_first_new,
        gains_second_new,
        gains_new,
        table_first_new,
        table_second_new,
        table_new,
    )


def solution(mesh):
    in_specs = (
        P(("dp", "fsdp"), None),
        P(("dp", "fsdp"), None),
        P("fsdp", None),
        P("fsdp", None),
        P("fsdp", None),
        P(),
        P(),
        P(),
        P(),
        P(),
        P(),
        P(),
        P(("dp", "fsdp")),
        P(),
        P(),
    )
    out_specs = (
        P(("dp", "fsdp"), None),
        P(("dp", "fsdp"), None),
        P("fsdp", None),
        P(),
        P(),
        P("fsdp", None),
        P("fsdp", None),
        P("fsdp", None),
        P("fsdp", None),
        P(),
        P(),
        P(),
        P(),
        P(),
        P(),
    )
    fast = dict(mesh.shape) == {"dp": 2, "fsdp": CHIPS}
    body = fast_body if fast else plain_body
    return jax.shard_map(
        body, mesh=mesh, in_specs=in_specs, out_specs=out_specs, check_vma=False)
```

```python
import functools
import jax
import jax.numpy as jnp
from jax import lax
from jax.experimental import pallas as pl
from jax.experimental.pallas import tpu as pltpu
from jax.sharding import PartitionSpec as P

HEADS = 12
HEAD_DIM = 64
LEN = 512
BROWS = 8
EPS_NORM = 1e-06
NEG_FILL = -1e30
HIGHEST = lax.Precision.HIGHEST
MESH = pl.DeviceIdType.MESH
BF = jnp.bfloat16
F32 = jnp.float32

CHIPS = 16
RANGE_BLOCKS = 72
RANGE_ROWS = 576
PAIR_ROWS = 80
PACK_ROWS = CHIPS * PAIR_ROWS
ROUNDS = 3
TILE = 128
HALF = 3 * TILE
FF_CHUNK = 512
GELU_A = 0.7978845608028654
GELU_B = 0.044715 * GELU_A
NN = (((1,), (0,)), ((), ()))
NT = (((1,), (1,)), ((), ()))
TN = (((0,), (0,)), ((), ()))
VM = pl.BlockSpec(memory_space=pltpu.VMEM)
SM = pl.BlockSpec(memory_space=pltpu.SMEM)
ANY = pl.BlockSpec(memory_space=pl.ANY)


def dotf(a, b, dims=NN):
    return lax.dot_general(a, b, dims, preferred_element_type=F32)


def unit_place(v):
    first = 1 - (v + 36) // 48
    last = (v + 30) // 48
    i = last * (v // 3 - 6)
    late, turn = i // 5, i % 5
    rng = (
        first * (v % 4)
        + (1 - first - last) * (v // 3)
        + last * (10 + 3 * late + turn // 2 - turn % 2 * (4 + late))
    )
    return rng, first * (v // 4) + (1 - first) * (v % 3)


def unit_slice(v, core):
    rng, til = unit_place(v)
    return (
        pl.ds(pl.multiple_of(rng * RANGE_ROWS, 64), RANGE_ROWS),
        pl.ds(pl.multiple_of(core * HALF + til * TILE, TILE), TILE),
    )


def half_slice(v, core, half):
    rng, til = unit_place(v)
    return (
        pl.ds(pl.multiple_of(rng * RANGE_ROWS + half * (RANGE_ROWS // 2), 32), RANGE_ROWS // 2),
        pl.ds(pl.multiple_of(core * HALF + til * TILE, TILE), TILE),
    )


def piece_rows(i):
    return pl.ds(pl.multiple_of(i * PAIR_ROWS, 16), PAIR_ROWS)


def place():
    core = lax.axis_index("dp")
    chip = lax.axis_index("fsdp")
    xpos = chip % 2
    ypos = (chip // 2) % 2
    zpos = chip // 4
    return core, chip, xpos, ypos, zpos, chip + 1 - 2 * xpos, chip + 2 - 4 * ypos


def remote(src, dst, ssem, rsem, device):
    return pltpu.make_async_remote_copy(
        src_ref=src, dst_ref=dst, send_sem=ssem, recv_sem=rsem, device_id=device, device_id_type=MESH
    )


def as_column(row):
    return jnp.broadcast_to(row, (8, row.shape[1])).astype(F32).T[:, :1].astype(jnp.int32)


def gelu_pair(v):
    sq = v * v
    half = 0.5 + 0.5 * jnp.tanh(v * (GELU_A + GELU_B * sq))
    act = v * half
    return act, half + act * (1.0 - half) * (2.0 * GELU_A + 6.0 * GELU_B * sq)


def layer_kernel(
    owner_ref, gains_ref, table_ref, buckets_ref, sizes_ref, len_ref,
    master_hbm, tokens_hbm, cot_hbm,
    out_hbm, gin_hbm, p_hbm, slot_ref, small_ref, index_ref, spare,
    weights, sib, xin, yin, dain, dbin, zin, ubuf, sendbuf, recvbuf,
    q_ref, k_ref, v_ref, ctx_ref, tokens, hidden, cb_ref, rb_ref, small, gacc,
    idx_row_ref, rel_ref, bucket_ref, weight_ref, pad,
    load_sem, out_sem, p_sem,
    fa_send, fa_recv, fz_send, fz_recv, f_send, fx_recv, fy_recv, fda_recv, fdb_recv, fs_recv,
    r_send, h_recv, da_recv, db_recv, x_recv, y_recv, z_send, z_recv, a2a_send, a2a_recv, half_send, half_recv,
    sm_send, sm_recv,
):
    core, chip, xpos, ypos, zpos, xnbr, ynbr = place()
    other = 1 - core
    ntok, model = tokens.shape
    hid = (weights.shape[0] - 4 * model) // 2
    nchunk = hid // FF_CHUNK
    first_in, first_down = 4 * model, 4 * model + hid
    col = ypos * 2 + xpos
    xcol = ypos * 2 + (1 - xpos)
    ycol = (1 - ypos) * 2 + xpos
    dcol = (1 - ypos) * 2 + (1 - xpos)
    own_cols = pl.ds(pl.multiple_of(core * HALF, TILE), HALF)
    tile = 256
    ntile = ntok // tile

    def units_copy(count, send_sem, recv_sem):
        at = spare.at[pl.ds(0, count * RANGE_ROWS)]
        return remote(at, at, send_sem, recv_sem, (other, chip))

    def pieces_copy(send_sem, recv_sem):
        at = recvbuf.at[0, pl.ds(0, (CHIPS - 1) * PAIR_ROWS)]
        return remote(at, at, send_sem, recv_sem, (other, chip))

    load_tokens = pltpu.make_async_copy(tokens_hbm, tokens, load_sem.at[0])
    load_tokens.start()

    barrier = pltpu.get_barrier_semaphore()
    for step in range(1, CHIPS):
        pl.semaphore_signal(
            barrier, inc=1, device_id=(core, lax.rem(chip + step, CHIPS)), device_id_type=MESH
        )
    pl.semaphore_signal(barrier, inc=1, device_id=(other, chip), device_id_type=MESH)

    def lanes(rows, width):
        return lax.broadcasted_iota(jnp.int32, (rows, width), 1)

    def steps(rows, width):
        return lax.broadcasted_iota(jnp.int32, (rows, width), 0)

    def mark(mask):
        return mask.astype(F32).astype(BF)

    def eight(row):
        return jnp.broadcast_to(row, (8, row.shape[1]))

    owners = owner_ref[...]
    nblock = owners.shape[1]

    def pack_index():
        mine = mark(eight(owners == chip))
        block, low = steps(nblock, 128), lanes(nblock, 128) * RANGE_BLOCKS
        count = dotf(mine, mark(jnp.logical_and(block >= low, block < low + RANGE_BLOCKS)))
        start = dotf(mine, mark(block < low))
        row, low = lanes(128, PACK_ROWS), steps(128, PACK_ROWS) * PAIR_ROWS
        spread = mark(jnp.logical_and(row >= low, row < low + PAIR_ROWS))
        count = dotf(count.astype(BF), spread)
        start = dotf(start.astype(BF), spread)
        rng = dotf(lanes(8, 128).astype(F32).astype(BF), spread)
        inner = lanes(8, PACK_ROWS).astype(F32) - PAIR_ROWS * rng
        turn = jnp.floor(inner * (1.0 / BROWS))
        index = jnp.where(turn < count, start * BROWS + inner, -1.0)
        index_ref[...] = index.astype(jnp.int32)

    def unit_index():
        row, low = lanes(128, RANGE_ROWS), steps(128, RANGE_ROWS) * BROWS
        spread = mark(jnp.logical_and(row >= low, row < low + BROWS))
        inner = lanes(8, RANGE_ROWS).astype(F32) - BROWS * dotf(lanes(8, 128).astype(F32).astype(BF), spread)
        values = eight(owners).astype(F32).astype(BF)
        for rnd in range(ROUNDS):
            rng, _ = unit_place(rnd * CHIPS + chip)
            at = lanes(nblock, 128)
            pick = jnp.logical_and(steps(nblock, 128) == at + rng * RANGE_BLOCKS, at < RANGE_BLOCKS)
            owner = dotf(values, mark(pick))
            same = jnp.logical_and(owner.T[:, :1] == owner[:1], steps(128, 128) < lanes(128, 128))
            rank = jnp.sum(same.astype(F32), axis=0, keepdims=True)
            index = (
                PAIR_ROWS * dotf(owner.astype(BF), spread)
                + BROWS * dotf(eight(rank).astype(BF), spread)
                + inner
            )
            idx_row_ref[rnd : rnd + 1, :] = index[:1].astype(jnp.int32)

    def relative():
        count = buckets_ref.shape[1]
        pad[...] = jnp.full((16, 128), 127.0, F32)
        for i in range(8):
            width = min(128, count - 128 * i)
            pad[i : i + 1, :width] = buckets_ref[:, 128 * i : 128 * i + width].astype(F32)
        turned = dotf(pad[:8].astype(BF), mark(steps(128, 128) + lanes(128, 128) == 127))
        for i in range(8):
            source = 6 - i if i < 7 else 7
            bucket_ref[:, 128 * i : 128 * (i + 1)] = turned[source : source + 1].astype(jnp.int32)
        pad[...] = jnp.zeros((16, 128), F32)
        pad[: table_ref.shape[0], : table_ref.shape[1]] = table_ref[...]
        rel_ref[...] = lax.dot_general(
            pad[...], (steps(128, 1024) == bucket_ref[...]).astype(F32), NN,
            precision=HIGHEST, preferred_element_type=F32,
        )

    def sequence_weights():
        count = sizes_ref.shape[1]
        seqs = ntok // LEN
        pad[...] = jnp.zeros((16, 128), F32)
        pad[:1, :count] = sizes_ref[...].astype(F32)
        sizes = pad[:8]
        ends = dotf(sizes.astype(BF), mark(steps(128, 128) <= lanes(128, 128)))
        for i in range(seqs):
            seq = ((core * CHIPS + chip) * seqs + i).astype(F32)
            inside = jnp.logical_and(ends - sizes <= seq, seq < ends)
            size = jnp.sum(jnp.where(inside, sizes, 0.0)[:1], axis=1, keepdims=True)
            weight = jnp.float32(seqs * 2 * CHIPS) / (jnp.float32(count) * size)
            weight_ref[i : i + 1, :] = jnp.broadcast_to(weight, (1, model))

    def pack(mbuf):
        load = pltpu.make_async_copy(master_hbm.at[:, own_cols], mbuf, load_sem.at[1])
        load.start()
        pack_index()
        load.wait()
        own_half = mbuf[...].astype(BF)
        index = as_column(index_ref[:1, :])
        for part in range(4):
            rows = PACK_ROWS // 4
            onehot = (
                lax.broadcasted_iota(jnp.int32, (rows, mbuf.shape[0]), 1)
                == index[part * rows : (part + 1) * rows, :]
            ).astype(F32).astype(BF)
            packed = dotf(onehot, own_half).astype(BF)
            for til in range(3):
                sendbuf[til, part * rows : (part + 1) * rows, :] = packed[:, til * TILE : (til + 1) * TILE]

    pl.run_scoped(pack, pltpu.VMEM((master_hbm.shape[0], HALF), F32))
    pl.semaphore_wait(barrier, CHIPS)

    def fa_copy(rnd, step):
        dest = lax.rem(chip + step, CHIPS)
        rng, til = unit_place(rnd * CHIPS + dest)
        return remote(
            sendbuf.at[til, piece_rows(rng), :], recvbuf.at[rnd, piece_rows(chip), :],
            fa_send.at[rnd], fa_recv.at[rnd], (core, dest),
        )

    def fa_start(rnd):
        for step in range(1, CHIPS):
            fa_copy(rnd, step).start()
        rng, til = unit_place(rnd * CHIPS + chip)
        recvbuf[rnd, piece_rows(chip), :] = sendbuf[til, piece_rows(rng), :]

    def own_unit(rnd):
        pieces_copy(fa_send.at[rnd], fa_recv.at[rnd]).wait_recv()
        v = rnd * CHIPS + chip
        index = as_column(idx_row_ref[rnd : rnd + 1, :])
        for part in range(2):
            rows = RANGE_ROWS // 2
            onehot = (
                lax.broadcasted_iota(jnp.int32, (rows, PACK_ROWS), 1)
                == index[part * rows : (part + 1) * rows, :]
            ).astype(F32).astype(BF)
            weights[half_slice(v, core, part)] = dotf(onehot, recvbuf[rnd]).astype(BF)

    def nearest(k):
        return (zpos, zpos + 1 - 2 * (zpos % 2), 2 - zpos // 2, 3 - 3 * (zpos // 2))[k]

    def behind(p):
        return nearest(p % 4) if p < 8 else p % 4

    def fwd_unit(p, column):
        return p // 4 * CHIPS + behind(p) * 4 + column

    def fz_copy(rnd, source, up):
        at = unit_slice(rnd * CHIPS + source * 4 + col, core)
        dest = chip + (4 if up else -4)
        return remote(weights.at[at], weights.at[at], fz_send.at[rnd], fz_recv.at[rnd, source], (core, dest))

    def fz_start(rnd):
        @pl.when(zpos < 3)
        def _():
            fz_copy(rnd, zpos, True).start()

        @pl.when(zpos > 0)
        def _():
            fz_copy(rnd, zpos, False).start()

    def fz_relay(rnd, k):
        source = nearest(k)
        units_copy(1, fz_send.at[rnd], fz_recv.at[rnd, source]).wait_recv()

        @pl.when(jnp.logical_and(source < zpos, zpos < 3))
        def _():
            fz_copy(rnd, source, True).start()

        @pl.when(jnp.logical_and(source > zpos, zpos > 0))
        def _():
            fz_copy(rnd, source, False).start()

    def fz_sent(rnd):
        inner = zpos % 3 > 0

        @pl.when(inner)
        def _():
            units_copy(5, fz_send.at[rnd], fz_recv.at[rnd, 0]).wait_send()

        @pl.when(jnp.logical_not(inner))
        def _():
            units_copy(1, fz_send.at[rnd], fz_recv.at[rnd, 0]).wait_send()

    def fx_copy(p):
        at = unit_slice(fwd_unit(p, col), core)
        return remote(weights.at[at], weights.at[at], f_send.at[p], fx_recv.at[p], (core, xnbr))

    def fy_copy(p):
        at = unit_slice(fwd_unit(p, col), core)
        return remote(weights.at[at], weights.at[at], f_send.at[p], fy_recv.at[p], (core, ynbr))

    def fda_copy(p):
        at = half_slice(fwd_unit(p, xcol), core, 0)
        return remote(weights.at[at], weights.at[at], f_send.at[p], fda_recv.at[p], (core, ynbr))

    def fdb_copy(p):
        at = half_slice(fwd_unit(p, ycol), core, 1)
        return remote(weights.at[at], weights.at[at], f_send.at[p], fdb_recv.at[p], (core, xnbr))

    def fs_copy(p, kind):
        at = unit_slice(fwd_unit(p, (col, xcol, ycol, dcol)[kind]), core)
        return remote(weights.at[at], weights.at[at], f_send.at[p], fs_recv.at[p], (other, chip))

    def fwd_a(p):
        if p < 8 and p % 4:
            fz_relay(p // 4, p % 4)
        fx_copy(p).start()
        fy_copy(p).start()
        fs_copy(p, 0).start()

    def fwd_b(p):
        fx_copy(p).wait_recv()
        fda_copy(p).start()
        fs_copy(p, 1).start()
        fy_copy(p).wait_recv()
        fdb_copy(p).start()
        fs_copy(p, 2).start()

    def fwd_c(p):
        fda_copy(p).wait_recv()
        fdb_copy(p).wait_recv()
        fs_copy(p, 3).start()

    def fwd_done(*pairs):
        for p in pairs:
            units_copy(4, f_send.at[p], fs_recv.at[p]).wait_recv()

    def fwd_sent(rounds, pairs):
        for rnd in rounds:
            pieces_copy(fa_send.at[rnd], fa_recv.at[rnd]).wait_send()
            fz_sent(rnd)
        for p in pairs:
            units_copy(7, f_send.at[p], fs_recv.at[p]).wait_send()

    lane_head = lax.broadcasted_iota(jnp.int32, (LEN, 128), 1) // HEAD_DIM

    def forward(base, s_scr, p_scr):
        fa_start(0)
        unit_index()
        relative()
        sequence_weights()
        load_tokens.wait()
        for part in range(ntok // 128):
            rows = slice(part * 128, (part + 1) * 128)
            values = tokens[rows, :].astype(F32)
            inv_rms = lax.rsqrt(jnp.mean(values * values, axis=-1, keepdims=True) + EPS_NORM)
            hidden[rows, :] = (values * inv_rms * gains_ref[0:1, :]).astype(BF)

        def bands(h, _):
            wide = jnp.broadcast_to(rel_ref[pl.ds(h, 1), :], (128, 1024))
            base[pl.ds(h, 1)] = pltpu.roll(wide, 0, 1, stride=1, stride_axis=0)[:, :896][None]
            return 0

        lax.fori_loop(0, HEADS, bands, 0)
        own_unit(0)
        fz_start(0)
        fwd_a(0)
        fwd_a(1)
        fwd_b(0)
        fwd_a(2)
        fa_start(1)
        fwd_b(1)
        fwd_c(0)
        fwd_a(3)
        fwd_b(2)
        fwd_c(1)
        own_unit(1)
        fz_start(1)
        fwd_a(4)
        fa_start(2)
        fwd_b(3)
        fwd_c(2)
        fwd_c(3)
        fwd_done(0, 1, 2, 3)

        between = ((lambda: fwd_a(5),), (lambda: fwd_b(4),), (lambda: fwd_a(6),))
        for mat, out_ref in enumerate((q_ref, k_ref, v_ref)):
            for til in range(model // 256):
                cols = slice(til * 256, (til + 1) * 256)
                out_ref[:, cols] = dotf(hidden[...], weights[mat * model : (mat + 1) * model, cols]).astype(BF)
            for act in between[mat]:
                act()

        row_id = lax.broadcasted_iota(jnp.int32, (128, LEN), 0)

        def p_copy(step, head):
            seq, pair = step // 6, step % 6
            return pltpu.make_async_copy(
                p_scr.at[step % 2, head], p_hbm.at[seq * HEADS + pair * 2 + head], p_sem.at[step % 2, head]
            )

        def attend(step):
            seq, pair = step // 6, step % 6
            rows = pl.ds(pl.multiple_of(seq * LEN, LEN), LEN)
            lanes = pl.ds(pl.multiple_of(pair * 128, 128), 128)
            length = len_ref[seq]

            @pl.when(step >= 2)
            def _():
                for head in range(2):
                    p_copy(step - 2, head).wait()

            q_two = q_ref[rows, lanes]
            k_two = k_ref[rows, lanes]
            v_two = v_ref[rows, lanes].T
            outs = []
            for head in range(2):
                k_one = jnp.where(lane_head == head, k_two, jnp.zeros_like(k_two))
                top = jnp.full((8, LEN), NEG_FILL, F32)
                for blk in range(4):
                    score = dotf(k_one[blk * 128 : (blk + 1) * 128], q_two, NT)
                    score = score + base[pair * 2 + head, :, 384 - 128 * blk : 896 - 128 * blk]
                    score = jnp.where(row_id + blk * 128 < length, score, NEG_FILL)
                    s_scr[head, blk * 128 : (blk + 1) * 128, :] = score
                    top = jnp.maximum(top, jnp.max(score.reshape(16, 8, LEN), axis=0))
                top = jnp.max(top, axis=0, keepdims=True)
                total = jnp.zeros((8, LEN), F32)
                for blk in range(4):
                    part = jnp.exp(s_scr[head, blk * 128 : (blk + 1) * 128, :] - top)
                    s_scr[head, blk * 128 : (blk + 1) * 128, :] = part
                    total = total + jnp.sum(part.reshape(16, 8, LEN), axis=0)
                inverse = 1.0 / jnp.sum(total, axis=0, keepdims=True)
                for blk in range(4):
                    p_scr[step % 2, head, blk * 128 : (blk + 1) * 128, :] = (
                        s_scr[head, blk * 128 : (blk + 1) * 128, :] * inverse
                    ).astype(BF)
                outs.append(dotf(v_two[head * HEAD_DIM : (head + 1) * HEAD_DIM], p_scr[step % 2, head]))
                p_copy(step, head).start()
            ctx_ref[rows, lanes] = jnp.concatenate(outs, axis=0).T.astype(BF)

        plan = {
            0: (lambda: own_unit(2), lambda: fz_start(2), lambda: fwd_b(5), lambda: fwd_c(4)),
            1: (lambda: fwd_a(7),),
            2: (lambda: fz_relay(2, 1), lambda: fwd_c(5)),
            3: (lambda: fwd_b(6),),
            5: (lambda: fz_relay(2, 2), lambda: fwd_b(7), lambda: fwd_c(6)),
            7: (lambda: fz_relay(2, 3), lambda: fwd_a(8)),
            8: (lambda: fwd_c(7), lambda: fwd_a(9), lambda: fwd_b(8)),
            10: (lambda: fwd_a(10), lambda: fwd_b(9), lambda: fwd_c(8)),
        }

        def attend_step(step, _):
            attend(step)
            for at, todo in plan.items():
                @pl.when(step == at)
                def _():
                    for act in todo:
                        act()
            return 0

        lax.fori_loop(0, 12, attend_step, 0)
        for step in (10, 11):
            for head in range(2):
                p_copy(step, head).wait()

    pl.run_scoped(
        forward,
        pltpu.VMEM((HEADS, 128, 896), F32),
        pltpu.VMEM((2, LEN, LEN), F32),
        pltpu.VMEM((2, 2, LEN, LEN), BF),
    )

    def src_of(p, gq):
        return gq if p < 3 else weights

    def unit(p, column):
        return p * 4 + column

    def sib_copy(p, column, gq=None):
        v = unit(p, column)
        return remote(
            src_of(p, gq).at[unit_slice(v, other)], sib.at[unit_slice(v, 0)],
            r_send.at[p], h_recv.at[p], (other, chip),
        )

    def da_copy(p, gq=None):
        at = half_slice(unit(p, dcol), core, 0)
        return remote(src_of(p, gq).at[at], dain.at[p], r_send.at[p], da_recv.at[p], (core, ynbr))

    def db_copy(p, gq=None):
        at = half_slice(unit(p, dcol), core, 1)
        return remote(src_of(p, gq).at[at], dbin.at[p], r_send.at[p], db_recv.at[p], (core, xnbr))

    def x_copy(p, gq=None):
        at = unit_slice(unit(p, xcol), core)
        return remote(src_of(p, gq).at[at], xin.at[p], r_send.at[p], x_recv.at[p], (core, xnbr))

    def y_copy(p, gq=None):
        at = unit_slice(unit(p, ycol), core)
        return remote(src_of(p, gq).at[at], yin.at[p], r_send.at[p], y_recv.at[p], (core, ynbr))

    def z_copy(p, gq=None):
        rnd, zt = p // 4, p % 4
        at = unit_slice(unit(p, col), core)
        return remote(
            src_of(p, gq).at[at], zin.at[rnd, zpos], z_send.at[rnd], z_recv.at[rnd, zpos], (core, zt * 4 + col)
        )

    def z_arrived(rnd, src):
        return remote(zin.at[rnd, src], zin.at[rnd, src], z_send.at[rnd], z_recv.at[rnd, src], (core, xnbr))

    def add(ref, at, incoming):
        ref[at] = (ref[at].astype(F32) + incoming.astype(F32)).astype(BF)

    def red_s(p, gq=None):
        for column in range(4):
            sib_copy(p, column, gq).start()

    def red_0(p, gq=None):
        units_copy(4, r_send.at[p], h_recv.at[p]).wait_recv()
        for column in range(4):
            add(src_of(p, gq), unit_slice(unit(p, column), core), sib[unit_slice(unit(p, column), 0)])
        da_copy(p, gq).start()
        db_copy(p, gq).start()

    def red_1(p, gq=None):
        da_copy(p, gq).wait_recv()
        add(src_of(p, gq), half_slice(unit(p, xcol), core, 0), dain[p])
        x_copy(p, gq).start()
        db_copy(p, gq).wait_recv()
        add(src_of(p, gq), half_slice(unit(p, ycol), core, 1), dbin[p])
        y_copy(p, gq).start()

    def red_2(p, gq=None):
        x_copy(p, gq).wait_recv()
        y_copy(p, gq).wait_recv()
        at = unit_slice(unit(p, col), core)
        total = (src_of(p, gq)[at].astype(F32) + xin[p].astype(F32) + yin[p].astype(F32)).astype(BF)

        @pl.when(zpos == p % 4)
        def _():
            ubuf[p // 4] = total

        @pl.when(zpos != p % 4)
        def _():
            src_of(p, gq)[at] = total
            z_copy(p, gq).start()

    def a2a_copy(rnd, step):
        dest = lax.rem(chip + step, CHIPS)
        rng, til = unit_place(rnd * CHIPS + chip)
        return remote(
            recvbuf.at[rnd, piece_rows(dest), :],
            slot_ref.at[piece_rows(rng), pl.ds(pl.multiple_of(core * HALF + til * TILE, TILE), TILE)],
            a2a_send.at[rnd], a2a_recv.at[rnd], (core, dest),
        )

    def keep_copy(rnd):
        rng, til = unit_place(rnd * CHIPS + chip)
        return pltpu.make_async_copy(
            recvbuf.at[rnd, piece_rows(chip), :],
            slot_ref.at[piece_rows(rng), pl.ds(pl.multiple_of(core * HALF + til * TILE, TILE), TILE)],
            load_sem.at[rnd],
        )

    def red_3(rnd):
        total = ubuf[rnd].astype(F32)
        for off in (1, 2, 3):
            src = lax.rem(zpos + off, 4)
            z_arrived(rnd, src).wait_recv()
            total = total + zin[rnd, src].astype(F32)
        total = total.astype(BF)
        for part in range(4):
            rows = PACK_ROWS // 4
            onehot = (
                lax.broadcasted_iota(jnp.int32, (rows, RANGE_ROWS), 0) + part * rows
                == idx_row_ref[rnd : rnd + 1, :]
            ).astype(F32).astype(BF)
            recvbuf[rnd, part * rows : (part + 1) * rows, :] = dotf(onehot, total).astype(BF)
        for step in range(1, CHIPS):
            a2a_copy(rnd, step).start()
        keep_copy(rnd).start()

    def red_sent(pairs):
        for p in pairs:
            units_copy(7, r_send.at[p], h_recv.at[p]).wait_send()

    def red_3_at(plane):
        @pl.when(zpos == plane)
        def _():
            red_3(0)

    def out_copy(i):
        rows = pl.ds(pl.multiple_of(i * tile, tile), tile)
        return pltpu.make_async_copy(hidden.at[rows], out_hbm.at[rows], out_sem.at[i])

    def feed(cot, down, out_acc, u_acc, act_s, pb_s):
        load_cot = pltpu.make_async_copy(cot_hbm, cot, load_sem.at[2])
        load_cot.start()
        load_cot.wait()
        fwd_done(4, 5, 6, 7)

        def head(i, _):
            rows = pl.ds(pl.multiple_of(i * tile, tile), tile)
            value = tokens[rows, :].astype(F32) + dotf(ctx_ref[rows, :], weights[3 * model : 4 * model, :])
            rb_ref[rows, :] = value
            inv_rms = lax.rsqrt(jnp.mean(value * value, axis=-1, keepdims=True) + EPS_NORM)
            hidden[rows, :] = (value * inv_rms * gains_ref[1:2, :]).astype(BF)
            down[rows, :] = (cot[rows, :].astype(F32) * weight_ref[pl.ds(i * tile // LEN, 1), :]).astype(BF)
            out_acc[rows, :] = jnp.zeros((tile, model), F32)
            u_acc[rows, :] = jnp.zeros((tile, model), F32)
            return 0

        lax.fori_loop(0, ntile, head, 0)
        fwd_a(11)
        fwd_b(10)

        middle = {
            0: (lambda: fwd_c(9), lambda: fwd_sent((0, 1), range(8))),
            1: (lambda: fwd_c(11), lambda: fwd_sent((2,), (8,))),
            3: (lambda: red_0(6), lambda: fwd_sent((), (9, 10))),
            4: (lambda: red_1(6), lambda: red_0(8), lambda: fwd_sent((), (11,))),
            5: (lambda: red_2(6), lambda: red_0(9), lambda: red_1(8)),
        }
        plan = {
            0: (lambda: fwd_done(8), lambda: fwd_b(11), lambda: fwd_c(10)),
            2: (lambda: red_s(6), lambda: red_s(7), lambda: fwd_done(9, 10)),
            3: (lambda: red_s(8), lambda: red_0(7), lambda: fwd_done(11)),
            4: (lambda: red_s(9), lambda: red_1(7)),
            5: (lambda: red_s(5), lambda: red_s(10), lambda: red_s(11), lambda: red_2(7)),
        }

        def run(what, now):
            for at, todo in what.items():
                @pl.when(now == at)
                def _():
                    for act in todo:
                        act()

        def chunk(c, _):
            rows_in = pl.ds(pl.multiple_of(first_in + c * FF_CHUNK, FF_CHUNK), FF_CHUNK)
            rows_down = pl.ds(pl.multiple_of(first_down + c * FF_CHUNK, FF_CHUNK), FF_CHUNK)
            for i in range(ntile):
                rows = slice(i * tile, (i + 1) * tile)
                pre = dotf(hidden[rows, :], weights[rows_in, :], NT)
                back = dotf(down[rows, :], weights[rows_down, :], NT)
                act, slope = gelu_pair(pre)
                act = act.astype(BF)
                pre_back = (back * slope).astype(BF)
                act_s[rows, :] = act
                pb_s[rows, :] = pre_back
                out_acc[rows, :] += dotf(act, weights[rows_down, :])
                u_acc[rows, :] += dotf(pre_back, weights[rows_in, :])
            run(middle, c)
            weights[rows_down, :] = dotf(act_s[...], down[...], TN).astype(BF)
            weights[rows_in, :] = dotf(pb_s[...], hidden[...], TN).astype(BF)
            run(plan, c)
            return 0

        lax.fori_loop(0, nchunk, chunk, 0)

        tail_plan = {
            0: (lambda: red_0(5),),
            1: (lambda: red_1(9),),
            2: (lambda: red_0(10),),
            3: (lambda: red_2(8),),
        }
        gacc[1] = jnp.zeros((8, model), F32)

        def tail(i, _):
            rows = pl.ds(pl.multiple_of(i * tile, tile), tile)
            value = rb_ref[rows, :]
            out = (value + out_acc[rows, :]).astype(BF)
            inv_rms = lax.rsqrt(jnp.mean(value * value, axis=-1, keepdims=True) + EPS_NORM)
            u = u_acc[rows, :]
            gu = u * gains_ref[1:2, :]
            normal = value * inv_rms
            mean = jnp.mean(gu * normal, axis=-1, keepdims=True)
            back = cot[rows, :].astype(F32) * weight_ref[pl.ds(i * tile // LEN, 1), :] + inv_rms * (gu - normal * mean)
            rb_ref[rows, :] = back
            low = back.astype(BF)
            down[rows, :] = low
            hidden[rows, :] = out
            out_copy(i).start()
            cb_ref[rows, :] = dotf(low, weights[3 * model : 4 * model, :], NT).astype(BF)
            gacc[1] += jnp.sum((u * normal).reshape(tile // 8, 8, model), axis=0)
            run(tail_plan, i)
            return 0

        lax.fori_loop(0, ntile, tail, 0)
        weights[3 * model : 4 * model, :] = dotf(ctx_ref[...], down[...], TN).astype(BF)
        red_s(4)
        red_s(3)
        red_1(5)
        for i in range(ntile):
            out_copy(i).wait()

    pl.run_scoped(
        feed,
        pltpu.VMEM((ntok, model), BF),
        pltpu.VMEM((ntok, model), BF),
        pltpu.VMEM((ntok, model), F32),
        pltpu.VMEM((ntok, model), F32),
        pltpu.VMEM((ntok, FF_CHUNK), BF),
        pltpu.VMEM((ntok, FF_CHUNK), BF),
    )

    def backward(gq, hid_t, diag, drow, p_scr, ds_scr):
        def split(step):
            turn = step // 2
            return step % 2, turn // 2 + 3 * (turn % 2)

        def p_copy(step, head):
            seq, pair = split(step)
            return pltpu.make_async_copy(
                p_hbm.at[seq * HEADS + pair * 2 + head], p_scr.at[step % 2, head], p_sem.at[step % 2, head]
            )

        for head in range(2):
            p_copy(0, head).start()
        diag[...] = jnp.zeros_like(diag)
        for part in range(ntok // 128):
            rows = slice(part * 128, (part + 1) * 128)
            values = tokens[rows, :].astype(F32)
            inv_rms = lax.rsqrt(jnp.mean(values * values, axis=-1, keepdims=True) + EPS_NORM)
            hid_t[:, rows] = (values * inv_rms * gains_ref[0:1, :]).astype(BF).T

        def attend_back(step):
            seq, pair = split(step)
            rows = pl.ds(pl.multiple_of(seq * LEN, LEN), LEN)
            lanes = pl.ds(pl.multiple_of(pair * 128, 128), 128)

            @pl.when(step + 1 < 12)
            def _():
                for head in range(2):
                    p_copy(step + 1, head).start()

            q_two, k_two, v_two, do_two = (
                q_ref[rows, lanes], k_ref[rows, lanes], v_ref[rows, lanes], cb_ref[rows, lanes]
            )
            k_turn = k_two.T
            inner = (do_two.astype(F32) * ctx_ref[rows, lanes].astype(F32)).T
            dv_parts, dk_parts, dq_parts = [], [], []
            for head in range(2):
                p_copy(step, head).wait()
                delta = jnp.sum(inner[head * HEAD_DIM : (head + 1) * HEAD_DIM], axis=0, keepdims=True)
                v_one = jnp.where(lane_head == head, v_two, jnp.zeros_like(v_two))
                for blk in range(4):
                    sub = slice(blk * 128, (blk + 1) * 128)
                    prob_back = dotf(v_one[sub], do_two, NT)
                    score = p_scr[step % 2, head, sub, :].astype(F32) * (prob_back - delta)
                    diag[pair * 2 + head, :, 384 - 128 * blk : 896 - 128 * blk] += score
                    ds_scr[head, sub, :] = score.astype(BF)
                dv_parts.append(dotf(p_scr[step % 2, head], do_two))
                dk_parts.append(dotf(ds_scr[head], q_two))
                dq_parts.append(dotf(k_turn[head * HEAD_DIM : (head + 1) * HEAD_DIM], ds_scr[head]))
            v_ref[rows, lanes] = jnp.where(lane_head == 0, dv_parts[0], dv_parts[1]).astype(BF)
            k_ref[rows, lanes] = jnp.where(lane_head == 0, dk_parts[0], dk_parts[1]).astype(BF)
            q_ref[rows, lanes] = jnp.concatenate(dq_parts, axis=0).T.astype(BF)

        def project(third):
            near = slice(third * TILE, (third + 1) * TILE)
            far = slice(HALF + third * TILE, HALF + (third + 1) * TILE)
            for mat, grad in enumerate((q_ref, k_ref, v_ref)):
                mat_rows = slice(mat * model, (mat + 1) * model)
                both = jnp.concatenate([grad[:, near], grad[:, far]], axis=1)
                value = dotf(hid_t[...], both).astype(BF)
                gq[mat_rows, near] = value[:, :TILE]
                gq[mat_rows, far] = value[:, TILE:]

        plan = {
            0: (lambda: red_0(11), lambda: red_2(9)),
            1: (lambda: red_1(10),),
            2: (lambda: red_0(4), lambda: red_2(5)),
            3: (lambda: project(0), lambda: red_s(0, gq), lambda: red_1(11), lambda: red_0(3)),
            4: (lambda: red_2(10),),
            5: (lambda: red_1(4), lambda: red_0(0, gq)),
            6: (lambda: red_2(11), lambda: red_1(3)),
            7: (lambda: project(1), lambda: red_s(1, gq), lambda: red_2(4)),
            8: (lambda: red_3(2), lambda: red_1(0, gq)),
            9: (lambda: red_0(1, gq), lambda: red_2(3)),
            11: (lambda: project(2), lambda: red_s(2, gq), lambda: red_1(1, gq), lambda: red_2(0, gq)),
        }

        def back_step(step, _):
            attend_back(step)
            for at, todo in plan.items():
                @pl.when(step == at)
                def _():
                    for act in todo:
                        act()
            return 0

        lax.fori_loop(0, 12, back_step, 0)

        gacc[0] = jnp.zeros((8, model), F32)

        def gin_copy(i):
            rows = slice(i * tile, (i + 1) * tile)
            return pltpu.make_async_copy(rb_ref.at[rows], gin_hbm.at[rows], out_sem.at[i])

        def tail(i):
            rows = slice(i * tile, (i + 1) * tile)
            u = (
                dotf(q_ref[rows, :], weights[:model, :], NT)
                + dotf(k_ref[rows, :], weights[model : 2 * model, :], NT)
                + dotf(v_ref[rows, :], weights[2 * model : 3 * model, :], NT)
            )
            value = tokens[rows, :].astype(F32)
            inv_rms = lax.rsqrt(jnp.mean(value * value, axis=-1, keepdims=True) + EPS_NORM)
            gu = u * gains_ref[0:1, :]
            normal = value * inv_rms
            mean = jnp.mean(gu * normal, axis=-1, keepdims=True)
            rb_ref[rows, :] += inv_rms * (gu - normal * mean)
            gin_copy(i).start()
            gacc[0] += jnp.sum((u * normal).reshape(tile // 8, 8, model), axis=0)

        def unskew(g, _):
            accs = [
                jnp.concatenate([diag[g * 4 + h], jnp.zeros((128, 128), F32)], axis=1) for h in range(4)
            ]
            size = 64
            while size >= 1:
                accs = [acc[:size] + pltpu.roll(acc[size:], 1024 - size, 1) for acc in accs]
                size //= 2
            for h in range(4):
                drow[pl.ds(g * 4 + h, 1), :] = accs[h]
            return 0

        drow[...] = jnp.zeros_like(drow)
        lax.fori_loop(0, HEADS // 4, unskew, 0)
        onehot = (lax.broadcasted_iota(jnp.int32, (128, 1024), 0) == bucket_ref[...]).astype(F32)
        table = lax.dot_general(drow[...], onehot, NT, precision=HIGHEST, preferred_element_type=F32)
        small[0, :, :model] = jnp.zeros((16, model), F32)
        small[0, 1:2, :model] = jnp.sum(gacc[1], axis=0, keepdims=True)
        small[0, :, model:] = table
        red_0(2, gq)
        red_3(1)
        red_3_at(3)
        tail(0)
        red_2(1, gq)
        red_1(2, gq)
        tail(1)
        tail(2)
        red_2(2, gq)
        red_3_at(0)
        tail(3)
        small[0, 0:1, :model] = jnp.sum(gacc[0], axis=0, keepdims=True)
        sm_copy(0).start()
        red_3_at(1)
        sm_next(0)
        sm_copy(1).start()
        red_3_at(2)
        sm_next(1)
        sm_copy(2).start()
        for i in range(ntile):
            gin_copy(i).wait()
        red_sent(range(4))
        units_copy(3, z_send.at[0], z_recv.at[0, 0]).wait_send()

    def sm_copy(step):
        device = ((other, chip), (core, xnbr), (core, ynbr))[step]
        return remote(small.at[2 * step], small.at[2 * step + 1], sm_send.at[step], sm_recv.at[step], device)

    def sm_plane(off):
        return remote(
            small.at[6], small.at[7 + zpos], sm_send.at[2 + off], sm_recv.at[2 + off],
            (core, lax.rem(zpos + off, 4) * 4 + col),
        )

    def sm_next(step):
        sm_copy(step).wait_recv()
        small[2 * step + 2] = small[2 * step] + small[2 * step + 1]

    pl.run_scoped(
        backward,
        pltpu.VMEM((3 * model, model), BF),
        pltpu.VMEM((model, ntok), BF),
        pltpu.VMEM((HEADS, 128, 896), F32),
        pltpu.VMEM((16, 1024), F32),
        pltpu.VMEM((2, 2, LEN, LEN), BF),
        pltpu.VMEM((2, LEN, LEN), BF),
    )

    early = 6 * PAIR_ROWS

    def half_copy(part):
        at = (slice(0, early), slice(early, PACK_ROWS))[part]
        return remote(
            slot_ref.at[at, own_cols], slot_ref.at[at, own_cols], half_send.at[part], half_recv.at[part],
            (other, chip),
        )

    sm_next(2)
    for off in (1, 2, 3):
        sm_plane(off).start()
    small[7 + zpos] = small[6]
    for rnd in (2, 1):
        keep_copy(rnd).wait()
        pieces_copy(a2a_send.at[rnd], a2a_recv.at[rnd]).wait_recv()
    half_copy(1).start()
    keep_copy(0).wait()
    pieces_copy(a2a_send.at[0], a2a_recv.at[0]).wait_recv()
    half_copy(0).start()
    for off in (1, 2, 3):
        sm_plane(off).wait_recv()
    small_ref[...] = small[7] + small[8] + small[9] + small[10]
    for step in range(3):
        sm_copy(step).wait_send()
    for off in (1, 2, 3):
        sm_plane(off).wait_send()
    red_sent(range(4, 4 * ROUNDS))
    for rnd in range(ROUNDS):
        pieces_copy(a2a_send.at[rnd], a2a_recv.at[rnd]).wait_send()
        if rnd:
            units_copy(3, z_send.at[rnd], z_recv.at[rnd, 0]).wait_send()
    half_copy(1).wait()
    half_copy(0).wait()


def layer_pass(owners, gains, table, buckets, sizes, lens, master, tokens, cot):
    ntok, model = tokens.shape
    rows = 8 * master.shape[0]
    dma = pltpu.SemaphoreType.DMA
    half = RANGE_ROWS // 2
    pairs = 4 * ROUNDS
    act = pltpu.VMEM((ntok, model), BF)
    return pl.pallas_call(
        layer_kernel,
        name="layer_pass",
        out_shape=(
            jax.ShapeDtypeStruct((ntok, model), BF),
            jax.ShapeDtypeStruct((ntok, model), F32),
            jax.ShapeDtypeStruct((2 * HEADS, LEN, LEN), BF),
            jax.ShapeDtypeStruct((PACK_ROWS, model), BF),
            jax.ShapeDtypeStruct((16, model + 128), F32),
            jax.ShapeDtypeStruct((8, PACK_ROWS), jnp.int32),
            jax.ShapeDtypeStruct((7 * RANGE_ROWS, TILE), BF),
        ),
        in_specs=[VM] * 5 + [SM] + [ANY] * 3,
        out_specs=(ANY, ANY, ANY, ANY, VM, VM, ANY),
        scratch_shapes=[
            pltpu.VMEM((rows, model), BF),
            pltpu.VMEM((rows, HALF), BF),
            pltpu.VMEM((pairs, RANGE_ROWS, TILE), BF),
            pltpu.VMEM((pairs, RANGE_ROWS, TILE), BF),
            pltpu.VMEM((pairs, half, TILE), BF),
            pltpu.VMEM((pairs, half, TILE), BF),
            pltpu.VMEM((ROUNDS, 4, RANGE_ROWS, TILE), BF),
            pltpu.VMEM((ROUNDS, RANGE_ROWS, TILE), BF),
            pltpu.VMEM((3, PACK_ROWS, TILE), BF),
            pltpu.VMEM((ROUNDS, PACK_ROWS, TILE), BF),
            act, act, act, act, act, act, act,
            pltpu.VMEM((ntok, model), F32),
            pltpu.VMEM((11, 16, model + 128), F32),
            pltpu.VMEM((2, 8, model), F32),
            pltpu.VMEM((ROUNDS, RANGE_ROWS), jnp.int32),
            pltpu.VMEM((16, 1024), F32),
            pltpu.VMEM((1, 1024), jnp.int32),
            pltpu.VMEM((8, model), F32),
            pltpu.VMEM((16, 128), F32),
            dma((3,)), dma((4,)), dma((2, 2)),
            dma((ROUNDS,)), dma((ROUNDS,)), dma((ROUNDS,)), dma((ROUNDS, 4)), dma((pairs,)),
            dma((pairs,)), dma((pairs,)), dma((pairs,)), dma((pairs,)), dma((pairs,)),
            dma((pairs,)), dma((pairs,)), dma((pairs,)), dma((pairs,)), dma((pairs,)), dma((pairs,)),
            dma((ROUNDS,)), dma((ROUNDS, 4)), dma((ROUNDS,)), dma((ROUNDS,)), dma((2,)), dma((2,)),
            dma((6,)), dma((6,)),
        ],
        compiler_params=pltpu.CompilerParams(
            collective_id=0, has_side_effects=True, vmem_limit_bytes=62 * 2**20
        ),
    )(owners, gains, table, buckets, sizes, lens, master, tokens, cot)


BETA_ONE = 0.5
BETA_TWO = 0.75
LEARN_RATE = 0.06
SMALL_RATE = 0.4
WEIGHT_DECAY = 0.01
EPS_ADAM = 1e-08
OPT_STEP = 3


def adamw(weight, gradient, first_in, second, rate):
    first_out = BETA_ONE * first_in + (1.0 - BETA_ONE) * gradient
    second_out = BETA_TWO * second + (1.0 - BETA_TWO) * gradient * gradient
    fix_first = 1.0 - BETA_ONE**OPT_STEP
    fix_second = 1.0 - BETA_TWO**OPT_STEP
    update = first_out / fix_first / (jnp.sqrt(second_out / fix_second) + EPS_ADAM)
    return (first_out, second_out, weight - rate * (update + WEIGHT_DECAY * weight))


def adam_kernel(
    idx_ref, packed_ref, small_ref, gains_ref, gains_first_ref, gains_second_ref,
    table_ref, table_first_ref, table_second_ref, master_ref, first_ref, second_ref, out_ref, gin_ref,
    grad_ref, fnew_ref, snew_ref, mnew_ref, copy_ref, out_new_ref, gin_new_ref,
    ggrad_ref, gfnew_ref, gsnew_ref, gnew_ref, tgrad_ref, tfnew_ref, tsnew_ref, tnew_ref,
):
    rows, model = master_ref.shape
    onehot = (
        lax.broadcasted_iota(jnp.int32, (rows, PACK_ROWS), 0) + pl.program_id(0) * rows == idx_ref[:1, :]
    ).astype(F32).astype(BF)
    grad = dotf(onehot, packed_ref[...])
    first_new, second_new, master_new = adamw(
        master_ref[...], grad, first_ref[...], second_ref[...], LEARN_RATE
    )
    grad_ref[...] = grad
    fnew_ref[...] = first_new
    snew_ref[...] = second_new
    mnew_ref[...] = master_new
    copy_ref[...] = master_new.astype(BF)
    out_new_ref[...] = out_ref[...]
    gin_new_ref[...] = gin_ref[...]

    @pl.when(pl.program_id(0) == 0)
    def _():
        heads, buckets = table_ref.shape
        grad = small_ref[:2, :model]
        ggrad_ref[...] = grad
        gfnew_ref[...], gsnew_ref[...], gnew_ref[...] = adamw(
            gains_ref[...], grad, gains_first_ref[...], gains_second_ref[...], SMALL_RATE
        )
        grad = small_ref[:heads, model : model + buckets]
        tgrad_ref[...] = grad
        tfnew_ref[...], tsnew_ref[...], tnew_ref[...] = adamw(
            table_ref[...], grad, table_first_ref[...], table_second_ref[...], SMALL_RATE
        )


ADAM_STEPS = 2


def adam_pass(whole, master, first, second, out, gin):
    rows, model = master.shape
    ntok = out.shape[0]

    def part(total):
        return pl.BlockSpec((total // ADAM_STEPS, model), lambda i: (i, 0))

    def full(a):
        return pl.BlockSpec(a.shape, lambda i: (0, 0))

    def like(a):
        return jax.ShapeDtypeStruct(a.shape, a.dtype)

    wide = like(master)
    gains, table = whole[3], whole[6]
    return pl.pallas_call(
        adam_kernel,
        name="adam_pass",
        grid=(ADAM_STEPS,),
        out_shape=(wide, wide, wide, wide, jax.ShapeDtypeStruct((rows, model), BF), like(out), like(gin))
        + (like(gains),) * 4 + (like(table),) * 4,
        in_specs=[full(a) for a in whole] + [part(rows)] * 3 + [part(ntok)] * 2,
        out_specs=(part(rows),) * 5 + (part(ntok),) * 2 + (full(gains),) * 4 + (full(table),) * 4,
        compiler_params=pltpu.CompilerParams(vmem_limit_bytes=60 * 2**20),
    )(*whole, master, first, second, out, gin)


def fast_body(
    tokens, cotangent, master_slots, first_slots, second_slots, norm_gains, gains_first, gains_second,
    bias_table, table_first, table_second, bucket_ids, valid_len, task_sizes, owner_list,
):
    block_out, grad_input, _, packed, small, index, _ = layer_pass(
        owner_list[None, :], norm_gains, bias_table.T, bucket_ids[None, :], task_sizes[None, :], valid_len,
        master_slots, tokens, cotangent,
    )
    whole = (
        index, packed, small, norm_gains, gains_first, gains_second, bias_table.T, table_first.T, table_second.T
    )
    (
        grad_slots, first_new, second_new, master_new, master_copy, block_out, grad_input,
        grad_gains, gains_first_new, gains_second_new, gains_new,
        grad_table, table_first_new, table_second_new, table_new,
    ) = adam_pass(whole, master_slots, first_slots, second_slots, block_out, grad_input)
    return (
        block_out, grad_input, grad_slots, grad_gains, grad_table.T, first_new, second_new, master_new, master_copy,
        gains_first_new, gains_second_new, gains_new, table_first_new.T, table_second_new.T, table_new.T,
    )


def product(left_side, right_side):
    return jnp.dot(left_side, right_side, preferred_element_type=jnp.float32)


def contract_rows(left_side, right_side):
    return lax.dot_general(
        left_side, right_side, (((0,), (0,)), ((), ())), preferred_element_type=jnp.float32
    )


def contract_cols(left_side, right_side):
    return lax.dot_general(
        left_side, right_side, (((1,), (1,)), ((), ())), preferred_element_type=jnp.float32
    )


def smooth_act(values):
    return jax.nn.gelu(values, approximate=True)


def slot_layout(owner_list, devices, capacity):
    block_count = owner_list.shape[0]
    onehot = (owner_list[:, None] == jnp.arange(devices, dtype=jnp.int32)[None, :]).astype(
        jnp.int32
    )
    rank_in = jnp.sum((jnp.cumsum(onehot, axis=0) - onehot) * onehot, axis=1)
    slot_of = owner_list * capacity + rank_in
    source = (
        jnp.zeros((devices * capacity,), jnp.int32)
        .at[slot_of]
        .set(jnp.arange(block_count, dtype=jnp.int32))
    )
    filled = (
        jnp.zeros((devices * capacity,), jnp.int32)
        .at[slot_of]
        .set(jnp.ones((block_count,), jnp.int32))
    )
    return (slot_of, source, filled, rank_in)


def split_rows(all_rows):
    model_width = all_rows.shape[1]
    hidden = (all_rows.shape[0] - 4 * model_width) // 2
    return (
        all_rows[:model_width],
        all_rows[model_width : 2 * model_width],
        all_rows[2 * model_width : 3 * model_width],
        all_rows[3 * model_width : 4 * model_width],
        all_rows[4 * model_width : 4 * model_width + hidden],
        all_rows[4 * model_width + hidden :],
    )


def norm_raw(values, gain_row):
    inv_rms = lax.rsqrt(jnp.mean(values * values, axis=-1, keepdims=True) + EPS_NORM)
    return values * inv_rms * gain_row


def expand_bias(bias_table, bucket_ids):
    length = (bucket_ids.shape[0] + 1) // 2
    onehot = jax.nn.one_hot(bucket_ids, bias_table.shape[0], dtype=jnp.float32)
    rel_rows = jnp.dot(onehot, bias_table, precision=HIGHEST)
    reverse = rel_rows[::-1].T
    tiled_rows = jnp.tile(reverse, (1, length + 1))[:, : 2 * length * length]
    return tiled_rows.reshape(reverse.shape[0], length, 2 * length)[:, :, :length][:, :, ::-1]


def masked_scores(seq_query, seq_key, rel_bias, length):
    scores = (
        jnp.einsum("qhd,khd->hqk", seq_query, seq_key, preferred_element_type=jnp.float32)
        + rel_bias
    )
    live = jnp.arange(seq_key.shape[0], dtype=jnp.int32)[None, None, :] < length
    return jnp.where(live, scores, NEG_FILL)


def adamw_step(weight, gradient, first_in, second, step_value, rate):
    first_out = BETA_ONE * first_in + (1.0 - BETA_ONE) * gradient
    second_out = BETA_TWO * second + (1.0 - BETA_TWO) * gradient * gradient
    fix_first = 1.0 - jnp.power(jnp.float32(BETA_ONE), step_value)
    fix_second = 1.0 - jnp.power(jnp.float32(BETA_TWO), step_value)
    update = first_out / fix_first / (jnp.sqrt(second_out / fix_second) + EPS_ADAM)
    return (first_out, second_out, weight - rate * (update + WEIGHT_DECAY * weight))


def plain_body(
    tokens,
    cotangent,
    master_slots,
    first_slots,
    second_slots,
    norm_gains,
    gains_first,
    gains_second,
    bias_table,
    table_first,
    table_second,
    bucket_ids,
    valid_len,
    task_sizes,
    owner_list,
):
    devices = lax.axis_size("fsdp")
    replicas = lax.axis_size("dp")
    my_index = lax.axis_index("fsdp")
    capacity = master_slots.shape[0] // BROWS
    model_width = master_slots.shape[1]
    seq_dev = valid_len.shape[0]
    slot_of, source, filled, rank_in = slot_layout(owner_list, devices, capacity)
    sent_shard = master_slots.astype(jnp.bfloat16)

    def rebuild(gathered):
        blocks = gathered.reshape(devices * capacity, BROWS, model_width)[slot_of]
        return split_rows(blocks.reshape(-1, model_width))

    def by_seq(array_in):
        return array_in.reshape(seq_dev, LEN, HEADS, HEAD_DIM)

    def to_rows(array_in):
        return array_in.reshape(-1, model_width).astype(jnp.bfloat16)

    w_query, w_key, w_value, w_out, w_in, w_down = rebuild(
        lax.all_gather(sent_shard, "fsdp", axis=0, tiled=True)
    )
    rel_bias, bias_pull = jax.vjp(lambda table_in: expand_bias(table_in, bucket_ids), bias_table)
    inputs = tokens.astype(jnp.float32)
    hidden_one, norm_one_pull = jax.vjp(norm_raw, inputs, norm_gains[0])
    hidden_one = hidden_one.astype(jnp.bfloat16)
    queries = product(hidden_one, w_query).astype(jnp.bfloat16)
    keys_in = product(hidden_one, w_key).astype(jnp.bfloat16)
    values_in = product(hidden_one, w_value).astype(jnp.bfloat16)

    def attend_one(packed):
        seq_query, seq_key, seq_value, length = packed
        scores = masked_scores(seq_query, seq_key, rel_bias, length)
        row_max = jnp.max(scores, axis=-1, keepdims=True)
        exp_scores = jnp.exp(scores - row_max)
        totals = jnp.sum(exp_scores, axis=-1, keepdims=True)
        attn_probs = (exp_scores / totals).astype(jnp.bfloat16)
        context = jnp.einsum(
            "hqk,khd->qhd", attn_probs, seq_value, preferred_element_type=jnp.float32
        )
        return (context, row_max + jnp.log(totals))

    context, log_sums = lax.map(
        attend_one, (by_seq(queries), by_seq(keys_in), by_seq(values_in), valid_len)
    )
    context = to_rows(context)
    resid = inputs + product(context, w_out)
    hidden_two, norm_two_pull = jax.vjp(norm_raw, resid, norm_gains[1])
    hidden_two = hidden_two.astype(jnp.bfloat16)
    pre_act = contract_cols(hidden_two, w_in)
    active_full, act_pull = jax.vjp(smooth_act, pre_act)
    active = active_full.astype(jnp.bfloat16)
    block_out = (resid + product(active, w_down)).astype(jnp.bfloat16)
    first_seq = (lax.axis_index("dp") * devices + my_index) * seq_dev
    seq_ids = first_seq + jnp.arange(seq_dev, dtype=jnp.int32)
    task_ends = jnp.cumsum(task_sizes)
    task_count = task_sizes.shape[0]
    task_of = jnp.sum((task_ends[None, :] <= seq_ids[:, None]).astype(jnp.int32), axis=1)
    size_of = jnp.sum(
        jnp.where(
            task_of[:, None] == jnp.arange(task_count, dtype=jnp.int32)[None, :],
            task_sizes[None, :],
            0,
        ),
        axis=1,
    )
    seq_weight = jnp.float32(seq_dev * replicas * devices) / (
        jnp.float32(task_count) * size_of.astype(jnp.float32)
    )
    back_out = (
        cotangent.astype(jnp.float32).reshape(seq_dev, LEN, model_width) * seq_weight[:, None, None]
    ).reshape(-1, model_width)
    w_query, w_key, w_value, w_out, w_in, w_down = rebuild(
        lax.all_gather(sent_shard, "fsdp", axis=0, tiled=True)
    )
    down_back = back_out.astype(jnp.bfloat16)
    grad_down = contract_rows(active, down_back)
    act_back = contract_cols(down_back, w_down)
    (pre_full,) = act_pull(act_back)
    pre_back = pre_full.astype(jnp.bfloat16)
    grad_in = contract_rows(pre_back, hidden_two)
    resid_part, gain_two = norm_two_pull(product(pre_back, w_in))
    resid_back = back_out + resid_part
    out_back = resid_back.astype(jnp.bfloat16)
    grad_out = contract_rows(context, out_back)
    context_back = contract_cols(out_back, w_out).astype(jnp.bfloat16)

    def attend_back(score_sum, packed):
        seq_query, seq_key, seq_value, seq_back, length, log_sum = packed
        scores = masked_scores(seq_query, seq_key, rel_bias, length)
        attn_probs = jnp.exp(scores - log_sum)
        value_grad = jnp.einsum(
            "hqk,qhd->khd",
            attn_probs.astype(jnp.bfloat16),
            seq_back,
            preferred_element_type=jnp.float32,
        )
        prob_grad = jnp.einsum(
            "qhd,khd->hqk", seq_back, seq_value, preferred_element_type=jnp.float32
        )
        score_back = (
            attn_probs * (prob_grad - jnp.sum(attn_probs * prob_grad, axis=-1, keepdims=True))
        ).astype(jnp.bfloat16)
        query_grad = jnp.einsum(
            "hqk,khd->qhd", score_back, seq_key, preferred_element_type=jnp.float32
        )
        key_grad = jnp.einsum(
            "hqk,qhd->khd", score_back, seq_query, preferred_element_type=jnp.float32
        )
        return (score_sum + score_back.astype(jnp.float32), (query_grad, key_grad, value_grad))

    score_sum, (query_grad, key_grad, value_grad) = lax.scan(
        attend_back,
        jnp.zeros_like(rel_bias),
        (
            by_seq(queries),
            by_seq(keys_in),
            by_seq(values_in),
            by_seq(context_back),
            valid_len,
            log_sums,
        ),
    )
    query_back = to_rows(query_grad)
    key_back = to_rows(key_grad)
    value_back = to_rows(value_grad)
    grad_query = contract_rows(hidden_one, query_back)
    grad_key = contract_rows(hidden_one, key_back)
    grad_value = contract_rows(hidden_one, value_back)
    hidden_back = (
        contract_cols(query_back, w_query)
        + contract_cols(key_back, w_key)
        + contract_cols(value_back, w_value)
    )
    input_part, gain_one = norm_one_pull(hidden_back)
    grad_input = resid_back + input_part
    (table_grad,) = bias_pull(score_sum)
    grad_rows = jnp.concatenate(
        [grad_query, grad_key, grad_value, grad_out, grad_in, grad_down], axis=0
    )
    slotted = jnp.where(
        filled[:, None, None] > 0, grad_rows.reshape(-1, BROWS, model_width)[source], 0.0
    ).reshape(-1, model_width)
    owned_grads = lax.psum_scatter(slotted, "fsdp", scatter_dimension=0, tiled=True)
    grad_slots = lax.psum(owned_grads, "dp")
    grad_gains, grad_table = lax.psum((jnp.stack([gain_one, gain_two]), table_grad), ("dp", "fsdp"))
    step_value = jnp.float32(OPT_STEP)
    first_new, second_new, master_new = adamw_step(
        master_slots, grad_slots, first_slots, second_slots, step_value, LEARN_RATE
    )
    gains_first_new, gains_second_new, gains_new = adamw_step(
        norm_gains, grad_gains, gains_first, gains_second, step_value, SMALL_RATE
    )
    table_first_new, table_second_new, table_new = adamw_step(
        bias_table, grad_table, table_first, table_second, step_value, SMALL_RATE
    )
    return (
        block_out,
        grad_input,
        grad_slots,
        grad_gains,
        grad_table,
        first_new,
        second_new,
        master_new,
        master_new.astype(jnp.bfloat16),
        gains_first_new,
        gains_second_new,
        gains_new,
        table_first_new,
        table_second_new,
        table_new,
    )


def solution(mesh):
    in_specs = (
        P(("dp", "fsdp"), None),
        P(("dp", "fsdp"), None),
        P("fsdp", None),
        P("fsdp", None),
        P("fsdp", None),
        P(),
        P(),
        P(),
        P(),
        P(),
        P(),
        P(),
        P(("dp", "fsdp")),
        P(),
        P(),
    )
    out_specs = (
        P(("dp", "fsdp"), None),
        P(("dp", "fsdp"), None),
        P("fsdp", None),
        P(),
        P(),
        P("fsdp", None),
        P("fsdp", None),
        P("fsdp", None),
        P("fsdp", None),
        P(),
        P(),
        P(),
        P(),
        P(),
        P(),
    )
    fast = dict(mesh.shape) == {"dp": 2, "fsdp": CHIPS}
    body = fast_body if fast else plain_body
    return jax.shard_map(
        body, mesh=mesh, in_specs=in_specs, out_specs=out_specs, check_vma=False)
```

```python
import functools
import jax
import jax.numpy as jnp
from jax import lax
from jax.experimental import pallas as pl
from jax.experimental.pallas import tpu as pltpu
from jax.sharding import PartitionSpec as P

HEADS = 12
HEAD_DIM = 64
LEN = 512
BROWS = 8
EPS_NORM = 1e-06
NEG_FILL = -1e30
HIGHEST = lax.Precision.HIGHEST
MESH = pl.DeviceIdType.MESH
BF = jnp.bfloat16
F32 = jnp.float32

CHIPS = 16
RANGE_BLOCKS = 72
RANGE_ROWS = 576
PAIR_ROWS = 80
PACK_ROWS = CHIPS * PAIR_ROWS
ROUNDS = 3
TILE = 128
HALF = 3 * TILE
FF_CHUNK = 512
GELU_A = 0.7978845608028654
GELU_B = 0.044715 * GELU_A
NN = (((1,), (0,)), ((), ()))
NT = (((1,), (1,)), ((), ()))
TN = (((0,), (0,)), ((), ()))
VM = pl.BlockSpec(memory_space=pltpu.VMEM)
SM = pl.BlockSpec(memory_space=pltpu.SMEM)
ANY = pl.BlockSpec(memory_space=pl.ANY)


def dotf(a, b, dims=NN):
    return lax.dot_general(a, b, dims, preferred_element_type=F32)


def unit_place(v):
    first = 1 - (v + 36) // 48
    last = (v + 30) // 48
    i = last * (v // 3 - 6)
    late, turn = i // 5, i % 5
    rng = (
        first * (v % 4)
        + (1 - first - last) * (v // 3)
        + last * (10 + 3 * late + turn // 2 - turn % 2 * (4 + late))
    )
    return rng, first * (v // 4) + (1 - first) * (v % 3)


def unit_slice(v, core):
    rng, til = unit_place(v)
    return (
        pl.ds(pl.multiple_of(rng * RANGE_ROWS, 64), RANGE_ROWS),
        pl.ds(pl.multiple_of(core * HALF + til * TILE, TILE), TILE),
    )


def half_slice(v, core, half):
    rng, til = unit_place(v)
    return (
        pl.ds(pl.multiple_of(rng * RANGE_ROWS + half * (RANGE_ROWS // 2), 32), RANGE_ROWS // 2),
        pl.ds(pl.multiple_of(core * HALF + til * TILE, TILE), TILE),
    )


def piece_rows(i):
    return pl.ds(pl.multiple_of(i * PAIR_ROWS, 16), PAIR_ROWS)


def place():
    core = lax.axis_index("dp")
    chip = lax.axis_index("fsdp")
    xpos = chip % 2
    ypos = (chip // 2) % 2
    zpos = chip // 4
    return core, chip, xpos, ypos, zpos, chip + 1 - 2 * xpos, chip + 2 - 4 * ypos


def remote(src, dst, ssem, rsem, device):
    return pltpu.make_async_remote_copy(
        src_ref=src, dst_ref=dst, send_sem=ssem, recv_sem=rsem, device_id=device, device_id_type=MESH
    )


def as_column(row):
    return jnp.broadcast_to(row, (8, row.shape[1])).astype(F32).T[:, :1].astype(jnp.int32)


def gelu_pair(v):
    sq = v * v
    half = 0.5 + 0.5 * jnp.tanh(v * (GELU_A + GELU_B * sq))
    act = v * half
    return act, half + act * (1.0 - half) * (2.0 * GELU_A + 6.0 * GELU_B * sq)


def layer_kernel(
    owner_ref, gains_ref, table_ref, buckets_ref, sizes_ref, len_ref,
    master_hbm, tokens_hbm, cot_hbm,
    out_hbm, gin_hbm, p_hbm, slot_ref, small_ref, index_ref, spare,
    weights, sib, xin, yin, dain, dbin, zin, ubuf, sendbuf, recvbuf,
    q_ref, k_ref, v_ref, ctx_ref, tokens, hidden, cb_ref, rb_ref, small, gacc,
    idx_row_ref, rel_ref, bucket_ref, weight_ref, pad,
    load_sem, out_sem, p_sem,
    fa_send, fa_recv, fz_send, fz_recv, f_send, fx_recv, fy_recv, fda_recv, fdb_recv, fs_recv,
    r_send, h_recv, da_recv, db_recv, x_recv, y_recv, z_send, z_recv, a2a_send, a2a_recv, half_send, half_recv,
    sm_send, sm_recv,
):
    core, chip, xpos, ypos, zpos, xnbr, ynbr = place()
    other = 1 - core
    ntok, model = tokens.shape
    hid = (weights.shape[0] - 4 * model) // 2
    nchunk = hid // FF_CHUNK
    first_in, first_down = 4 * model, 4 * model + hid
    col = ypos * 2 + xpos
    xcol = ypos * 2 + (1 - xpos)
    ycol = (1 - ypos) * 2 + xpos
    dcol = (1 - ypos) * 2 + (1 - xpos)
    own_cols = pl.ds(pl.multiple_of(core * HALF, TILE), HALF)
    tile = 256
    ntile = ntok // tile

    def units_copy(count, send_sem, recv_sem):
        at = spare.at[pl.ds(0, count * RANGE_ROWS)]
        return remote(at, at, send_sem, recv_sem, (other, chip))

    def pieces_copy(send_sem, recv_sem):
        at = recvbuf.at[0, pl.ds(0, (CHIPS - 1) * PAIR_ROWS)]
        return remote(at, at, send_sem, recv_sem, (other, chip))

    load_tokens = pltpu.make_async_copy(tokens_hbm, tokens, load_sem.at[0])
    load_tokens.start()

    barrier = pltpu.get_barrier_semaphore()
    for step in range(1, CHIPS):
        pl.semaphore_signal(
            barrier, inc=1, device_id=(core, lax.rem(chip + step, CHIPS)), device_id_type=MESH
        )
    pl.semaphore_signal(barrier, inc=1, device_id=(other, chip), device_id_type=MESH)

    def lanes(rows, width):
        return lax.broadcasted_iota(jnp.int32, (rows, width), 1)

    def steps(rows, width):
        return lax.broadcasted_iota(jnp.int32, (rows, width), 0)

    def mark(mask):
        return mask.astype(F32).astype(BF)

    def eight(row):
        return jnp.broadcast_to(row, (8, row.shape[1]))

    owners = owner_ref[...]
    nblock = owners.shape[1]

    def pack_index():
        mine = mark(eight(owners == chip))
        block, low = steps(nblock, 128), lanes(nblock, 128) * RANGE_BLOCKS
        count = dotf(mine, mark(jnp.logical_and(block >= low, block < low + RANGE_BLOCKS)))
        start = dotf(mine, mark(block < low))
        row, low = lanes(128, PACK_ROWS), steps(128, PACK_ROWS) * PAIR_ROWS
        spread = mark(jnp.logical_and(row >= low, row < low + PAIR_ROWS))
        count = dotf(count.astype(BF), spread)
        start = dotf(start.astype(BF), spread)
        rng = dotf(lanes(8, 128).astype(F32).astype(BF), spread)
        inner = lanes(8, PACK_ROWS).astype(F32) - PAIR_ROWS * rng
        turn = jnp.floor(inner * (1.0 / BROWS))
        index = jnp.where(turn < count, start * BROWS + inner, -1.0)
        index_ref[...] = index.astype(jnp.int32)

    def unit_index():
        row, low = lanes(128, RANGE_ROWS), steps(128, RANGE_ROWS) * BROWS
        spread = mark(jnp.logical_and(row >= low, row < low + BROWS))
        inner = lanes(8, RANGE_ROWS).astype(F32) - BROWS * dotf(lanes(8, 128).astype(F32).astype(BF), spread)
        values = eight(owners).astype(F32).astype(BF)
        for rnd in range(ROUNDS):
            rng, _ = unit_place(rnd * CHIPS + chip)
            at = lanes(nblock, 128)
            pick = jnp.logical_and(steps(nblock, 128) == at + rng * RANGE_BLOCKS, at < RANGE_BLOCKS)
            owner = dotf(values, mark(pick))
            same = jnp.logical_and(owner.T[:, :1] == owner[:1], steps(128, 128) < lanes(128, 128))
            rank = jnp.sum(same.astype(F32), axis=0, keepdims=True)
            index = (
                PAIR_ROWS * dotf(owner.astype(BF), spread)
                + BROWS * dotf(eight(rank).astype(BF), spread)
                + inner
            )
            idx_row_ref[rnd : rnd + 1, :] = index[:1].astype(jnp.int32)

    def relative():
        count = buckets_ref.shape[1]
        pad[...] = jnp.full((16, 128), 127.0, F32)
        for i in range(8):
            width = min(128, count - 128 * i)
            pad[i : i + 1, :width] = buckets_ref[:, 128 * i : 128 * i + width].astype(F32)
        turned = dotf(pad[:8].astype(BF), mark(steps(128, 128) + lanes(128, 128) == 127))
        for i in range(8):
            source = 6 - i if i < 7 else 7
            bucket_ref[:, 128 * i : 128 * (i + 1)] = turned[source : source + 1].astype(jnp.int32)
        pad[...] = jnp.zeros((16, 128), F32)
        pad[: table_ref.shape[0], : table_ref.shape[1]] = table_ref[...]
        rel_ref[...] = lax.dot_general(
            pad[...], (steps(128, 1024) == bucket_ref[...]).astype(F32), NN,
            precision=HIGHEST, preferred_element_type=F32,
        )

    def sequence_weights():
        count = sizes_ref.shape[1]
        seqs = ntok // LEN
        pad[...] = jnp.zeros((16, 128), F32)
        pad[:1, :count] = sizes_ref[...].astype(F32)
        sizes = pad[:8]
        ends = dotf(sizes.astype(BF), mark(steps(128, 128) <= lanes(128, 128)))
        for i in range(seqs):
            seq = ((core * CHIPS + chip) * seqs + i).astype(F32)
            inside = jnp.logical_and(ends - sizes <= seq, seq < ends)
            size = jnp.sum(jnp.where(inside, sizes, 0.0)[:1], axis=1, keepdims=True)
            weight = jnp.float32(seqs * 2 * CHIPS) / (jnp.float32(count) * size)
            weight_ref[i : i + 1, :] = jnp.broadcast_to(weight, (1, model))

    def pack(mbuf):
        load = pltpu.make_async_copy(master_hbm.at[:, own_cols], mbuf, load_sem.at[1])
        load.start()
        pack_index()
        load.wait()
        own_half = mbuf[...].astype(BF)
        index = as_column(index_ref[:1, :])
        for part in range(4):
            rows = PACK_ROWS // 4
            onehot = (
                lax.broadcasted_iota(jnp.int32, (rows, mbuf.shape[0]), 1)
                == index[part * rows : (part + 1) * rows, :]
            ).astype(F32).astype(BF)
            packed = dotf(onehot, own_half).astype(BF)
            for til in range(3):
                sendbuf[til, part * rows : (part + 1) * rows, :] = packed[:, til * TILE : (til + 1) * TILE]

    pl.run_scoped(pack, pltpu.VMEM((master_hbm.shape[0], HALF), F32))
    pl.semaphore_wait(barrier, CHIPS)

    def fa_copy(rnd, step):
        dest = lax.rem(chip + step, CHIPS)
        rng, til = unit_place(rnd * CHIPS + dest)
        return remote(
            sendbuf.at[til, piece_rows(rng), :], recvbuf.at[rnd, piece_rows(chip), :],
            fa_send.at[rnd], fa_recv.at[rnd], (core, dest),
        )

    def fa_start(rnd):
        for step in range(1, CHIPS):
            fa_copy(rnd, step).start()
        rng, til = unit_place(rnd * CHIPS + chip)
        recvbuf[rnd, piece_rows(chip), :] = sendbuf[til, piece_rows(rng), :]

    def own_unit(rnd):
        pieces_copy(fa_send.at[rnd], fa_recv.at[rnd]).wait_recv()
        v = rnd * CHIPS + chip
        index = as_column(idx_row_ref[rnd : rnd + 1, :])
        for part in range(2):
            rows = RANGE_ROWS // 2
            onehot = (
                lax.broadcasted_iota(jnp.int32, (rows, PACK_ROWS), 1)
                == index[part * rows : (part + 1) * rows, :]
            ).astype(F32).astype(BF)
            weights[half_slice(v, core, part)] = dotf(onehot, recvbuf[rnd]).astype(BF)

    def nearest(k):
        return (zpos, zpos + 1 - 2 * (zpos % 2), 2 - zpos // 2, 3 - 3 * (zpos // 2))[k]

    def behind(p):
        return nearest(p % 4) if p < 8 else p % 4

    def fwd_unit(p, column):
        return p // 4 * CHIPS + behind(p) * 4 + column

    def fz_copy(rnd, source, up):
        at = unit_slice(rnd * CHIPS + source * 4 + col, core)
        dest = chip + (4 if up else -4)
        return remote(weights.at[at], weights.at[at], fz_send.at[rnd], fz_recv.at[rnd, source], (core, dest))

    def fz_start(rnd):
        @pl.when(zpos < 3)
        def _():
            fz_copy(rnd, zpos, True).start()

        @pl.when(zpos > 0)
        def _():
            fz_copy(rnd, zpos, False).start()

    def fz_relay(rnd, k):
        source = nearest(k)
        units_copy(1, fz_send.at[rnd], fz_recv.at[rnd, source]).wait_recv()

        @pl.when(jnp.logical_and(source < zpos, zpos < 3))
        def _():
            fz_copy(rnd, source, True).start()

        @pl.when(jnp.logical_and(source > zpos, zpos > 0))
        def _():
            fz_copy(rnd, source, False).start()

    def fz_sent(rnd):
        inner = zpos % 3 > 0

        @pl.when(inner)
        def _():
            units_copy(5, fz_send.at[rnd], fz_recv.at[rnd, 0]).wait_send()

        @pl.when(jnp.logical_not(inner))
        def _():
            units_copy(1, fz_send.at[rnd], fz_recv.at[rnd, 0]).wait_send()

    def fx_copy(p):
        at = unit_slice(fwd_unit(p, col), core)
        return remote(weights.at[at], weights.at[at], f_send.at[p], fx_recv.at[p], (core, xnbr))

    def fy_copy(p):
        at = unit_slice(fwd_unit(p, col), core)
        return remote(weights.at[at], weights.at[at], f_send.at[p], fy_recv.at[p], (core, ynbr))

    def fda_copy(p):
        at = half_slice(fwd_unit(p, xcol), core, 0)
        return remote(weights.at[at], weights.at[at], f_send.at[p], fda_recv.at[p], (core, ynbr))

    def fdb_copy(p):
        at = half_slice(fwd_unit(p, ycol), core, 1)
        return remote(weights.at[at], weights.at[at], f_send.at[p], fdb_recv.at[p], (core, xnbr))

    def fs_copy(p, kind):
        at = unit_slice(fwd_unit(p, (col, xcol, ycol, dcol)[kind]), core)
        return remote(weights.at[at], weights.at[at], f_send.at[p], fs_recv.at[p], (other, chip))

    def fwd_a(p):
        if p < 8 and p % 4:
            fz_relay(p // 4, p % 4)
        fx_copy(p).start()
        fy_copy(p).start()
        fs_copy(p, 0).start()

    def fwd_b(p):
        fx_copy(p).wait_recv()
        fda_copy(p).start()
        fs_copy(p, 1).start()
        fy_copy(p).wait_recv()
        fdb_copy(p).start()
        fs_copy(p, 2).start()

    def fwd_c(p):
        fda_copy(p).wait_recv()
        fdb_copy(p).wait_recv()
        fs_copy(p, 3).start()

    def fwd_done(*pairs):
        for p in pairs:
            units_copy(4, f_send.at[p], fs_recv.at[p]).wait_recv()

    def fwd_sent(rounds, pairs):
        for rnd in rounds:
            pieces_copy(fa_send.at[rnd], fa_recv.at[rnd]).wait_send()
            fz_sent(rnd)
        for p in pairs:
            units_copy(7, f_send.at[p], fs_recv.at[p]).wait_send()

    lane_head = lax.broadcasted_iota(jnp.int32, (LEN, 128), 1) // HEAD_DIM

    def forward(base, s_scr, p_scr):
        fa_start(0)
        unit_index()
        relative()
        sequence_weights()
        load_tokens.wait()
        for part in range(ntok // 128):
            rows = slice(part * 128, (part + 1) * 128)
            values = tokens[rows, :].astype(F32)
            inv_rms = lax.rsqrt(jnp.mean(values * values, axis=-1, keepdims=True) + EPS_NORM)
            hidden[rows, :] = (values * inv_rms * gains_ref[0:1, :]).astype(BF)

        def bands(h, _):
            wide = jnp.broadcast_to(rel_ref[pl.ds(h, 1), :], (128, 1024))
            base[pl.ds(h, 1)] = pltpu.roll(wide, 0, 1, stride=1, stride_axis=0)[:, :896][None]
            return 0

        lax.fori_loop(0, HEADS, bands, 0)
        own_unit(0)
        fz_start(0)
        fwd_a(0)
        fwd_a(1)
        fwd_b(0)
        fwd_a(2)
        fa_start(1)
        fa_start(2)
        fwd_b(1)
        fwd_c(0)
        fwd_a(3)
        fwd_b(2)
        fwd_c(1)
        fwd_done(0, 1)

        def third_of(step):
            nearer = jnp.minimum(zpos, 2)
            middle = 1 - zpos % 2 * (1 - zpos // 2)
            turn = step // 4
            return jnp.where(turn == 0, nearer, jnp.where(turn == 1, middle, 3 - nearer - middle))

        def projections(step):
            third = third_of(step)
            near = pl.ds(pl.multiple_of(third * TILE, TILE), TILE)
            far = pl.ds(pl.multiple_of(HALF + third * TILE, TILE), TILE)
            for mat, out_ref in enumerate((q_ref, k_ref, v_ref)):
                mat_rows = slice(mat * model, (mat + 1) * model)
                both = jnp.concatenate([weights[mat_rows, near], weights[mat_rows, far]], axis=1)
                value = dotf(hidden[...], both).astype(BF)
                out_ref[:, near] = value[:, :TILE]
                out_ref[:, far] = value[:, TILE:]

        row_id = lax.broadcasted_iota(jnp.int32, (128, LEN), 0)

        def seq_pair(step):
            return step % 2, third_of(step) + 3 * (step // 2 % 2)

        def p_copy(step, head):
            seq, pair = seq_pair(step)
            return pltpu.make_async_copy(
                p_scr.at[step % 2, head], p_hbm.at[seq * HEADS + pair * 2 + head], p_sem.at[step % 2, head]
            )

        def attend(step):
            seq, pair = seq_pair(step)
            rows = pl.ds(pl.multiple_of(seq * LEN, LEN), LEN)
            lanes = pl.ds(pl.multiple_of(pair * 128, 128), 128)
            length = len_ref[seq]

            @pl.when(step >= 2)
            def _():
                for head in range(2):
                    p_copy(step - 2, head).wait()

            q_two = q_ref[rows, lanes]
            k_two = k_ref[rows, lanes]
            v_two = v_ref[rows, lanes].T
            outs = []
            for head in range(2):
                k_one = jnp.where(lane_head == head, k_two, jnp.zeros_like(k_two))
                top = jnp.full((8, LEN), NEG_FILL, F32)
                for blk in range(4):
                    score = dotf(k_one[blk * 128 : (blk + 1) * 128], q_two, NT)
                    score = score + base[pair * 2 + head, :, 384 - 128 * blk : 896 - 128 * blk]
                    score = jnp.where(row_id + blk * 128 < length, score, NEG_FILL)
                    s_scr[head, blk * 128 : (blk + 1) * 128, :] = score
                    top = jnp.maximum(top, jnp.max(score.reshape(16, 8, LEN), axis=0))
                top = jnp.max(top, axis=0, keepdims=True)
                total = jnp.zeros((8, LEN), F32)
                for blk in range(4):
                    part = jnp.exp(s_scr[head, blk * 128 : (blk + 1) * 128, :] - top)
                    s_scr[head, blk * 128 : (blk + 1) * 128, :] = part
                    total = total + jnp.sum(part.reshape(16, 8, LEN), axis=0)
                inverse = 1.0 / jnp.sum(total, axis=0, keepdims=True)
                for blk in range(4):
                    p_scr[step % 2, head, blk * 128 : (blk + 1) * 128, :] = (
                        s_scr[head, blk * 128 : (blk + 1) * 128, :] * inverse
                    ).astype(BF)
                outs.append(dotf(v_two[head * HEAD_DIM : (head + 1) * HEAD_DIM], p_scr[step % 2, head]))
                p_copy(step, head).start()
            ctx_ref[rows, lanes] = jnp.concatenate(outs, axis=0).T.astype(BF)

        plan = {
            0: (lambda: own_unit(1), lambda: fz_start(1), lambda: fwd_a(4), lambda: fwd_c(2)),
            1: (lambda: fwd_b(3),),
            3: (lambda: fwd_c(3), lambda: fwd_a(5), lambda: fwd_done(2)),
            4: (lambda: own_unit(2), lambda: fz_start(2), lambda: fwd_b(4)),
            5: (lambda: fwd_a(6),),
            6: (lambda: fwd_c(4), lambda: fwd_b(5)),
            7: (lambda: fwd_a(7), lambda: fwd_done(3)),
            8: (lambda: fz_relay(2, 1), lambda: fwd_c(5), lambda: fwd_b(6)),
            9: (lambda: fwd_b(7),),
            10: (lambda: fz_relay(2, 2), lambda: fwd_c(6)),
            11: (lambda: fz_relay(2, 3), lambda: fwd_a(8), lambda: fwd_c(7)),
        }

        def attend_step(step, _):
            @pl.when(step % 4 == 0)
            def _():
                projections(step)

            attend(step)
            for at, todo in plan.items():
                @pl.when(step == at)
                def _():
                    for act in todo:
                        act()
            return 0

        lax.fori_loop(0, 12, attend_step, 0)
        for step in (10, 11):
            for head in range(2):
                p_copy(step, head).wait()

    pl.run_scoped(
        forward,
        pltpu.VMEM((HEADS, 128, 896), F32),
        pltpu.VMEM((2, LEN, LEN), F32),
        pltpu.VMEM((2, 2, LEN, LEN), BF),
    )

    def src_of(p, gq):
        return gq if p < 3 else weights

    def unit(p, column):
        return p * 4 + column

    def sib_copy(p, column, gq=None):
        v = unit(p, column)
        return remote(
            src_of(p, gq).at[unit_slice(v, other)], sib.at[unit_slice(v, 0)],
            r_send.at[p], h_recv.at[p], (other, chip),
        )

    def da_copy(p, gq=None):
        at = half_slice(unit(p, dcol), core, 0)
        return remote(src_of(p, gq).at[at], dain.at[p], r_send.at[p], da_recv.at[p], (core, ynbr))

    def db_copy(p, gq=None):
        at = half_slice(unit(p, dcol), core, 1)
        return remote(src_of(p, gq).at[at], dbin.at[p], r_send.at[p], db_recv.at[p], (core, xnbr))

    def x_copy(p, gq=None):
        at = unit_slice(unit(p, xcol), core)
        return remote(src_of(p, gq).at[at], xin.at[p], r_send.at[p], x_recv.at[p], (core, xnbr))

    def y_copy(p, gq=None):
        at = unit_slice(unit(p, ycol), core)
        return remote(src_of(p, gq).at[at], yin.at[p], r_send.at[p], y_recv.at[p], (core, ynbr))

    def z_copy(p, gq=None):
        rnd, zt = p // 4, p % 4
        at = unit_slice(unit(p, col), core)
        return remote(
            src_of(p, gq).at[at], zin.at[rnd, zpos], z_send.at[rnd], z_recv.at[rnd, zpos], (core, zt * 4 + col)
        )

    def z_arrived(rnd, src):
        return remote(zin.at[rnd, src], zin.at[rnd, src], z_send.at[rnd], z_recv.at[rnd, src], (core, xnbr))

    def add(ref, at, incoming):
        ref[at] = (ref[at].astype(F32) + incoming.astype(F32)).astype(BF)

    def red_s(p, gq=None):
        for column in range(4):
            sib_copy(p, column, gq).start()

    def red_0(p, gq=None):
        units_copy(4, r_send.at[p], h_recv.at[p]).wait_recv()
        for column in range(4):
            add(src_of(p, gq), unit_slice(unit(p, column), core), sib[unit_slice(unit(p, column), 0)])
        da_copy(p, gq).start()
        db_copy(p, gq).start()

    def red_1(p, gq=None):
        da_copy(p, gq).wait_recv()
        add(src_of(p, gq), half_slice(unit(p, xcol), core, 0), dain[p])
        x_copy(p, gq).start()
        db_copy(p, gq).wait_recv()
        add(src_of(p, gq), half_slice(unit(p, ycol), core, 1), dbin[p])
        y_copy(p, gq).start()

    def red_2(p, gq=None):
        x_copy(p, gq).wait_recv()
        y_copy(p, gq).wait_recv()
        at = unit_slice(unit(p, col), core)
        total = (src_of(p, gq)[at].astype(F32) + xin[p].astype(F32) + yin[p].astype(F32)).astype(BF)

        @pl.when(zpos == p % 4)
        def _():
            ubuf[p // 4] = total

        @pl.when(zpos != p % 4)
        def _():
            src_of(p, gq)[at] = total
            z_copy(p, gq).start()

    def a2a_copy(rnd, step):
        dest = lax.rem(chip + step, CHIPS)
        rng, til = unit_place(rnd * CHIPS + chip)
        return remote(
            recvbuf.at[rnd, piece_rows(dest), :],
            slot_ref.at[piece_rows(rng), pl.ds(pl.multiple_of(core * HALF + til * TILE, TILE), TILE)],
            a2a_send.at[rnd], a2a_recv.at[rnd], (core, dest),
        )

    def keep_copy(rnd):
        rng, til = unit_place(rnd * CHIPS + chip)
        return pltpu.make_async_copy(
            recvbuf.at[rnd, piece_rows(chip), :],
            slot_ref.at[piece_rows(rng), pl.ds(pl.multiple_of(core * HALF + til * TILE, TILE), TILE)],
            load_sem.at[rnd],
        )

    def red_3(rnd):
        total = ubuf[rnd].astype(F32)
        for off in (1, 2, 3):
            src = lax.rem(zpos + off, 4)
            z_arrived(rnd, src).wait_recv()
            total = total + zin[rnd, src].astype(F32)
        total = total.astype(BF)
        for part in range(4):
            rows = PACK_ROWS // 4
            onehot = (
                lax.broadcasted_iota(jnp.int32, (rows, RANGE_ROWS), 0) + part * rows
                == idx_row_ref[rnd : rnd + 1, :]
            ).astype(F32).astype(BF)
            recvbuf[rnd, part * rows : (part + 1) * rows, :] = dotf(onehot, total).astype(BF)
        for step in range(1, CHIPS):
            a2a_copy(rnd, step).start()
        keep_copy(rnd).start()

    def red_sent(pairs):
        for p in pairs:
            units_copy(7, r_send.at[p], h_recv.at[p]).wait_send()

    def red_3_at(plane):
        @pl.when(zpos == plane)
        def _():
            red_3(0)

    def out_copy(i):
        rows = pl.ds(pl.multiple_of(i * tile, tile), tile)
        return pltpu.make_async_copy(hidden.at[rows], out_hbm.at[rows], out_sem.at[i])

    def feed(cot, down, out_acc, u_acc, act_s, pb_s):
        load_cot = pltpu.make_async_copy(cot_hbm, cot, load_sem.at[2])
        load_cot.start()
        load_cot.wait()
        fwd_a(9)
        fwd_done(4, 5, 6, 7)

        def head(i, _):
            rows = pl.ds(pl.multiple_of(i * tile, tile), tile)
            value = tokens[rows, :].astype(F32) + dotf(ctx_ref[rows, :], weights[3 * model : 4 * model, :])
            rb_ref[rows, :] = value
            inv_rms = lax.rsqrt(jnp.mean(value * value, axis=-1, keepdims=True) + EPS_NORM)
            hidden[rows, :] = (value * inv_rms * gains_ref[1:2, :]).astype(BF)
            down[rows, :] = (cot[rows, :].astype(F32) * weight_ref[pl.ds(i * tile // LEN, 1), :]).astype(BF)
            out_acc[rows, :] = jnp.zeros((tile, model), F32)
            u_acc[rows, :] = jnp.zeros((tile, model), F32)
            return 0

        lax.fori_loop(0, ntile, head, 0)
        fwd_a(10)
        fwd_b(8)

        middle = {
            0: (lambda: fwd_a(11), lambda: fwd_b(9), lambda: fwd_c(8), lambda: fwd_sent((0, 1), range(8))),
            1: (lambda: fwd_b(11), lambda: fwd_c(10), lambda: fwd_sent((2,), (8,))),
            2: (lambda: fwd_c(11),),
            3: (lambda: red_0(6), lambda: fwd_sent((), (9, 10))),
            4: (lambda: red_1(6), lambda: red_0(8), lambda: fwd_sent((), (11,))),
            5: (lambda: red_2(6), lambda: red_0(9), lambda: red_1(8)),
        }
        plan = {
            0: (lambda: fwd_done(8), lambda: fwd_b(10), lambda: fwd_c(9)),
            2: (lambda: red_s(6), lambda: red_s(7), lambda: fwd_done(9, 10)),
            3: (lambda: red_s(8), lambda: red_0(7), lambda: fwd_done(11)),
            4: (lambda: red_s(9), lambda: red_1(7)),
            5: (lambda: red_s(5), lambda: red_s(10), lambda: red_s(11), lambda: red_2(7)),
        }

        def run(what, now):
            for at, todo in what.items():
                @pl.when(now == at)
                def _():
                    for act in todo:
                        act()

        def chunk(c, _):
            rows_in = pl.ds(pl.multiple_of(first_in + c * FF_CHUNK, FF_CHUNK), FF_CHUNK)
            rows_down = pl.ds(pl.multiple_of(first_down + c * FF_CHUNK, FF_CHUNK), FF_CHUNK)
            for i in range(ntile):
                rows = slice(i * tile, (i + 1) * tile)
                pre = dotf(hidden[rows, :], weights[rows_in, :], NT)
                back = dotf(down[rows, :], weights[rows_down, :], NT)
                act, slope = gelu_pair(pre)
                act = act.astype(BF)
                pre_back = (back * slope).astype(BF)
                act_s[rows, :] = act
                pb_s[rows, :] = pre_back
                out_acc[rows, :] += dotf(act, weights[rows_down, :])
                u_acc[rows, :] += dotf(pre_back, weights[rows_in, :])
            run(middle, c)
            weights[rows_down, :] = dotf(act_s[...], down[...], TN).astype(BF)
            weights[rows_in, :] = dotf(pb_s[...], hidden[...], TN).astype(BF)
            run(plan, c)
            return 0

        lax.fori_loop(0, nchunk, chunk, 0)

        tail_plan = {
            0: (lambda: red_0(5),),
            1: (lambda: red_1(9),),
            2: (lambda: red_0(10),),
            3: (lambda: red_2(8),),
        }
        gacc[1] = jnp.zeros((8, model), F32)

        def tail(i, _):
            rows = pl.ds(pl.multiple_of(i * tile, tile), tile)
            value = rb_ref[rows, :]
            out = (value + out_acc[rows, :]).astype(BF)
            inv_rms = lax.rsqrt(jnp.mean(value * value, axis=-1, keepdims=True) + EPS_NORM)
            u = u_acc[rows, :]
            gu = u * gains_ref[1:2, :]
            normal = value * inv_rms
            mean = jnp.mean(gu * normal, axis=-1, keepdims=True)
            back = cot[rows, :].astype(F32) * weight_ref[pl.ds(i * tile // LEN, 1), :] + inv_rms * (gu - normal * mean)
            rb_ref[rows, :] = back
            low = back.astype(BF)
            down[rows, :] = low
            hidden[rows, :] = out
            out_copy(i).start()
            cb_ref[rows, :] = dotf(low, weights[3 * model : 4 * model, :], NT).astype(BF)
            gacc[1] += jnp.sum((u * normal).reshape(tile // 8, 8, model), axis=0)
            run(tail_plan, i)
            return 0

        lax.fori_loop(0, ntile, tail, 0)
        weights[3 * model : 4 * model, :] = dotf(ctx_ref[...], down[...], TN).astype(BF)
        red_s(4)
        red_s(3)
        red_1(5)
        for i in range(ntile):
            out_copy(i).wait()

    pl.run_scoped(
        feed,
        pltpu.VMEM((ntok, model), BF),
        pltpu.VMEM((ntok, model), BF),
        pltpu.VMEM((ntok, model), F32),
        pltpu.VMEM((ntok, model), F32),
        pltpu.VMEM((ntok, FF_CHUNK), BF),
        pltpu.VMEM((ntok, FF_CHUNK), BF),
    )

    def backward(gq, hid_t, diag, drow, p_scr, ds_scr):
        def split(step):
            turn = step // 2
            return step % 2, turn // 2 + 3 * (turn % 2)

        def p_copy(step, head):
            seq, pair = split(step)
            return pltpu.make_async_copy(
                p_hbm.at[seq * HEADS + pair * 2 + head], p_scr.at[step % 2, head], p_sem.at[step % 2, head]
            )

        for head in range(2):
            p_copy(0, head).start()
        diag[...] = jnp.zeros_like(diag)
        for part in range(ntok // 128):
            rows = slice(part * 128, (part + 1) * 128)
            values = tokens[rows, :].astype(F32)
            inv_rms = lax.rsqrt(jnp.mean(values * values, axis=-1, keepdims=True) + EPS_NORM)
            hid_t[:, rows] = (values * inv_rms * gains_ref[0:1, :]).astype(BF).T

        def attend_back(step):
            seq, pair = split(step)
            rows = pl.ds(pl.multiple_of(seq * LEN, LEN), LEN)
            lanes = pl.ds(pl.multiple_of(pair * 128, 128), 128)

            @pl.when(step + 1 < 12)
            def _():
                for head in range(2):
                    p_copy(step + 1, head).start()

            q_two, k_two, v_two, do_two = (
                q_ref[rows, lanes], k_ref[rows, lanes], v_ref[rows, lanes], cb_ref[rows, lanes]
            )
            k_turn = k_two.T
            inner = (do_two.astype(F32) * ctx_ref[rows, lanes].astype(F32)).T
            dv_parts, dk_parts, dq_parts = [], [], []
            for head in range(2):
                p_copy(step, head).wait()
                delta = jnp.sum(inner[head * HEAD_DIM : (head + 1) * HEAD_DIM], axis=0, keepdims=True)
                v_one = jnp.where(lane_head == head, v_two, jnp.zeros_like(v_two))
                for blk in range(4):
                    sub = slice(blk * 128, (blk + 1) * 128)
                    prob_back = dotf(v_one[sub], do_two, NT)
                    score = p_scr[step % 2, head, sub, :].astype(F32) * (prob_back - delta)
                    diag[pair * 2 + head, :, 384 - 128 * blk : 896 - 128 * blk] += score
                    ds_scr[head, sub, :] = score.astype(BF)
                dv_parts.append(dotf(p_scr[step % 2, head], do_two))
                dk_parts.append(dotf(ds_scr[head], q_two))
                dq_parts.append(dotf(k_turn[head * HEAD_DIM : (head + 1) * HEAD_DIM], ds_scr[head]))
            v_ref[rows, lanes] = jnp.where(lane_head == 0, dv_parts[0], dv_parts[1]).astype(BF)
            k_ref[rows, lanes] = jnp.where(lane_head == 0, dk_parts[0], dk_parts[1]).astype(BF)
            q_ref[rows, lanes] = jnp.concatenate(dq_parts, axis=0).T.astype(BF)

        def project(third):
            near = slice(third * TILE, (third + 1) * TILE)
            far = slice(HALF + third * TILE, HALF + (third + 1) * TILE)
            for mat, grad in enumerate((q_ref, k_ref, v_ref)):
                mat_rows = slice(mat * model, (mat + 1) * model)
                both = jnp.concatenate([grad[:, near], grad[:, far]], axis=1)
                value = dotf(hid_t[...], both).astype(BF)
                gq[mat_rows, near] = value[:, :TILE]
                gq[mat_rows, far] = value[:, TILE:]

        plan = {
            0: (lambda: red_0(11), lambda: red_2(9)),
            1: (lambda: red_1(10),),
            2: (lambda: red_0(4), lambda: red_2(5)),
            3: (lambda: project(0), lambda: red_s(0, gq), lambda: red_1(11), lambda: red_0(3)),
            4: (lambda: red_2(10),),
            5: (lambda: red_1(4), lambda: red_0(0, gq)),
            6: (lambda: red_2(11), lambda: red_1(3)),
            7: (lambda: project(1), lambda: red_s(1, gq), lambda: red_2(4)),
            8: (lambda: red_3(2), lambda: red_1(0, gq)),
            9: (lambda: red_0(1, gq), lambda: red_2(3)),
            11: (lambda: project(2), lambda: red_s(2, gq), lambda: red_1(1, gq), lambda: red_2(0, gq)),
        }

        def back_step(step, _):
            attend_back(step)
            for at, todo in plan.items():
                @pl.when(step == at)
                def _():
                    for act in todo:
                        act()
            return 0

        lax.fori_loop(0, 12, back_step, 0)

        gacc[0] = jnp.zeros((8, model), F32)

        def gin_copy(i):
            rows = slice(i * tile, (i + 1) * tile)
            return pltpu.make_async_copy(rb_ref.at[rows], gin_hbm.at[rows], out_sem.at[i])

        def tail(i):
            rows = slice(i * tile, (i + 1) * tile)
            u = (
                dotf(q_ref[rows, :], weights[:model, :], NT)
                + dotf(k_ref[rows, :], weights[model : 2 * model, :], NT)
                + dotf(v_ref[rows, :], weights[2 * model : 3 * model, :], NT)
            )
            value = tokens[rows, :].astype(F32)
            inv_rms = lax.rsqrt(jnp.mean(value * value, axis=-1, keepdims=True) + EPS_NORM)
            gu = u * gains_ref[0:1, :]
            normal = value * inv_rms
            mean = jnp.mean(gu * normal, axis=-1, keepdims=True)
            rb_ref[rows, :] += inv_rms * (gu - normal * mean)
            gin_copy(i).start()
            gacc[0] += jnp.sum((u * normal).reshape(tile // 8, 8, model), axis=0)

        def unskew(g, _):
            accs = [
                jnp.concatenate([diag[g * 4 + h], jnp.zeros((128, 128), F32)], axis=1) for h in range(4)
            ]
            size = 64
            while size >= 1:
                accs = [acc[:size] + pltpu.roll(acc[size:], 1024 - size, 1) for acc in accs]
                size //= 2
            for h in range(4):
                drow[pl.ds(g * 4 + h, 1), :] = accs[h]
            return 0

        drow[...] = jnp.zeros_like(drow)
        lax.fori_loop(0, HEADS // 4, unskew, 0)
        onehot = (lax.broadcasted_iota(jnp.int32, (128, 1024), 0) == bucket_ref[...]).astype(F32)
        table = lax.dot_general(drow[...], onehot, NT, precision=HIGHEST, preferred_element_type=F32)
        small[0, :, :model] = jnp.zeros((16, model), F32)
        small[0, 1:2, :model] = jnp.sum(gacc[1], axis=0, keepdims=True)
        small[0, :, model:] = table
        red_0(2, gq)
        red_3(1)
        red_3_at(3)
        tail(0)
        red_2(1, gq)
        red_1(2, gq)
        tail(1)
        tail(2)
        red_2(2, gq)
        red_3_at(0)
        tail(3)
        small[0, 0:1, :model] = jnp.sum(gacc[0], axis=0, keepdims=True)
        sm_copy(0).start()
        red_3_at(1)
        sm_next(0)
        sm_copy(1).start()
        red_3_at(2)
        sm_next(1)
        sm_copy(2).start()
        for i in range(ntile):
            gin_copy(i).wait()
        red_sent(range(4))
        units_copy(3, z_send.at[0], z_recv.at[0, 0]).wait_send()

    def sm_copy(step):
        device = ((other, chip), (core, xnbr), (core, ynbr))[step]
        return remote(small.at[2 * step], small.at[2 * step + 1], sm_send.at[step], sm_recv.at[step], device)

    def sm_plane(off):
        return remote(
            small.at[6], small.at[7 + zpos], sm_send.at[2 + off], sm_recv.at[2 + off],
            (core, lax.rem(zpos + off, 4) * 4 + col),
        )

    def sm_next(step):
        sm_copy(step).wait_recv()
        small[2 * step + 2] = small[2 * step] + small[2 * step + 1]

    pl.run_scoped(
        backward,
        pltpu.VMEM((3 * model, model), BF),
        pltpu.VMEM((model, ntok), BF),
        pltpu.VMEM((HEADS, 128, 896), F32),
        pltpu.VMEM((16, 1024), F32),
        pltpu.VMEM((2, 2, LEN, LEN), BF),
        pltpu.VMEM((2, LEN, LEN), BF),
    )

    early = 6 * PAIR_ROWS

    def half_copy(part):
        at = (slice(0, early), slice(early, PACK_ROWS))[part]
        return remote(
            slot_ref.at[at, own_cols], slot_ref.at[at, own_cols], half_send.at[part], half_recv.at[part],
            (other, chip),
        )

    sm_next(2)
    for off in (1, 2, 3):
        sm_plane(off).start()
    small[7 + zpos] = small[6]
    for rnd in (2, 1):
        keep_copy(rnd).wait()
        pieces_copy(a2a_send.at[rnd], a2a_recv.at[rnd]).wait_recv()
    half_copy(1).start()
    keep_copy(0).wait()
    pieces_copy(a2a_send.at[0], a2a_recv.at[0]).wait_recv()
    half_copy(0).start()
    for off in (1, 2, 3):
        sm_plane(off).wait_recv()
    small_ref[...] = small[7] + small[8] + small[9] + small[10]
    for step in range(3):
        sm_copy(step).wait_send()
    for off in (1, 2, 3):
        sm_plane(off).wait_send()
    red_sent(range(4, 4 * ROUNDS))
    for rnd in range(ROUNDS):
        pieces_copy(a2a_send.at[rnd], a2a_recv.at[rnd]).wait_send()
        if rnd:
            units_copy(3, z_send.at[rnd], z_recv.at[rnd, 0]).wait_send()
    half_copy(1).wait()
    half_copy(0).wait()


def layer_pass(owners, gains, table, buckets, sizes, lens, master, tokens, cot):
    ntok, model = tokens.shape
    rows = 8 * master.shape[0]
    dma = pltpu.SemaphoreType.DMA
    half = RANGE_ROWS // 2
    pairs = 4 * ROUNDS
    act = pltpu.VMEM((ntok, model), BF)
    return pl.pallas_call(
        layer_kernel,
        name="layer_pass",
        out_shape=(
            jax.ShapeDtypeStruct((ntok, model), BF),
            jax.ShapeDtypeStruct((ntok, model), F32),
            jax.ShapeDtypeStruct((2 * HEADS, LEN, LEN), BF),
            jax.ShapeDtypeStruct((PACK_ROWS, model), BF),
            jax.ShapeDtypeStruct((16, model + 128), F32),
            jax.ShapeDtypeStruct((8, PACK_ROWS), jnp.int32),
            jax.ShapeDtypeStruct((7 * RANGE_ROWS, TILE), BF),
        ),
        in_specs=[VM] * 5 + [SM] + [ANY] * 3,
        out_specs=(ANY, ANY, ANY, ANY, VM, VM, ANY),
        scratch_shapes=[
            pltpu.VMEM((rows, model), BF),
            pltpu.VMEM((rows, HALF), BF),
            pltpu.VMEM((pairs, RANGE_ROWS, TILE), BF),
            pltpu.VMEM((pairs, RANGE_ROWS, TILE), BF),
            pltpu.VMEM((pairs, half, TILE), BF),
            pltpu.VMEM((pairs, half, TILE), BF),
            pltpu.VMEM((ROUNDS, 4, RANGE_ROWS, TILE), BF),
            pltpu.VMEM((ROUNDS, RANGE_ROWS, TILE), BF),
            pltpu.VMEM((3, PACK_ROWS, TILE), BF),
            pltpu.VMEM((ROUNDS, PACK_ROWS, TILE), BF),
            act, act, act, act, act, act, act,
            pltpu.VMEM((ntok, model), F32),
            pltpu.VMEM((11, 16, model + 128), F32),
            pltpu.VMEM((2, 8, model), F32),
            pltpu.VMEM((ROUNDS, RANGE_ROWS), jnp.int32),
            pltpu.VMEM((16, 1024), F32),
            pltpu.VMEM((1, 1024), jnp.int32),
            pltpu.VMEM((8, model), F32),
            pltpu.VMEM((16, 128), F32),
            dma((3,)), dma((4,)), dma((2, 2)),
            dma((ROUNDS,)), dma((ROUNDS,)), dma((ROUNDS,)), dma((ROUNDS, 4)), dma((pairs,)),
            dma((pairs,)), dma((pairs,)), dma((pairs,)), dma((pairs,)), dma((pairs,)),
            dma((pairs,)), dma((pairs,)), dma((pairs,)), dma((pairs,)), dma((pairs,)), dma((pairs,)),
            dma((ROUNDS,)), dma((ROUNDS, 4)), dma((ROUNDS,)), dma((ROUNDS,)), dma((2,)), dma((2,)),
            dma((6,)), dma((6,)),
        ],
        compiler_params=pltpu.CompilerParams(
            collective_id=0, has_side_effects=True, vmem_limit_bytes=62 * 2**20
        ),
    )(owners, gains, table, buckets, sizes, lens, master, tokens, cot)


BETA_ONE = 0.5
BETA_TWO = 0.75
LEARN_RATE = 0.06
SMALL_RATE = 0.4
WEIGHT_DECAY = 0.01
EPS_ADAM = 1e-08
OPT_STEP = 3


def adamw(weight, gradient, first_in, second, rate):
    first_out = BETA_ONE * first_in + (1.0 - BETA_ONE) * gradient
    second_out = BETA_TWO * second + (1.0 - BETA_TWO) * gradient * gradient
    fix_first = 1.0 - BETA_ONE**OPT_STEP
    fix_second = 1.0 - BETA_TWO**OPT_STEP
    update = first_out / fix_first / (jnp.sqrt(second_out / fix_second) + EPS_ADAM)
    return (first_out, second_out, weight - rate * (update + WEIGHT_DECAY * weight))


def adam_kernel(
    idx_ref, packed_ref, small_ref, gains_ref, gains_first_ref, gains_second_ref,
    table_ref, table_first_ref, table_second_ref, master_ref, first_ref, second_ref, out_ref, gin_ref,
    grad_ref, fnew_ref, snew_ref, mnew_ref, copy_ref, out_new_ref, gin_new_ref,
    ggrad_ref, gfnew_ref, gsnew_ref, gnew_ref, tgrad_ref, tfnew_ref, tsnew_ref, tnew_ref,
):
    rows, model = master_ref.shape
    onehot = (
        lax.broadcasted_iota(jnp.int32, (rows, PACK_ROWS), 0) + pl.program_id(0) * rows == idx_ref[:1, :]
    ).astype(F32).astype(BF)
    grad = dotf(onehot, packed_ref[...])
    first_new, second_new, master_new = adamw(
        master_ref[...], grad, first_ref[...], second_ref[...], LEARN_RATE
    )
    grad_ref[...] = grad
    fnew_ref[...] = first_new
    snew_ref[...] = second_new
    mnew_ref[...] = master_new
    copy_ref[...] = master_new.astype(BF)
    out_new_ref[...] = out_ref[...]
    gin_new_ref[...] = gin_ref[...]

    @pl.when(pl.program_id(0) == 0)
    def _():
        heads, buckets = table_ref.shape
        grad = small_ref[:2, :model]
        ggrad_ref[...] = grad
        gfnew_ref[...], gsnew_ref[...], gnew_ref[...] = adamw(
            gains_ref[...], grad, gains_first_ref[...], gains_second_ref[...], SMALL_RATE
        )
        grad = small_ref[:heads, model : model + buckets]
        tgrad_ref[...] = grad
        tfnew_ref[...], tsnew_ref[...], tnew_ref[...] = adamw(
            table_ref[...], grad, table_first_ref[...], table_second_ref[...], SMALL_RATE
        )


ADAM_STEPS = 2


def adam_pass(whole, master, first, second, out, gin):
    rows, model = master.shape
    ntok = out.shape[0]

    def part(total):
        return pl.BlockSpec((total // ADAM_STEPS, model), lambda i: (i, 0))

    def full(a):
        return pl.BlockSpec(a.shape, lambda i: (0, 0))

    def like(a):
        return jax.ShapeDtypeStruct(a.shape, a.dtype)

    wide = like(master)
    gains, table = whole[3], whole[6]
    return pl.pallas_call(
        adam_kernel,
        name="adam_pass",
        grid=(ADAM_STEPS,),
        out_shape=(wide, wide, wide, wide, jax.ShapeDtypeStruct((rows, model), BF), like(out), like(gin))
        + (like(gains),) * 4 + (like(table),) * 4,
        in_specs=[full(a) for a in whole] + [part(rows)] * 3 + [part(ntok)] * 2,
        out_specs=(part(rows),) * 5 + (part(ntok),) * 2 + (full(gains),) * 4 + (full(table),) * 4,
        compiler_params=pltpu.CompilerParams(vmem_limit_bytes=60 * 2**20),
    )(*whole, master, first, second, out, gin)


def fast_body(
    tokens, cotangent, master_slots, first_slots, second_slots, norm_gains, gains_first, gains_second,
    bias_table, table_first, table_second, bucket_ids, valid_len, task_sizes, owner_list,
):
    block_out, grad_input, _, packed, small, index, _ = layer_pass(
        owner_list[None, :], norm_gains, bias_table.T, bucket_ids[None, :], task_sizes[None, :], valid_len,
        master_slots, tokens, cotangent,
    )
    whole = (
        index, packed, small, norm_gains, gains_first, gains_second, bias_table.T, table_first.T, table_second.T
    )
    (
        grad_slots, first_new, second_new, master_new, master_copy, block_out, grad_input,
        grad_gains, gains_first_new, gains_second_new, gains_new,
        grad_table, table_first_new, table_second_new, table_new,
    ) = adam_pass(whole, master_slots, first_slots, second_slots, block_out, grad_input)
    return (
        block_out, grad_input, grad_slots, grad_gains, grad_table.T, first_new, second_new, master_new, master_copy,
        gains_first_new, gains_second_new, gains_new, table_first_new.T, table_second_new.T, table_new.T,
    )


def product(left_side, right_side):
    return jnp.dot(left_side, right_side, preferred_element_type=jnp.float32)


def contract_rows(left_side, right_side):
    return lax.dot_general(
        left_side, right_side, (((0,), (0,)), ((), ())), preferred_element_type=jnp.float32
    )


def contract_cols(left_side, right_side):
    return lax.dot_general(
        left_side, right_side, (((1,), (1,)), ((), ())), preferred_element_type=jnp.float32
    )


def smooth_act(values):
    return jax.nn.gelu(values, approximate=True)


def slot_layout(owner_list, devices, capacity):
    block_count = owner_list.shape[0]
    onehot = (owner_list[:, None] == jnp.arange(devices, dtype=jnp.int32)[None, :]).astype(
        jnp.int32
    )
    rank_in = jnp.sum((jnp.cumsum(onehot, axis=0) - onehot) * onehot, axis=1)
    slot_of = owner_list * capacity + rank_in
    source = (
        jnp.zeros((devices * capacity,), jnp.int32)
        .at[slot_of]
        .set(jnp.arange(block_count, dtype=jnp.int32))
    )
    filled = (
        jnp.zeros((devices * capacity,), jnp.int32)
        .at[slot_of]
        .set(jnp.ones((block_count,), jnp.int32))
    )
    return (slot_of, source, filled, rank_in)


def split_rows(all_rows):
    model_width = all_rows.shape[1]
    hidden = (all_rows.shape[0] - 4 * model_width) // 2
    return (
        all_rows[:model_width],
        all_rows[model_width : 2 * model_width],
        all_rows[2 * model_width : 3 * model_width],
        all_rows[3 * model_width : 4 * model_width],
        all_rows[4 * model_width : 4 * model_width + hidden],
        all_rows[4 * model_width + hidden :],
    )


def norm_raw(values, gain_row):
    inv_rms = lax.rsqrt(jnp.mean(values * values, axis=-1, keepdims=True) + EPS_NORM)
    return values * inv_rms * gain_row


def expand_bias(bias_table, bucket_ids):
    length = (bucket_ids.shape[0] + 1) // 2
    onehot = jax.nn.one_hot(bucket_ids, bias_table.shape[0], dtype=jnp.float32)
    rel_rows = jnp.dot(onehot, bias_table, precision=HIGHEST)
    reverse = rel_rows[::-1].T
    tiled_rows = jnp.tile(reverse, (1, length + 1))[:, : 2 * length * length]
    return tiled_rows.reshape(reverse.shape[0], length, 2 * length)[:, :, :length][:, :, ::-1]


def masked_scores(seq_query, seq_key, rel_bias, length):
    scores = (
        jnp.einsum("qhd,khd->hqk", seq_query, seq_key, preferred_element_type=jnp.float32)
        + rel_bias
    )
    live = jnp.arange(seq_key.shape[0], dtype=jnp.int32)[None, None, :] < length
    return jnp.where(live, scores, NEG_FILL)


def adamw_step(weight, gradient, first_in, second, step_value, rate):
    first_out = BETA_ONE * first_in + (1.0 - BETA_ONE) * gradient
    second_out = BETA_TWO * second + (1.0 - BETA_TWO) * gradient * gradient
    fix_first = 1.0 - jnp.power(jnp.float32(BETA_ONE), step_value)
    fix_second = 1.0 - jnp.power(jnp.float32(BETA_TWO), step_value)
    update = first_out / fix_first / (jnp.sqrt(second_out / fix_second) + EPS_ADAM)
    return (first_out, second_out, weight - rate * (update + WEIGHT_DECAY * weight))


def plain_body(
    tokens,
    cotangent,
    master_slots,
    first_slots,
    second_slots,
    norm_gains,
    gains_first,
    gains_second,
    bias_table,
    table_first,
    table_second,
    bucket_ids,
    valid_len,
    task_sizes,
    owner_list,
):
    devices = lax.axis_size("fsdp")
    replicas = lax.axis_size("dp")
    my_index = lax.axis_index("fsdp")
    capacity = master_slots.shape[0] // BROWS
    model_width = master_slots.shape[1]
    seq_dev = valid_len.shape[0]
    slot_of, source, filled, rank_in = slot_layout(owner_list, devices, capacity)
    sent_shard = master_slots.astype(jnp.bfloat16)

    def rebuild(gathered):
        blocks = gathered.reshape(devices * capacity, BROWS, model_width)[slot_of]
        return split_rows(blocks.reshape(-1, model_width))

    def by_seq(array_in):
        return array_in.reshape(seq_dev, LEN, HEADS, HEAD_DIM)

    def to_rows(array_in):
        return array_in.reshape(-1, model_width).astype(jnp.bfloat16)

    w_query, w_key, w_value, w_out, w_in, w_down = rebuild(
        lax.all_gather(sent_shard, "fsdp", axis=0, tiled=True)
    )
    rel_bias, bias_pull = jax.vjp(lambda table_in: expand_bias(table_in, bucket_ids), bias_table)
    inputs = tokens.astype(jnp.float32)
    hidden_one, norm_one_pull = jax.vjp(norm_raw, inputs, norm_gains[0])
    hidden_one = hidden_one.astype(jnp.bfloat16)
    queries = product(hidden_one, w_query).astype(jnp.bfloat16)
    keys_in = product(hidden_one, w_key).astype(jnp.bfloat16)
    values_in = product(hidden_one, w_value).astype(jnp.bfloat16)

    def attend_one(packed):
        seq_query, seq_key, seq_value, length = packed
        scores = masked_scores(seq_query, seq_key, rel_bias, length)
        row_max = jnp.max(scores, axis=-1, keepdims=True)
        exp_scores = jnp.exp(scores - row_max)
        totals = jnp.sum(exp_scores, axis=-1, keepdims=True)
        attn_probs = (exp_scores / totals).astype(jnp.bfloat16)
        context = jnp.einsum(
            "hqk,khd->qhd", attn_probs, seq_value, preferred_element_type=jnp.float32
        )
        return (context, row_max + jnp.log(totals))

    context, log_sums = lax.map(
        attend_one, (by_seq(queries), by_seq(keys_in), by_seq(values_in), valid_len)
    )
    context = to_rows(context)
    resid = inputs + product(context, w_out)
    hidden_two, norm_two_pull = jax.vjp(norm_raw, resid, norm_gains[1])
    hidden_two = hidden_two.astype(jnp.bfloat16)
    pre_act = contract_cols(hidden_two, w_in)
    active_full, act_pull = jax.vjp(smooth_act, pre_act)
    active = active_full.astype(jnp.bfloat16)
    block_out = (resid + product(active, w_down)).astype(jnp.bfloat16)
    first_seq = (lax.axis_index("dp") * devices + my_index) * seq_dev
    seq_ids = first_seq + jnp.arange(seq_dev, dtype=jnp.int32)
    task_ends = jnp.cumsum(task_sizes)
    task_count = task_sizes.shape[0]
    task_of = jnp.sum((task_ends[None, :] <= seq_ids[:, None]).astype(jnp.int32), axis=1)
    size_of = jnp.sum(
        jnp.where(
            task_of[:, None] == jnp.arange(task_count, dtype=jnp.int32)[None, :],
            task_sizes[None, :],
            0,
        ),
        axis=1,
    )
    seq_weight = jnp.float32(seq_dev * replicas * devices) / (
        jnp.float32(task_count) * size_of.astype(jnp.float32)
    )
    back_out = (
        cotangent.astype(jnp.float32).reshape(seq_dev, LEN, model_width) * seq_weight[:, None, None]
    ).reshape(-1, model_width)
    w_query, w_key, w_value, w_out, w_in, w_down = rebuild(
        lax.all_gather(sent_shard, "fsdp", axis=0, tiled=True)
    )
    down_back = back_out.astype(jnp.bfloat16)
    grad_down = contract_rows(active, down_back)
    act_back = contract_cols(down_back, w_down)
    (pre_full,) = act_pull(act_back)
    pre_back = pre_full.astype(jnp.bfloat16)
    grad_in = contract_rows(pre_back, hidden_two)
    resid_part, gain_two = norm_two_pull(product(pre_back, w_in))
    resid_back = back_out + resid_part
    out_back = resid_back.astype(jnp.bfloat16)
    grad_out = contract_rows(context, out_back)
    context_back = contract_cols(out_back, w_out).astype(jnp.bfloat16)

    def attend_back(score_sum, packed):
        seq_query, seq_key, seq_value, seq_back, length, log_sum = packed
        scores = masked_scores(seq_query, seq_key, rel_bias, length)
        attn_probs = jnp.exp(scores - log_sum)
        value_grad = jnp.einsum(
            "hqk,qhd->khd",
            attn_probs.astype(jnp.bfloat16),
            seq_back,
            preferred_element_type=jnp.float32,
        )
        prob_grad = jnp.einsum(
            "qhd,khd->hqk", seq_back, seq_value, preferred_element_type=jnp.float32
        )
        score_back = (
            attn_probs * (prob_grad - jnp.sum(attn_probs * prob_grad, axis=-1, keepdims=True))
        ).astype(jnp.bfloat16)
        query_grad = jnp.einsum(
            "hqk,khd->qhd", score_back, seq_key, preferred_element_type=jnp.float32
        )
        key_grad = jnp.einsum(
            "hqk,qhd->khd", score_back, seq_query, preferred_element_type=jnp.float32
        )
        return (score_sum + score_back.astype(jnp.float32), (query_grad, key_grad, value_grad))

    score_sum, (query_grad, key_grad, value_grad) = lax.scan(
        attend_back,
        jnp.zeros_like(rel_bias),
        (
            by_seq(queries),
            by_seq(keys_in),
            by_seq(values_in),
            by_seq(context_back),
            valid_len,
            log_sums,
        ),
    )
    query_back = to_rows(query_grad)
    key_back = to_rows(key_grad)
    value_back = to_rows(value_grad)
    grad_query = contract_rows(hidden_one, query_back)
    grad_key = contract_rows(hidden_one, key_back)
    grad_value = contract_rows(hidden_one, value_back)
    hidden_back = (
        contract_cols(query_back, w_query)
        + contract_cols(key_back, w_key)
        + contract_cols(value_back, w_value)
    )
    input_part, gain_one = norm_one_pull(hidden_back)
    grad_input = resid_back + input_part
    (table_grad,) = bias_pull(score_sum)
    grad_rows = jnp.concatenate(
        [grad_query, grad_key, grad_value, grad_out, grad_in, grad_down], axis=0
    )
    slotted = jnp.where(
        filled[:, None, None] > 0, grad_rows.reshape(-1, BROWS, model_width)[source], 0.0
    ).reshape(-1, model_width)
    owned_grads = lax.psum_scatter(slotted, "fsdp", scatter_dimension=0, tiled=True)
    grad_slots = lax.psum(owned_grads, "dp")
    grad_gains, grad_table = lax.psum((jnp.stack([gain_one, gain_two]), table_grad), ("dp", "fsdp"))
    step_value = jnp.float32(OPT_STEP)
    first_new, second_new, master_new = adamw_step(
        master_slots, grad_slots, first_slots, second_slots, step_value, LEARN_RATE
    )
    gains_first_new, gains_second_new, gains_new = adamw_step(
        norm_gains, grad_gains, gains_first, gains_second, step_value, SMALL_RATE
    )
    table_first_new, table_second_new, table_new = adamw_step(
        bias_table, grad_table, table_first, table_second, step_value, SMALL_RATE
    )
    return (
        block_out,
        grad_input,
        grad_slots,
        grad_gains,
        grad_table,
        first_new,
        second_new,
        master_new,
        master_new.astype(jnp.bfloat16),
        gains_first_new,
        gains_second_new,
        gains_new,
        table_first_new,
        table_second_new,
        table_new,
    )


def solution(mesh):
    in_specs = (
        P(("dp", "fsdp"), None),
        P(("dp", "fsdp"), None),
        P("fsdp", None),
        P("fsdp", None),
        P("fsdp", None),
        P(),
        P(),
        P(),
        P(),
        P(),
        P(),
        P(),
        P(("dp", "fsdp")),
        P(),
        P(),
    )
    out_specs = (
        P(("dp", "fsdp"), None),
        P(("dp", "fsdp"), None),
        P("fsdp", None),
        P(),
        P(),
        P("fsdp", None),
        P("fsdp", None),
        P("fsdp", None),
        P("fsdp", None),
        P(),
        P(),
        P(),
        P(),
        P(),
        P(),
    )
    fast = dict(mesh.shape) == {"dp": 2, "fsdp": CHIPS}
    body = fast_body if fast else plain_body
    return jax.shard_map(
        body, mesh=mesh, in_specs=in_specs, out_specs=out_specs, check_vma=False)
```

```python
import functools
import jax
import jax.numpy as jnp
from jax import lax
from jax.experimental import pallas as pl
from jax.experimental.pallas import tpu as pltpu
from jax.sharding import PartitionSpec as P

HEADS = 12
HEAD_DIM = 64
LEN = 512
BROWS = 8
EPS_NORM = 1e-06
NEG_FILL = -1e30
HIGHEST = lax.Precision.HIGHEST
MESH = pl.DeviceIdType.MESH
BF = jnp.bfloat16
F32 = jnp.float32

CHIPS = 16
RANGE_BLOCKS = 72
RANGE_ROWS = 576
PAIR_ROWS = 80
PACK_ROWS = CHIPS * PAIR_ROWS
ROUNDS = 3
TILE = 128
HALF = 3 * TILE
FF_CHUNK = 512
GELU_A = 0.7978845608028654
GELU_B = 0.044715 * GELU_A
NN = (((1,), (0,)), ((), ()))
NT = (((1,), (1,)), ((), ()))
TN = (((0,), (0,)), ((), ()))
VM = pl.BlockSpec(memory_space=pltpu.VMEM)
SM = pl.BlockSpec(memory_space=pltpu.SMEM)
ANY = pl.BlockSpec(memory_space=pl.ANY)


def dotf(a, b, dims=NN):
    return lax.dot_general(a, b, dims, preferred_element_type=F32)


def unit_place(v):
    first = 1 - (v + 36) // 48
    last = (v + 30) // 48
    i = last * (v // 3 - 6)
    late, turn = i // 5, i % 5
    rng = (
        first * (v % 4)
        + (1 - first - last) * (v // 3)
        + last * (10 + 3 * late + turn // 2 - turn % 2 * (4 + late))
    )
    return rng, first * (v // 4) + (1 - first) * (v % 3)


def unit_slice(v, core):
    rng, til = unit_place(v)
    return (
        pl.ds(pl.multiple_of(rng * RANGE_ROWS, 64), RANGE_ROWS),
        pl.ds(pl.multiple_of(core * HALF + til * TILE, TILE), TILE),
    )


def half_slice(v, core, half):
    rng, til = unit_place(v)
    return (
        pl.ds(pl.multiple_of(rng * RANGE_ROWS + half * (RANGE_ROWS // 2), 32), RANGE_ROWS // 2),
        pl.ds(pl.multiple_of(core * HALF + til * TILE, TILE), TILE),
    )


def piece_rows(i):
    return pl.ds(pl.multiple_of(i * PAIR_ROWS, 16), PAIR_ROWS)


def place():
    core = lax.axis_index("dp")
    chip = lax.axis_index("fsdp")
    xpos = chip % 2
    ypos = (chip // 2) % 2
    zpos = chip // 4
    return core, chip, xpos, ypos, zpos, chip + 1 - 2 * xpos, chip + 2 - 4 * ypos


def remote(src, dst, ssem, rsem, device):
    return pltpu.make_async_remote_copy(
        src_ref=src, dst_ref=dst, send_sem=ssem, recv_sem=rsem, device_id=device, device_id_type=MESH
    )


def as_column(row):
    return jnp.broadcast_to(row, (8, row.shape[1])).astype(F32).T[:, :1].astype(jnp.int32)


def gelu_pair(v):
    sq = v * v
    half = 0.5 + 0.5 * jnp.tanh(v * (GELU_A + GELU_B * sq))
    act = v * half
    return act, half + act * (1.0 - half) * (2.0 * GELU_A + 6.0 * GELU_B * sq)


def layer_kernel(
    owner_ref, gains_ref, table_ref, buckets_ref, sizes_ref, len_ref,
    master_hbm, tokens_hbm, cot_hbm,
    out_hbm, gin_hbm, p_hbm, slot_ref, small_ref, index_ref, spare,
    weights, sib, xin, yin, dain, dbin, zin, ubuf, sendbuf, recvbuf,
    q_ref, k_ref, v_ref, ctx_ref, tokens, hidden, cb_ref, rb_ref, small, gacc,
    idx_row_ref, rel_ref, bucket_ref, weight_ref, pad,
    load_sem, out_sem, p_sem,
    fa_send, fa_recv, fz_send, fz_recv, f_send, fx_recv, fy_recv, fda_recv, fdb_recv, fs_recv,
    r_send, h_recv, da_recv, db_recv, x_recv, y_recv, z_send, z_recv, a2a_send, a2a_recv, half_send, half_recv,
    sm_send, sm_recv,
):
    core, chip, xpos, ypos, zpos, xnbr, ynbr = place()
    other = 1 - core
    ntok, model = tokens.shape
    hid = (weights.shape[0] - 4 * model) // 2
    nchunk = hid // FF_CHUNK
    first_in, first_down = 4 * model, 4 * model + hid
    col = ypos * 2 + xpos
    xcol = ypos * 2 + (1 - xpos)
    ycol = (1 - ypos) * 2 + xpos
    dcol = (1 - ypos) * 2 + (1 - xpos)
    own_cols = pl.ds(pl.multiple_of(core * HALF, TILE), HALF)
    tile = 256
    ntile = ntok // tile

    def units_copy(count, send_sem, recv_sem):
        at = spare.at[pl.ds(0, count * RANGE_ROWS)]
        return remote(at, at, send_sem, recv_sem, (other, chip))

    def pieces_copy(send_sem, recv_sem):
        at = recvbuf.at[0, pl.ds(0, (CHIPS - 1) * PAIR_ROWS)]
        return remote(at, at, send_sem, recv_sem, (other, chip))

    load_tokens = pltpu.make_async_copy(tokens_hbm, tokens, load_sem.at[0])
    load_tokens.start()

    barrier = pltpu.get_barrier_semaphore()
    for step in range(1, CHIPS):
        pl.semaphore_signal(
            barrier, inc=1, device_id=(core, lax.rem(chip + step, CHIPS)), device_id_type=MESH
        )
    pl.semaphore_signal(barrier, inc=1, device_id=(other, chip), device_id_type=MESH)

    def lanes(rows, width):
        return lax.broadcasted_iota(jnp.int32, (rows, width), 1)

    def steps(rows, width):
        return lax.broadcasted_iota(jnp.int32, (rows, width), 0)

    def mark(mask):
        return mask.astype(F32).astype(BF)

    def eight(row):
        return jnp.broadcast_to(row, (8, row.shape[1]))

    owners = owner_ref[...]
    nblock = owners.shape[1]

    def pack_index():
        mine = mark(eight(owners == chip))
        block, low = steps(nblock, 128), lanes(nblock, 128) * RANGE_BLOCKS
        count = dotf(mine, mark(jnp.logical_and(block >= low, block < low + RANGE_BLOCKS)))
        start = dotf(mine, mark(block < low))
        row, low = lanes(128, PACK_ROWS), steps(128, PACK_ROWS) * PAIR_ROWS
        spread = mark(jnp.logical_and(row >= low, row < low + PAIR_ROWS))
        count = dotf(count.astype(BF), spread)
        start = dotf(start.astype(BF), spread)
        rng = dotf(lanes(8, 128).astype(F32).astype(BF), spread)
        inner = lanes(8, PACK_ROWS).astype(F32) - PAIR_ROWS * rng
        turn = jnp.floor(inner * (1.0 / BROWS))
        index = jnp.where(turn < count, start * BROWS + inner, -1.0)
        index_ref[...] = index.astype(jnp.int32)

    def unit_index():
        row, low = lanes(128, RANGE_ROWS), steps(128, RANGE_ROWS) * BROWS
        spread = mark(jnp.logical_and(row >= low, row < low + BROWS))
        inner = lanes(8, RANGE_ROWS).astype(F32) - BROWS * dotf(lanes(8, 128).astype(F32).astype(BF), spread)
        values = eight(owners).astype(F32).astype(BF)
        for rnd in range(ROUNDS):
            rng, _ = unit_place(rnd * CHIPS + chip)
            at = lanes(nblock, 128)
            pick = jnp.logical_and(steps(nblock, 128) == at + rng * RANGE_BLOCKS, at < RANGE_BLOCKS)
            owner = dotf(values, mark(pick))
            same = jnp.logical_and(owner.T[:, :1] == owner[:1], steps(128, 128) < lanes(128, 128))
            rank = jnp.sum(same.astype(F32), axis=0, keepdims=True)
            index = (
                PAIR_ROWS * dotf(owner.astype(BF), spread)
                + BROWS * dotf(eight(rank).astype(BF), spread)
                + inner
            )
            idx_row_ref[rnd : rnd + 1, :] = index[:1].astype(jnp.int32)

    def relative():
        count = buckets_ref.shape[1]
        pad[...] = jnp.full((16, 128), 127.0, F32)
        for i in range(8):
            width = min(128, count - 128 * i)
            pad[i : i + 1, :width] = buckets_ref[:, 128 * i : 128 * i + width].astype(F32)
        turned = dotf(pad[:8].astype(BF), mark(steps(128, 128) + lanes(128, 128) == 127))
        for i in range(8):
            source = 6 - i if i < 7 else 7
            bucket_ref[:, 128 * i : 128 * (i + 1)] = turned[source : source + 1].astype(jnp.int32)
        pad[...] = jnp.zeros((16, 128), F32)
        pad[: table_ref.shape[0], : table_ref.shape[1]] = table_ref[...]
        rel_ref[...] = lax.dot_general(
            pad[...], (steps(128, 1024) == bucket_ref[...]).astype(F32), NN,
            precision=HIGHEST, preferred_element_type=F32,
        )

    def sequence_weights():
        count = sizes_ref.shape[1]
        seqs = ntok // LEN
        pad[...] = jnp.zeros((16, 128), F32)
        pad[:1, :count] = sizes_ref[...].astype(F32)
        sizes = pad[:8]
        ends = dotf(sizes.astype(BF), mark(steps(128, 128) <= lanes(128, 128)))
        for i in range(seqs):
            seq = ((core * CHIPS + chip) * seqs + i).astype(F32)
            inside = jnp.logical_and(ends - sizes <= seq, seq < ends)
            size = jnp.sum(jnp.where(inside, sizes, 0.0)[:1], axis=1, keepdims=True)
            weight = jnp.float32(seqs * 2 * CHIPS) / (jnp.float32(count) * size)
            weight_ref[i : i + 1, :] = jnp.broadcast_to(weight, (1, model))

    def pack(mbuf):
        load = pltpu.make_async_copy(master_hbm.at[:, own_cols], mbuf, load_sem.at[1])
        load.start()
        pack_index()
        load.wait()
        own_half = mbuf[...].astype(BF)
        index = as_column(index_ref[:1, :])
        for part in range(4):
            rows = PACK_ROWS // 4
            onehot = (
                lax.broadcasted_iota(jnp.int32, (rows, mbuf.shape[0]), 1)
                == index[part * rows : (part + 1) * rows, :]
            ).astype(F32).astype(BF)
            packed = dotf(onehot, own_half).astype(BF)
            for til in range(3):
                sendbuf[til, part * rows : (part + 1) * rows, :] = packed[:, til * TILE : (til + 1) * TILE]

    pl.run_scoped(pack, pltpu.VMEM((master_hbm.shape[0], HALF), F32))
    pl.semaphore_wait(barrier, CHIPS)

    def fa_copy(rnd, step):
        dest = lax.rem(chip + step, CHIPS)
        rng, til = unit_place(rnd * CHIPS + dest)
        return remote(
            sendbuf.at[til, piece_rows(rng), :], recvbuf.at[rnd, piece_rows(chip), :],
            fa_send.at[rnd], fa_recv.at[rnd], (core, dest),
        )

    def fa_start(rnd):
        for step in range(1, CHIPS):
            fa_copy(rnd, step).start()
        rng, til = unit_place(rnd * CHIPS + chip)
        recvbuf[rnd, piece_rows(chip), :] = sendbuf[til, piece_rows(rng), :]

    def own_unit(rnd):
        pieces_copy(fa_send.at[rnd], fa_recv.at[rnd]).wait_recv()
        v = rnd * CHIPS + chip
        index = as_column(idx_row_ref[rnd : rnd + 1, :])
        for part in range(2):
            rows = RANGE_ROWS // 2
            onehot = (
                lax.broadcasted_iota(jnp.int32, (rows, PACK_ROWS), 1)
                == index[part * rows : (part + 1) * rows, :]
            ).astype(F32).astype(BF)
            weights[half_slice(v, core, part)] = dotf(onehot, recvbuf[rnd]).astype(BF)

    def nearest(k):
        return (zpos, zpos + 1 - 2 * (zpos % 2), 2 - zpos // 2, 3 - 3 * (zpos // 2))[k]

    def behind(p):
        return nearest(p % 4) if p < 8 else p % 4

    def fwd_unit(p, column):
        return p // 4 * CHIPS + behind(p) * 4 + column

    def fz_copy(rnd, source, up):
        at = unit_slice(rnd * CHIPS + source * 4 + col, core)
        dest = chip + (4 if up else -4)
        return remote(weights.at[at], weights.at[at], fz_send.at[rnd], fz_recv.at[rnd, source], (core, dest))

    def fz_start(rnd):
        @pl.when(zpos < 3)
        def _():
            fz_copy(rnd, zpos, True).start()

        @pl.when(zpos > 0)
        def _():
            fz_copy(rnd, zpos, False).start()

    def fz_relay(rnd, k):
        source = nearest(k)
        units_copy(1, fz_send.at[rnd], fz_recv.at[rnd, source]).wait_recv()

        @pl.when(jnp.logical_and(source < zpos, zpos < 3))
        def _():
            fz_copy(rnd, source, True).start()

        @pl.when(jnp.logical_and(source > zpos, zpos > 0))
        def _():
            fz_copy(rnd, source, False).start()

    def fz_sent(rnd):
        inner = zpos % 3 > 0

        @pl.when(inner)
        def _():
            units_copy(5, fz_send.at[rnd], fz_recv.at[rnd, 0]).wait_send()

        @pl.when(jnp.logical_not(inner))
        def _():
            units_copy(1, fz_send.at[rnd], fz_recv.at[rnd, 0]).wait_send()

    def fx_copy(p):
        at = unit_slice(fwd_unit(p, col), core)
        return remote(weights.at[at], weights.at[at], f_send.at[p], fx_recv.at[p], (core, xnbr))

    def fy_copy(p):
        at = unit_slice(fwd_unit(p, col), core)
        return remote(weights.at[at], weights.at[at], f_send.at[p], fy_recv.at[p], (core, ynbr))

    def fda_copy(p):
        at = half_slice(fwd_unit(p, xcol), core, 0)
        return remote(weights.at[at], weights.at[at], f_send.at[p], fda_recv.at[p], (core, ynbr))

    def fdb_copy(p):
        at = half_slice(fwd_unit(p, ycol), core, 1)
        return remote(weights.at[at], weights.at[at], f_send.at[p], fdb_recv.at[p], (core, xnbr))

    def fs_copy(p, kind):
        at = unit_slice(fwd_unit(p, (col, xcol, ycol, dcol)[kind]), core)
        return remote(weights.at[at], weights.at[at], f_send.at[p], fs_recv.at[p], (other, chip))

    def fwd_a(p):
        if p < 8 and p % 4:
            fz_relay(p // 4, p % 4)
        fx_copy(p).start()
        fy_copy(p).start()
        fs_copy(p, 0).start()

    def fwd_b(p):
        fx_copy(p).wait_recv()
        fda_copy(p).start()
        fs_copy(p, 1).start()
        fy_copy(p).wait_recv()
        fdb_copy(p).start()
        fs_copy(p, 2).start()

    def fwd_c(p):
        fda_copy(p).wait_recv()
        fdb_copy(p).wait_recv()
        fs_copy(p, 3).start()

    def fwd_done(*pairs):
        for p in pairs:
            units_copy(4, f_send.at[p], fs_recv.at[p]).wait_recv()

    def fwd_sent(rounds, pairs):
        for rnd in rounds:
            pieces_copy(fa_send.at[rnd], fa_recv.at[rnd]).wait_send()
            fz_sent(rnd)
        for p in pairs:
            units_copy(7, f_send.at[p], fs_recv.at[p]).wait_send()

    lane_head = lax.broadcasted_iota(jnp.int32, (LEN, 128), 1) // HEAD_DIM

    def forward(base, s_scr, p_scr):
        fa_start(0)
        unit_index()
        relative()
        sequence_weights()
        load_tokens.wait()
        for part in range(ntok // 128):
            rows = slice(part * 128, (part + 1) * 128)
            values = tokens[rows, :].astype(F32)
            inv_rms = lax.rsqrt(jnp.mean(values * values, axis=-1, keepdims=True) + EPS_NORM)
            hidden[rows, :] = (values * inv_rms * gains_ref[0:1, :]).astype(BF)

        def bands(h, _):
            wide = jnp.broadcast_to(rel_ref[pl.ds(h, 1), :], (128, 1024))
            base[pl.ds(h, 1)] = pltpu.roll(wide, 0, 1, stride=1, stride_axis=0)[:, :896][None]
            return 0

        lax.fori_loop(0, HEADS, bands, 0)
        own_unit(0)
        fz_start(0)
        fwd_a(0)
        fwd_a(1)
        fwd_b(0)
        fwd_a(2)
        fwd_b(1)
        fwd_c(0)
        fwd_a(3)
        fa_start(1)
        fwd_b(2)
        fwd_c(1)
        fwd_done(0, 1)

        def third_of(step):
            nearer = jnp.minimum(zpos, 2)
            middle = 1 - zpos % 2 * (1 - zpos // 2)
            turn = step // 4
            return jnp.where(turn == 0, nearer, jnp.where(turn == 1, middle, 3 - nearer - middle))

        def projections(step):
            third = third_of(step)
            near = pl.ds(pl.multiple_of(third * TILE, TILE), TILE)
            far = pl.ds(pl.multiple_of(HALF + third * TILE, TILE), TILE)
            for mat, out_ref in enumerate((q_ref, k_ref, v_ref)):
                mat_rows = slice(mat * model, (mat + 1) * model)
                both = jnp.concatenate([weights[mat_rows, near], weights[mat_rows, far]], axis=1)
                value = dotf(hidden[...], both).astype(BF)
                out_ref[:, near] = value[:, :TILE]
                out_ref[:, far] = value[:, TILE:]

        row_id = lax.broadcasted_iota(jnp.int32, (128, LEN), 0)

        def seq_pair(step):
            return step % 2, third_of(step) + 3 * (step // 2 % 2)

        def p_copy(step, head):
            seq, pair = seq_pair(step)
            return pltpu.make_async_copy(
                p_scr.at[step % 2, head], p_hbm.at[seq * HEADS + pair * 2 + head], p_sem.at[step % 2, head]
            )

        def attend(step):
            seq, pair = seq_pair(step)
            rows = pl.ds(pl.multiple_of(seq * LEN, LEN), LEN)
            lanes = pl.ds(pl.multiple_of(pair * 128, 128), 128)
            length = len_ref[seq]

            @pl.when(step >= 2)
            def _():
                for head in range(2):
                    p_copy(step - 2, head).wait()

            q_two = q_ref[rows, lanes]
            k_two = k_ref[rows, lanes]
            v_two = v_ref[rows, lanes].T
            outs = []
            for head in range(2):
                k_one = jnp.where(lane_head == head, k_two, jnp.zeros_like(k_two))
                top = jnp.full((8, LEN), NEG_FILL, F32)
                for blk in range(4):
                    score = dotf(k_one[blk * 128 : (blk + 1) * 128], q_two, NT)
                    score = score + base[pair * 2 + head, :, 384 - 128 * blk : 896 - 128 * blk]
                    score = jnp.where(row_id + blk * 128 < length, score, NEG_FILL)
                    s_scr[head, blk * 128 : (blk + 1) * 128, :] = score
                    top = jnp.maximum(top, jnp.max(score.reshape(16, 8, LEN), axis=0))
                top = jnp.max(top, axis=0, keepdims=True)
                total = jnp.zeros((8, LEN), F32)
                for blk in range(4):
                    part = jnp.exp(s_scr[head, blk * 128 : (blk + 1) * 128, :] - top)
                    s_scr[head, blk * 128 : (blk + 1) * 128, :] = part
                    total = total + jnp.sum(part.reshape(16, 8, LEN), axis=0)
                inverse = 1.0 / jnp.sum(total, axis=0, keepdims=True)
                for blk in range(4):
                    p_scr[step % 2, head, blk * 128 : (blk + 1) * 128, :] = (
                        s_scr[head, blk * 128 : (blk + 1) * 128, :] * inverse
                    ).astype(BF)
                outs.append(dotf(v_two[head * HEAD_DIM : (head + 1) * HEAD_DIM], p_scr[step % 2, head]))
                p_copy(step, head).start()
            ctx_ref[rows, lanes] = jnp.concatenate(outs, axis=0).T.astype(BF)

        plan = {
            0: (lambda: own_unit(1), lambda: fz_start(1), lambda: fwd_a(4), lambda: fa_start(2), lambda: fwd_c(2)),
            1: (lambda: fwd_b(3),),
            3: (lambda: fwd_c(3), lambda: fwd_a(5), lambda: fwd_done(2)),
            4: (lambda: own_unit(2), lambda: fz_start(2), lambda: fwd_b(4)),
            5: (lambda: fwd_a(6),),
            6: (lambda: fwd_c(4), lambda: fwd_b(5)),
            7: (lambda: fwd_a(7), lambda: fwd_done(3)),
            8: (lambda: fz_relay(2, 1), lambda: fwd_c(5), lambda: fwd_b(6)),
            9: (lambda: fwd_b(7),),
            10: (lambda: fz_relay(2, 2), lambda: fwd_c(6)),
            11: (lambda: fz_relay(2, 3), lambda: fwd_a(8), lambda: fwd_c(7)),
        }

        def attend_step(step, _):
            @pl.when(step % 4 == 0)
            def _():
                projections(step)

            attend(step)
            for at, todo in plan.items():
                @pl.when(step == at)
                def _():
                    for act in todo:
                        act()
            return 0

        lax.fori_loop(0, 12, attend_step, 0)
        for step in (10, 11):
            for head in range(2):
                p_copy(step, head).wait()

    pl.run_scoped(
        forward,
        pltpu.VMEM((HEADS, 128, 896), F32),
        pltpu.VMEM((2, LEN, LEN), F32),
        pltpu.VMEM((2, 2, LEN, LEN), BF),
    )

    def src_of(p, gq):
        return gq if p < 3 else weights

    def unit(p, column):
        return p * 4 + column

    def sib_copy(p, column, gq=None):
        v = unit(p, column)
        return remote(
            src_of(p, gq).at[unit_slice(v, other)], sib.at[unit_slice(v, 0)],
            r_send.at[p], h_recv.at[p], (other, chip),
        )

    def da_copy(p, gq=None):
        at = half_slice(unit(p, dcol), core, 0)
        return remote(src_of(p, gq).at[at], dain.at[p], r_send.at[p], da_recv.at[p], (core, ynbr))

    def db_copy(p, gq=None):
        at = half_slice(unit(p, dcol), core, 1)
        return remote(src_of(p, gq).at[at], dbin.at[p], r_send.at[p], db_recv.at[p], (core, xnbr))

    def x_copy(p, gq=None):
        at = unit_slice(unit(p, xcol), core)
        return remote(src_of(p, gq).at[at], xin.at[p], r_send.at[p], x_recv.at[p], (core, xnbr))

    def y_copy(p, gq=None):
        at = unit_slice(unit(p, ycol), core)
        return remote(src_of(p, gq).at[at], yin.at[p], r_send.at[p], y_recv.at[p], (core, ynbr))

    def z_copy(p, gq=None):
        rnd, zt = p // 4, p % 4
        at = unit_slice(unit(p, col), core)
        return remote(
            src_of(p, gq).at[at], zin.at[rnd, zpos], z_send.at[rnd], z_recv.at[rnd, zpos], (core, zt * 4 + col)
        )

    def z_arrived(rnd, src):
        return remote(zin.at[rnd, src], zin.at[rnd, src], z_send.at[rnd], z_recv.at[rnd, src], (core, xnbr))

    def add(ref, at, incoming):
        ref[at] = (ref[at].astype(F32) + incoming.astype(F32)).astype(BF)

    def red_s(p, gq=None):
        for column in range(4):
            sib_copy(p, column, gq).start()

    def red_0(p, gq=None):
        units_copy(4, r_send.at[p], h_recv.at[p]).wait_recv()
        for column in range(4):
            add(src_of(p, gq), unit_slice(unit(p, column), core), sib[unit_slice(unit(p, column), 0)])
        da_copy(p, gq).start()
        db_copy(p, gq).start()

    def red_1(p, gq=None):
        da_copy(p, gq).wait_recv()
        add(src_of(p, gq), half_slice(unit(p, xcol), core, 0), dain[p])
        x_copy(p, gq).start()
        db_copy(p, gq).wait_recv()
        add(src_of(p, gq), half_slice(unit(p, ycol), core, 1), dbin[p])
        y_copy(p, gq).start()

    def red_2(p, gq=None):
        x_copy(p, gq).wait_recv()
        y_copy(p, gq).wait_recv()
        at = unit_slice(unit(p, col), core)
        total = (src_of(p, gq)[at].astype(F32) + xin[p].astype(F32) + yin[p].astype(F32)).astype(BF)

        @pl.when(zpos == p % 4)
        def _():
            ubuf[p // 4] = total

        @pl.when(zpos != p % 4)
        def _():
            src_of(p, gq)[at] = total
            z_copy(p, gq).start()

    def a2a_copy(rnd, step):
        dest = lax.rem(chip + step, CHIPS)
        rng, til = unit_place(rnd * CHIPS + chip)
        return remote(
            recvbuf.at[rnd, piece_rows(dest), :],
            slot_ref.at[piece_rows(rng), pl.ds(pl.multiple_of(core * HALF + til * TILE, TILE), TILE)],
            a2a_send.at[rnd], a2a_recv.at[rnd], (core, dest),
        )

    def keep_copy(rnd):
        rng, til = unit_place(rnd * CHIPS + chip)
        return pltpu.make_async_copy(
            recvbuf.at[rnd, piece_rows(chip), :],
            slot_ref.at[piece_rows(rng), pl.ds(pl.multiple_of(core * HALF + til * TILE, TILE), TILE)],
            load_sem.at[rnd],
        )

    def red_3(rnd):
        total = ubuf[rnd].astype(F32)
        for off in (1, 2, 3):
            src = lax.rem(zpos + off, 4)
            z_arrived(rnd, src).wait_recv()
            total = total + zin[rnd, src].astype(F32)
        total = total.astype(BF)
        for part in range(4):
            rows = PACK_ROWS // 4
            onehot = (
                lax.broadcasted_iota(jnp.int32, (rows, RANGE_ROWS), 0) + part * rows
                == idx_row_ref[rnd : rnd + 1, :]
            ).astype(F32).astype(BF)
            recvbuf[rnd, part * rows : (part + 1) * rows, :] = dotf(onehot, total).astype(BF)
        for step in range(1, CHIPS):
            a2a_copy(rnd, step).start()
        keep_copy(rnd).start()

    def red_sent(pairs):
        for p in pairs:
            units_copy(7, r_send.at[p], h_recv.at[p]).wait_send()

    def red_3_at(plane):
        @pl.when(zpos == plane)
        def _():
            red_3(0)

    def out_copy(i):
        rows = pl.ds(pl.multiple_of(i * tile, tile), tile)
        return pltpu.make_async_copy(hidden.at[rows], out_hbm.at[rows], out_sem.at[i])

    def feed(cot, down, out_acc, u_acc, act_s, pb_s):
        load_cot = pltpu.make_async_copy(cot_hbm, cot, load_sem.at[2])
        load_cot.start()
        load_cot.wait()
        fwd_a(9)
        fwd_done(4, 5, 6, 7)

        def head(i, _):
            rows = pl.ds(pl.multiple_of(i * tile, tile), tile)
            value = tokens[rows, :].astype(F32) + dotf(ctx_ref[rows, :], weights[3 * model : 4 * model, :])
            rb_ref[rows, :] = value
            inv_rms = lax.rsqrt(jnp.mean(value * value, axis=-1, keepdims=True) + EPS_NORM)
            hidden[rows, :] = (value * inv_rms * gains_ref[1:2, :]).astype(BF)
            down[rows, :] = (cot[rows, :].astype(F32) * weight_ref[pl.ds(i * tile // LEN, 1), :]).astype(BF)
            out_acc[rows, :] = jnp.zeros((tile, model), F32)
            u_acc[rows, :] = jnp.zeros((tile, model), F32)
            return 0

        lax.fori_loop(0, ntile, head, 0)
        fwd_a(10)
        fwd_b(8)

        middle = {
            0: (lambda: fwd_a(11), lambda: fwd_b(9), lambda: fwd_c(8), lambda: fwd_sent((0, 1), range(8))),
            1: (lambda: fwd_b(11), lambda: fwd_c(10), lambda: fwd_sent((2,), (8,))),
            2: (lambda: fwd_c(11),),
            3: (lambda: red_0(6), lambda: fwd_sent((), (9, 10))),
            4: (lambda: red_1(6), lambda: red_0(8), lambda: fwd_sent((), (11,))),
            5: (lambda: red_2(6), lambda: red_0(9), lambda: red_1(8)),
        }
        plan = {
            0: (lambda: fwd_done(8), lambda: fwd_b(10), lambda: fwd_c(9)),
            2: (lambda: red_s(6), lambda: red_s(7), lambda: fwd_done(9, 10)),
            3: (lambda: red_s(8), lambda: red_0(7), lambda: fwd_done(11)),
            4: (lambda: red_s(9), lambda: red_1(7)),
            5: (lambda: red_s(5), lambda: red_s(10), lambda: red_s(11), lambda: red_2(7)),
        }

        def run(what, now):
            for at, todo in what.items():
                @pl.when(now == at)
                def _():
                    for act in todo:
                        act()

        def chunk(c, _):
            rows_in = pl.ds(pl.multiple_of(first_in + c * FF_CHUNK, FF_CHUNK), FF_CHUNK)
            rows_down = pl.ds(pl.multiple_of(first_down + c * FF_CHUNK, FF_CHUNK), FF_CHUNK)
            for i in range(ntile):
                rows = slice(i * tile, (i + 1) * tile)
                pre = dotf(hidden[rows, :], weights[rows_in, :], NT)
                back = dotf(down[rows, :], weights[rows_down, :], NT)
                act, slope = gelu_pair(pre)
                act = act.astype(BF)
                pre_back = (back * slope).astype(BF)
                act_s[rows, :] = act
                pb_s[rows, :] = pre_back
                out_acc[rows, :] += dotf(act, weights[rows_down, :])
                u_acc[rows, :] += dotf(pre_back, weights[rows_in, :])
            run(middle, c)
            weights[rows_down, :] = dotf(act_s[...], down[...], TN).astype(BF)
            weights[rows_in, :] = dotf(pb_s[...], hidden[...], TN).astype(BF)
            run(plan, c)
            return 0

        lax.fori_loop(0, nchunk, chunk, 0)

        tail_plan = {
            0: (lambda: red_0(5),),
            1: (lambda: red_1(9),),
            2: (lambda: red_0(10),),
            3: (lambda: red_2(8),),
        }
        gacc[1] = jnp.zeros((8, model), F32)

        def tail(i, _):
            rows = pl.ds(pl.multiple_of(i * tile, tile), tile)
            value = rb_ref[rows, :]
            out = (value + out_acc[rows, :]).astype(BF)
            inv_rms = lax.rsqrt(jnp.mean(value * value, axis=-1, keepdims=True) + EPS_NORM)
            u = u_acc[rows, :]
            gu = u * gains_ref[1:2, :]
            normal = value * inv_rms
            mean = jnp.mean(gu * normal, axis=-1, keepdims=True)
            back = cot[rows, :].astype(F32) * weight_ref[pl.ds(i * tile // LEN, 1), :] + inv_rms * (gu - normal * mean)
            rb_ref[rows, :] = back
            low = back.astype(BF)
            down[rows, :] = low
            hidden[rows, :] = out
            out_copy(i).start()
            cb_ref[rows, :] = dotf(low, weights[3 * model : 4 * model, :], NT).astype(BF)
            gacc[1] += jnp.sum((u * normal).reshape(tile // 8, 8, model), axis=0)
            run(tail_plan, i)
            return 0

        lax.fori_loop(0, ntile, tail, 0)
        weights[3 * model : 4 * model, :] = dotf(ctx_ref[...], down[...], TN).astype(BF)
        red_s(4)
        red_s(3)
        red_1(5)
        for i in range(ntile):
            out_copy(i).wait()

    pl.run_scoped(
        feed,
        pltpu.VMEM((ntok, model), BF),
        pltpu.VMEM((ntok, model), BF),
        pltpu.VMEM((ntok, model), F32),
        pltpu.VMEM((ntok, model), F32),
        pltpu.VMEM((ntok, FF_CHUNK), BF),
        pltpu.VMEM((ntok, FF_CHUNK), BF),
    )

    def backward(gq, hid_t, diag, drow, p_scr, ds_scr):
        def split(step):
            turn = step // 2
            return step % 2, turn // 2 + 3 * (turn % 2)

        def p_copy(step, head):
            seq, pair = split(step)
            return pltpu.make_async_copy(
                p_hbm.at[seq * HEADS + pair * 2 + head], p_scr.at[step % 2, head], p_sem.at[step % 2, head]
            )

        for head in range(2):
            p_copy(0, head).start()
        diag[...] = jnp.zeros_like(diag)
        for part in range(ntok // 128):
            rows = slice(part * 128, (part + 1) * 128)
            values = tokens[rows, :].astype(F32)
            inv_rms = lax.rsqrt(jnp.mean(values * values, axis=-1, keepdims=True) + EPS_NORM)
            hid_t[:, rows] = (values * inv_rms * gains_ref[0:1, :]).astype(BF).T

        def attend_back(step):
            seq, pair = split(step)
            rows = pl.ds(pl.multiple_of(seq * LEN, LEN), LEN)
            lanes = pl.ds(pl.multiple_of(pair * 128, 128), 128)

            @pl.when(step + 1 < 12)
            def _():
                for head in range(2):
                    p_copy(step + 1, head).start()

            q_two, k_two, v_two, do_two = (
                q_ref[rows, lanes], k_ref[rows, lanes], v_ref[rows, lanes], cb_ref[rows, lanes]
            )
            k_turn = k_two.T
            inner = (do_two.astype(F32) * ctx_ref[rows, lanes].astype(F32)).T
            dv_parts, dk_parts, dq_parts = [], [], []
            for head in range(2):
                p_copy(step, head).wait()
                delta = jnp.sum(inner[head * HEAD_DIM : (head + 1) * HEAD_DIM], axis=0, keepdims=True)
                v_one = jnp.where(lane_head == head, v_two, jnp.zeros_like(v_two))
                for blk in range(4):
                    sub = slice(blk * 128, (blk + 1) * 128)
                    prob_back = dotf(v_one[sub], do_two, NT)
                    score = p_scr[step % 2, head, sub, :].astype(F32) * (prob_back - delta)
                    diag[pair * 2 + head, :, 384 - 128 * blk : 896 - 128 * blk] += score
                    ds_scr[head, sub, :] = score.astype(BF)
                dv_parts.append(dotf(p_scr[step % 2, head], do_two))
                dk_parts.append(dotf(ds_scr[head], q_two))
                dq_parts.append(dotf(k_turn[head * HEAD_DIM : (head + 1) * HEAD_DIM], ds_scr[head]))
            v_ref[rows, lanes] = jnp.where(lane_head == 0, dv_parts[0], dv_parts[1]).astype(BF)
            k_ref[rows, lanes] = jnp.where(lane_head == 0, dk_parts[0], dk_parts[1]).astype(BF)
            q_ref[rows, lanes] = jnp.concatenate(dq_parts, axis=0).T.astype(BF)

        def project(third):
            near = slice(third * TILE, (third + 1) * TILE)
            far = slice(HALF + third * TILE, HALF + (third + 1) * TILE)
            for mat, grad in enumerate((q_ref, k_ref, v_ref)):
                mat_rows = slice(mat * model, (mat + 1) * model)
                both = jnp.concatenate([grad[:, near], grad[:, far]], axis=1)
                value = dotf(hid_t[...], both).astype(BF)
                gq[mat_rows, near] = value[:, :TILE]
                gq[mat_rows, far] = value[:, TILE:]

        plan = {
            0: (lambda: red_0(11), lambda: red_2(9)),
            1: (lambda: red_1(10),),
            2: (lambda: red_0(4), lambda: red_2(5)),
            3: (lambda: project(0), lambda: red_s(0, gq), lambda: red_1(11), lambda: red_0(3)),
            4: (lambda: red_2(10),),
            5: (lambda: red_1(4), lambda: red_0(0, gq)),
            6: (lambda: red_2(11), lambda: red_1(3)),
            7: (lambda: project(1), lambda: red_s(1, gq), lambda: red_2(4)),
            8: (lambda: red_3(2), lambda: red_1(0, gq)),
            9: (lambda: red_0(1, gq), lambda: red_2(3)),
            11: (lambda: project(2), lambda: red_s(2, gq), lambda: red_1(1, gq), lambda: red_2(0, gq)),
        }

        def back_step(step, _):
            attend_back(step)
            for at, todo in plan.items():
                @pl.when(step == at)
                def _():
                    for act in todo:
                        act()
            return 0

        lax.fori_loop(0, 12, back_step, 0)

        gacc[0] = jnp.zeros((8, model), F32)

        def gin_copy(i):
            rows = slice(i * tile, (i + 1) * tile)
            return pltpu.make_async_copy(rb_ref.at[rows], gin_hbm.at[rows], out_sem.at[i])

        def tail(i):
            rows = slice(i * tile, (i + 1) * tile)
            u = (
                dotf(q_ref[rows, :], weights[:model, :], NT)
                + dotf(k_ref[rows, :], weights[model : 2 * model, :], NT)
                + dotf(v_ref[rows, :], weights[2 * model : 3 * model, :], NT)
            )
            value = tokens[rows, :].astype(F32)
            inv_rms = lax.rsqrt(jnp.mean(value * value, axis=-1, keepdims=True) + EPS_NORM)
            gu = u * gains_ref[0:1, :]
            normal = value * inv_rms
            mean = jnp.mean(gu * normal, axis=-1, keepdims=True)
            rb_ref[rows, :] += inv_rms * (gu - normal * mean)
            gin_copy(i).start()
            gacc[0] += jnp.sum((u * normal).reshape(tile // 8, 8, model), axis=0)

        def unskew(g, _):
            accs = [
                jnp.concatenate([diag[g * 4 + h], jnp.zeros((128, 128), F32)], axis=1) for h in range(4)
            ]
            size = 64
            while size >= 1:
                accs = [acc[:size] + pltpu.roll(acc[size:], 1024 - size, 1) for acc in accs]
                size //= 2
            for h in range(4):
                drow[pl.ds(g * 4 + h, 1), :] = accs[h]
            return 0

        drow[...] = jnp.zeros_like(drow)
        lax.fori_loop(0, HEADS // 4, unskew, 0)
        onehot = (lax.broadcasted_iota(jnp.int32, (128, 1024), 0) == bucket_ref[...]).astype(F32)
        table = lax.dot_general(drow[...], onehot, NT, precision=HIGHEST, preferred_element_type=F32)
        small[0, :, :model] = jnp.zeros((16, model), F32)
        small[0, 1:2, :model] = jnp.sum(gacc[1], axis=0, keepdims=True)
        small[0, :, model:] = table
        red_0(2, gq)
        red_3(1)
        red_3_at(3)
        tail(0)
        red_2(1, gq)
        red_1(2, gq)
        tail(1)
        tail(2)
        red_2(2, gq)
        red_3_at(0)
        tail(3)
        small[0, 0:1, :model] = jnp.sum(gacc[0], axis=0, keepdims=True)
        sm_copy(0).start()
        red_3_at(1)
        sm_next(0)
        sm_copy(1).start()
        red_3_at(2)
        sm_next(1)
        sm_copy(2).start()
        for i in range(ntile):
            gin_copy(i).wait()
        red_sent(range(4))
        units_copy(3, z_send.at[0], z_recv.at[0, 0]).wait_send()

    def sm_copy(step):
        device = ((other, chip), (core, xnbr), (core, ynbr))[step]
        return remote(small.at[2 * step], small.at[2 * step + 1], sm_send.at[step], sm_recv.at[step], device)

    def sm_plane(off):
        return remote(
            small.at[6], small.at[7 + zpos], sm_send.at[2 + off], sm_recv.at[2 + off],
            (core, lax.rem(zpos + off, 4) * 4 + col),
        )

    def sm_next(step):
        sm_copy(step).wait_recv()
        small[2 * step + 2] = small[2 * step] + small[2 * step + 1]

    pl.run_scoped(
        backward,
        pltpu.VMEM((3 * model, model), BF),
        pltpu.VMEM((model, ntok), BF),
        pltpu.VMEM((HEADS, 128, 896), F32),
        pltpu.VMEM((16, 1024), F32),
        pltpu.VMEM((2, 2, LEN, LEN), BF),
        pltpu.VMEM((2, LEN, LEN), BF),
    )

    early = 6 * PAIR_ROWS

    def half_copy(part):
        at = (slice(0, early), slice(early, PACK_ROWS))[part]
        return remote(
            slot_ref.at[at, own_cols], slot_ref.at[at, own_cols], half_send.at[part], half_recv.at[part],
            (other, chip),
        )

    sm_next(2)
    for off in (1, 2, 3):
        sm_plane(off).start()
    small[7 + zpos] = small[6]
    for rnd in (2, 1):
        keep_copy(rnd).wait()
        pieces_copy(a2a_send.at[rnd], a2a_recv.at[rnd]).wait_recv()
    half_copy(1).start()
    keep_copy(0).wait()
    pieces_copy(a2a_send.at[0], a2a_recv.at[0]).wait_recv()
    half_copy(0).start()
    for off in (1, 2, 3):
        sm_plane(off).wait_recv()
    small_ref[...] = small[7] + small[8] + small[9] + small[10]
    for step in range(3):
        sm_copy(step).wait_send()
    for off in (1, 2, 3):
        sm_plane(off).wait_send()
    red_sent(range(4, 4 * ROUNDS))
    for rnd in range(ROUNDS):
        pieces_copy(a2a_send.at[rnd], a2a_recv.at[rnd]).wait_send()
        if rnd:
            units_copy(3, z_send.at[rnd], z_recv.at[rnd, 0]).wait_send()
    half_copy(1).wait()
    half_copy(0).wait()


def layer_pass(owners, gains, table, buckets, sizes, lens, master, tokens, cot):
    ntok, model = tokens.shape
    rows = 8 * master.shape[0]
    dma = pltpu.SemaphoreType.DMA
    half = RANGE_ROWS // 2
    pairs = 4 * ROUNDS
    act = pltpu.VMEM((ntok, model), BF)
    return pl.pallas_call(
        layer_kernel,
        name="layer_pass",
        out_shape=(
            jax.ShapeDtypeStruct((ntok, model), BF),
            jax.ShapeDtypeStruct((ntok, model), F32),
            jax.ShapeDtypeStruct((2 * HEADS, LEN, LEN), BF),
            jax.ShapeDtypeStruct((PACK_ROWS, model), BF),
            jax.ShapeDtypeStruct((16, model + 128), F32),
            jax.ShapeDtypeStruct((8, PACK_ROWS), jnp.int32),
            jax.ShapeDtypeStruct((7 * RANGE_ROWS, TILE), BF),
        ),
        in_specs=[VM] * 5 + [SM] + [ANY] * 3,
        out_specs=(ANY, ANY, ANY, ANY, VM, VM, ANY),
        scratch_shapes=[
            pltpu.VMEM((rows, model), BF),
            pltpu.VMEM((rows, HALF), BF),
            pltpu.VMEM((pairs, RANGE_ROWS, TILE), BF),
            pltpu.VMEM((pairs, RANGE_ROWS, TILE), BF),
            pltpu.VMEM((pairs, half, TILE), BF),
            pltpu.VMEM((pairs, half, TILE), BF),
            pltpu.VMEM((ROUNDS, 4, RANGE_ROWS, TILE), BF),
            pltpu.VMEM((ROUNDS, RANGE_ROWS, TILE), BF),
            pltpu.VMEM((3, PACK_ROWS, TILE), BF),
            pltpu.VMEM((ROUNDS, PACK_ROWS, TILE), BF),
            act, act, act, act, act, act, act,
            pltpu.VMEM((ntok, model), F32),
            pltpu.VMEM((11, 16, model + 128), F32),
            pltpu.VMEM((2, 8, model), F32),
            pltpu.VMEM((ROUNDS, RANGE_ROWS), jnp.int32),
            pltpu.VMEM((16, 1024), F32),
            pltpu.VMEM((1, 1024), jnp.int32),
            pltpu.VMEM((8, model), F32),
            pltpu.VMEM((16, 128), F32),
            dma((3,)), dma((4,)), dma((2, 2)),
            dma((ROUNDS,)), dma((ROUNDS,)), dma((ROUNDS,)), dma((ROUNDS, 4)), dma((pairs,)),
            dma((pairs,)), dma((pairs,)), dma((pairs,)), dma((pairs,)), dma((pairs,)),
            dma((pairs,)), dma((pairs,)), dma((pairs,)), dma((pairs,)), dma((pairs,)), dma((pairs,)),
            dma((ROUNDS,)), dma((ROUNDS, 4)), dma((ROUNDS,)), dma((ROUNDS,)), dma((2,)), dma((2,)),
            dma((6,)), dma((6,)),
        ],
        compiler_params=pltpu.CompilerParams(
            collective_id=0, has_side_effects=True, vmem_limit_bytes=62 * 2**20
        ),
    )(owners, gains, table, buckets, sizes, lens, master, tokens, cot)


BETA_ONE = 0.5
BETA_TWO = 0.75
LEARN_RATE = 0.06
SMALL_RATE = 0.4
WEIGHT_DECAY = 0.01
EPS_ADAM = 1e-08
OPT_STEP = 3


def adamw(weight, gradient, first_in, second, rate):
    first_out = BETA_ONE * first_in + (1.0 - BETA_ONE) * gradient
    second_out = BETA_TWO * second + (1.0 - BETA_TWO) * gradient * gradient
    fix_first = 1.0 - BETA_ONE**OPT_STEP
    fix_second = 1.0 - BETA_TWO**OPT_STEP
    update = first_out / fix_first / (jnp.sqrt(second_out / fix_second) + EPS_ADAM)
    return (first_out, second_out, weight - rate * (update + WEIGHT_DECAY * weight))


def adam_kernel(
    idx_ref, packed_ref, small_ref, gains_ref, gains_first_ref, gains_second_ref,
    table_ref, table_first_ref, table_second_ref, master_ref, first_ref, second_ref, out_ref, gin_ref,
    grad_ref, fnew_ref, snew_ref, mnew_ref, copy_ref, out_new_ref, gin_new_ref,
    ggrad_ref, gfnew_ref, gsnew_ref, gnew_ref, tgrad_ref, tfnew_ref, tsnew_ref, tnew_ref,
):
    rows, model = master_ref.shape
    onehot = (
        lax.broadcasted_iota(jnp.int32, (rows, PACK_ROWS), 0) + pl.program_id(0) * rows == idx_ref[:1, :]
    ).astype(F32).astype(BF)
    grad = dotf(onehot, packed_ref[...])
    first_new, second_new, master_new = adamw(
        master_ref[...], grad, first_ref[...], second_ref[...], LEARN_RATE
    )
    grad_ref[...] = grad
    fnew_ref[...] = first_new
    snew_ref[...] = second_new
    mnew_ref[...] = master_new
    copy_ref[...] = master_new.astype(BF)
    out_new_ref[...] = out_ref[...]
    gin_new_ref[...] = gin_ref[...]

    @pl.when(pl.program_id(0) == 0)
    def _():
        heads, buckets = table_ref.shape
        grad = small_ref[:2, :model]
        ggrad_ref[...] = grad
        gfnew_ref[...], gsnew_ref[...], gnew_ref[...] = adamw(
            gains_ref[...], grad, gains_first_ref[...], gains_second_ref[...], SMALL_RATE
        )
        grad = small_ref[:heads, model : model + buckets]
        tgrad_ref[...] = grad
        tfnew_ref[...], tsnew_ref[...], tnew_ref[...] = adamw(
            table_ref[...], grad, table_first_ref[...], table_second_ref[...], SMALL_RATE
        )


ADAM_STEPS = 2


def adam_pass(whole, master, first, second, out, gin):
    rows, model = master.shape
    ntok = out.shape[0]

    def part(total):
        return pl.BlockSpec((total // ADAM_STEPS, model), lambda i: (i, 0))

    def full(a):
        return pl.BlockSpec(a.shape, lambda i: (0, 0))

    def like(a):
        return jax.ShapeDtypeStruct(a.shape, a.dtype)

    wide = like(master)
    gains, table = whole[3], whole[6]
    return pl.pallas_call(
        adam_kernel,
        name="adam_pass",
        grid=(ADAM_STEPS,),
        out_shape=(wide, wide, wide, wide, jax.ShapeDtypeStruct((rows, model), BF), like(out), like(gin))
        + (like(gains),) * 4 + (like(table),) * 4,
        in_specs=[full(a) for a in whole] + [part(rows)] * 3 + [part(ntok)] * 2,
        out_specs=(part(rows),) * 5 + (part(ntok),) * 2 + (full(gains),) * 4 + (full(table),) * 4,
        compiler_params=pltpu.CompilerParams(vmem_limit_bytes=60 * 2**20),
    )(*whole, master, first, second, out, gin)


def fast_body(
    tokens, cotangent, master_slots, first_slots, second_slots, norm_gains, gains_first, gains_second,
    bias_table, table_first, table_second, bucket_ids, valid_len, task_sizes, owner_list,
):
    block_out, grad_input, _, packed, small, index, _ = layer_pass(
        owner_list[None, :], norm_gains, bias_table.T, bucket_ids[None, :], task_sizes[None, :], valid_len,
        master_slots, tokens, cotangent,
    )
    whole = (
        index, packed, small, norm_gains, gains_first, gains_second, bias_table.T, table_first.T, table_second.T
    )
    (
        grad_slots, first_new, second_new, master_new, master_copy, block_out, grad_input,
        grad_gains, gains_first_new, gains_second_new, gains_new,
        grad_table, table_first_new, table_second_new, table_new,
    ) = adam_pass(whole, master_slots, first_slots, second_slots, block_out, grad_input)
    return (
        block_out, grad_input, grad_slots, grad_gains, grad_table.T, first_new, second_new, master_new, master_copy,
        gains_first_new, gains_second_new, gains_new, table_first_new.T, table_second_new.T, table_new.T,
    )


def product(left_side, right_side):
    return jnp.dot(left_side, right_side, preferred_element_type=jnp.float32)


def contract_rows(left_side, right_side):
    return lax.dot_general(
        left_side, right_side, (((0,), (0,)), ((), ())), preferred_element_type=jnp.float32
    )


def contract_cols(left_side, right_side):
    return lax.dot_general(
        left_side, right_side, (((1,), (1,)), ((), ())), preferred_element_type=jnp.float32
    )


def smooth_act(values):
    return jax.nn.gelu(values, approximate=True)


def slot_layout(owner_list, devices, capacity):
    block_count = owner_list.shape[0]
    onehot = (owner_list[:, None] == jnp.arange(devices, dtype=jnp.int32)[None, :]).astype(
        jnp.int32
    )
    rank_in = jnp.sum((jnp.cumsum(onehot, axis=0) - onehot) * onehot, axis=1)
    slot_of = owner_list * capacity + rank_in
    source = (
        jnp.zeros((devices * capacity,), jnp.int32)
        .at[slot_of]
        .set(jnp.arange(block_count, dtype=jnp.int32))
    )
    filled = (
        jnp.zeros((devices * capacity,), jnp.int32)
        .at[slot_of]
        .set(jnp.ones((block_count,), jnp.int32))
    )
    return (slot_of, source, filled, rank_in)


def split_rows(all_rows):
    model_width = all_rows.shape[1]
    hidden = (all_rows.shape[0] - 4 * model_width) // 2
    return (
        all_rows[:model_width],
        all_rows[model_width : 2 * model_width],
        all_rows[2 * model_width : 3 * model_width],
        all_rows[3 * model_width : 4 * model_width],
        all_rows[4 * model_width : 4 * model_width + hidden],
        all_rows[4 * model_width + hidden :],
    )


def norm_raw(values, gain_row):
    inv_rms = lax.rsqrt(jnp.mean(values * values, axis=-1, keepdims=True) + EPS_NORM)
    return values * inv_rms * gain_row


def expand_bias(bias_table, bucket_ids):
    length = (bucket_ids.shape[0] + 1) // 2
    onehot = jax.nn.one_hot(bucket_ids, bias_table.shape[0], dtype=jnp.float32)
    rel_rows = jnp.dot(onehot, bias_table, precision=HIGHEST)
    reverse = rel_rows[::-1].T
    tiled_rows = jnp.tile(reverse, (1, length + 1))[:, : 2 * length * length]
    return tiled_rows.reshape(reverse.shape[0], length, 2 * length)[:, :, :length][:, :, ::-1]


def masked_scores(seq_query, seq_key, rel_bias, length):
    scores = (
        jnp.einsum("qhd,khd->hqk", seq_query, seq_key, preferred_element_type=jnp.float32)
        + rel_bias
    )
    live = jnp.arange(seq_key.shape[0], dtype=jnp.int32)[None, None, :] < length
    return jnp.where(live, scores, NEG_FILL)


def adamw_step(weight, gradient, first_in, second, step_value, rate):
    first_out = BETA_ONE * first_in + (1.0 - BETA_ONE) * gradient
    second_out = BETA_TWO * second + (1.0 - BETA_TWO) * gradient * gradient
    fix_first = 1.0 - jnp.power(jnp.float32(BETA_ONE), step_value)
    fix_second = 1.0 - jnp.power(jnp.float32(BETA_TWO), step_value)
    update = first_out / fix_first / (jnp.sqrt(second_out / fix_second) + EPS_ADAM)
    return (first_out, second_out, weight - rate * (update + WEIGHT_DECAY * weight))


def plain_body(
    tokens,
    cotangent,
    master_slots,
    first_slots,
    second_slots,
    norm_gains,
    gains_first,
    gains_second,
    bias_table,
    table_first,
    table_second,
    bucket_ids,
    valid_len,
    task_sizes,
    owner_list,
):
    devices = lax.axis_size("fsdp")
    replicas = lax.axis_size("dp")
    my_index = lax.axis_index("fsdp")
    capacity = master_slots.shape[0] // BROWS
    model_width = master_slots.shape[1]
    seq_dev = valid_len.shape[0]
    slot_of, source, filled, rank_in = slot_layout(owner_list, devices, capacity)
    sent_shard = master_slots.astype(jnp.bfloat16)

    def rebuild(gathered):
        blocks = gathered.reshape(devices * capacity, BROWS, model_width)[slot_of]
        return split_rows(blocks.reshape(-1, model_width))

    def by_seq(array_in):
        return array_in.reshape(seq_dev, LEN, HEADS, HEAD_DIM)

    def to_rows(array_in):
        return array_in.reshape(-1, model_width).astype(jnp.bfloat16)

    w_query, w_key, w_value, w_out, w_in, w_down = rebuild(
        lax.all_gather(sent_shard, "fsdp", axis=0, tiled=True)
    )
    rel_bias, bias_pull = jax.vjp(lambda table_in: expand_bias(table_in, bucket_ids), bias_table)
    inputs = tokens.astype(jnp.float32)
    hidden_one, norm_one_pull = jax.vjp(norm_raw, inputs, norm_gains[0])
    hidden_one = hidden_one.astype(jnp.bfloat16)
    queries = product(hidden_one, w_query).astype(jnp.bfloat16)
    keys_in = product(hidden_one, w_key).astype(jnp.bfloat16)
    values_in = product(hidden_one, w_value).astype(jnp.bfloat16)

    def attend_one(packed):
        seq_query, seq_key, seq_value, length = packed
        scores = masked_scores(seq_query, seq_key, rel_bias, length)
        row_max = jnp.max(scores, axis=-1, keepdims=True)
        exp_scores = jnp.exp(scores - row_max)
        totals = jnp.sum(exp_scores, axis=-1, keepdims=True)
        attn_probs = (exp_scores / totals).astype(jnp.bfloat16)
        context = jnp.einsum(
            "hqk,khd->qhd", attn_probs, seq_value, preferred_element_type=jnp.float32
        )
        return (context, row_max + jnp.log(totals))

    context, log_sums = lax.map(
        attend_one, (by_seq(queries), by_seq(keys_in), by_seq(values_in), valid_len)
    )
    context = to_rows(context)
    resid = inputs + product(context, w_out)
    hidden_two, norm_two_pull = jax.vjp(norm_raw, resid, norm_gains[1])
    hidden_two = hidden_two.astype(jnp.bfloat16)
    pre_act = contract_cols(hidden_two, w_in)
    active_full, act_pull = jax.vjp(smooth_act, pre_act)
    active = active_full.astype(jnp.bfloat16)
    block_out = (resid + product(active, w_down)).astype(jnp.bfloat16)
    first_seq = (lax.axis_index("dp") * devices + my_index) * seq_dev
    seq_ids = first_seq + jnp.arange(seq_dev, dtype=jnp.int32)
    task_ends = jnp.cumsum(task_sizes)
    task_count = task_sizes.shape[0]
    task_of = jnp.sum((task_ends[None, :] <= seq_ids[:, None]).astype(jnp.int32), axis=1)
    size_of = jnp.sum(
        jnp.where(
            task_of[:, None] == jnp.arange(task_count, dtype=jnp.int32)[None, :],
            task_sizes[None, :],
            0,
        ),
        axis=1,
    )
    seq_weight = jnp.float32(seq_dev * replicas * devices) / (
        jnp.float32(task_count) * size_of.astype(jnp.float32)
    )
    back_out = (
        cotangent.astype(jnp.float32).reshape(seq_dev, LEN, model_width) * seq_weight[:, None, None]
    ).reshape(-1, model_width)
    w_query, w_key, w_value, w_out, w_in, w_down = rebuild(
        lax.all_gather(sent_shard, "fsdp", axis=0, tiled=True)
    )
    down_back = back_out.astype(jnp.bfloat16)
    grad_down = contract_rows(active, down_back)
    act_back = contract_cols(down_back, w_down)
    (pre_full,) = act_pull(act_back)
    pre_back = pre_full.astype(jnp.bfloat16)
    grad_in = contract_rows(pre_back, hidden_two)
    resid_part, gain_two = norm_two_pull(product(pre_back, w_in))
    resid_back = back_out + resid_part
    out_back = resid_back.astype(jnp.bfloat16)
    grad_out = contract_rows(context, out_back)
    context_back = contract_cols(out_back, w_out).astype(jnp.bfloat16)

    def attend_back(score_sum, packed):
        seq_query, seq_key, seq_value, seq_back, length, log_sum = packed
        scores = masked_scores(seq_query, seq_key, rel_bias, length)
        attn_probs = jnp.exp(scores - log_sum)
        value_grad = jnp.einsum(
            "hqk,qhd->khd",
            attn_probs.astype(jnp.bfloat16),
            seq_back,
            preferred_element_type=jnp.float32,
        )
        prob_grad = jnp.einsum(
            "qhd,khd->hqk", seq_back, seq_value, preferred_element_type=jnp.float32
        )
        score_back = (
            attn_probs * (prob_grad - jnp.sum(attn_probs * prob_grad, axis=-1, keepdims=True))
        ).astype(jnp.bfloat16)
        query_grad = jnp.einsum(
            "hqk,khd->qhd", score_back, seq_key, preferred_element_type=jnp.float32
        )
        key_grad = jnp.einsum(
            "hqk,qhd->khd", score_back, seq_query, preferred_element_type=jnp.float32
        )
        return (score_sum + score_back.astype(jnp.float32), (query_grad, key_grad, value_grad))

    score_sum, (query_grad, key_grad, value_grad) = lax.scan(
        attend_back,
        jnp.zeros_like(rel_bias),
        (
            by_seq(queries),
            by_seq(keys_in),
            by_seq(values_in),
            by_seq(context_back),
            valid_len,
            log_sums,
        ),
    )
    query_back = to_rows(query_grad)
    key_back = to_rows(key_grad)
    value_back = to_rows(value_grad)
    grad_query = contract_rows(hidden_one, query_back)
    grad_key = contract_rows(hidden_one, key_back)
    grad_value = contract_rows(hidden_one, value_back)
    hidden_back = (
        contract_cols(query_back, w_query)
        + contract_cols(key_back, w_key)
        + contract_cols(value_back, w_value)
    )
    input_part, gain_one = norm_one_pull(hidden_back)
    grad_input = resid_back + input_part
    (table_grad,) = bias_pull(score_sum)
    grad_rows = jnp.concatenate(
        [grad_query, grad_key, grad_value, grad_out, grad_in, grad_down], axis=0
    )
    slotted = jnp.where(
        filled[:, None, None] > 0, grad_rows.reshape(-1, BROWS, model_width)[source], 0.0
    ).reshape(-1, model_width)
    owned_grads = lax.psum_scatter(slotted, "fsdp", scatter_dimension=0, tiled=True)
    grad_slots = lax.psum(owned_grads, "dp")
    grad_gains, grad_table = lax.psum((jnp.stack([gain_one, gain_two]), table_grad), ("dp", "fsdp"))
    step_value = jnp.float32(OPT_STEP)
    first_new, second_new, master_new = adamw_step(
        master_slots, grad_slots, first_slots, second_slots, step_value, LEARN_RATE
    )
    gains_first_new, gains_second_new, gains_new = adamw_step(
        norm_gains, grad_gains, gains_first, gains_second, step_value, SMALL_RATE
    )
    table_first_new, table_second_new, table_new = adamw_step(
        bias_table, grad_table, table_first, table_second, step_value, SMALL_RATE
    )
    return (
        block_out,
        grad_input,
        grad_slots,
        grad_gains,
        grad_table,
        first_new,
        second_new,
        master_new,
        master_new.astype(jnp.bfloat16),
        gains_first_new,
        gains_second_new,
        gains_new,
        table_first_new,
        table_second_new,
        table_new,
    )


def solution(mesh):
    in_specs = (
        P(("dp", "fsdp"), None),
        P(("dp", "fsdp"), None),
        P("fsdp", None),
        P("fsdp", None),
        P("fsdp", None),
        P(),
        P(),
        P(),
        P(),
        P(),
        P(),
        P(),
        P(("dp", "fsdp")),
        P(),
        P(),
    )
    out_specs = (
        P(("dp", "fsdp"), None),
        P(("dp", "fsdp"), None),
        P("fsdp", None),
        P(),
        P(),
        P("fsdp", None),
        P("fsdp", None),
        P("fsdp", None),
        P("fsdp", None),
        P(),
        P(),
        P(),
        P(),
        P(),
        P(),
    )
    fast = dict(mesh.shape) == {"dp": 2, "fsdp": CHIPS}
    body = fast_body if fast else plain_body
    return jax.shard_map(
        body, mesh=mesh, in_specs=in_specs, out_specs=out_specs, check_vma=False)
```

```python
import functools
import jax
import jax.numpy as jnp
from jax import lax
from jax.experimental import pallas as pl
from jax.experimental.pallas import tpu as pltpu
from jax.sharding import PartitionSpec as P

HEADS = 12
HEAD_DIM = 64
LEN = 512
BROWS = 8
EPS_NORM = 1e-06
NEG_FILL = -1e30
HIGHEST = lax.Precision.HIGHEST
MESH = pl.DeviceIdType.MESH
BF = jnp.bfloat16
F32 = jnp.float32

CHIPS = 16
RANGE_BLOCKS = 72
RANGE_ROWS = 576
PAIR_ROWS = 80
PACK_ROWS = CHIPS * PAIR_ROWS
ROUNDS = 3
TILE = 128
HALF = 3 * TILE
FF_CHUNK = 512
GELU_A = 0.7978845608028654
GELU_B = 0.044715 * GELU_A
NN = (((1,), (0,)), ((), ()))
NT = (((1,), (1,)), ((), ()))
TN = (((0,), (0,)), ((), ()))
VM = pl.BlockSpec(memory_space=pltpu.VMEM)
SM = pl.BlockSpec(memory_space=pltpu.SMEM)
ANY = pl.BlockSpec(memory_space=pl.ANY)


def dotf(a, b, dims=NN):
    return lax.dot_general(a, b, dims, preferred_element_type=F32)


def unit_place(v):
    first = 1 - (v + 36) // 48
    last = (v + 30) // 48
    i = last * (v // 3 - 6)
    late, turn = i // 5, i % 5
    rng = (
        first * (v % 4)
        + (1 - first - last) * (v // 3)
        + last * (10 + 3 * late + turn // 2 - turn % 2 * (4 + late))
    )
    return rng, first * (v // 4) + (1 - first) * (v % 3)


def unit_slice(v, core):
    rng, til = unit_place(v)
    return (
        pl.ds(pl.multiple_of(rng * RANGE_ROWS, 64), RANGE_ROWS),
        pl.ds(pl.multiple_of(core * HALF + til * TILE, TILE), TILE),
    )


def half_slice(v, core, half):
    rng, til = unit_place(v)
    return (
        pl.ds(pl.multiple_of(rng * RANGE_ROWS + half * (RANGE_ROWS // 2), 32), RANGE_ROWS // 2),
        pl.ds(pl.multiple_of(core * HALF + til * TILE, TILE), TILE),
    )


def piece_rows(i):
    return pl.ds(pl.multiple_of(i * PAIR_ROWS, 16), PAIR_ROWS)


def place():
    core = lax.axis_index("dp")
    chip = lax.axis_index("fsdp")
    xpos = chip % 2
    ypos = (chip // 2) % 2
    zpos = chip // 4
    return core, chip, xpos, ypos, zpos, chip + 1 - 2 * xpos, chip + 2 - 4 * ypos


def remote(src, dst, ssem, rsem, device):
    return pltpu.make_async_remote_copy(
        src_ref=src, dst_ref=dst, send_sem=ssem, recv_sem=rsem, device_id=device, device_id_type=MESH
    )


def as_column(row):
    return jnp.broadcast_to(row, (8, row.shape[1])).astype(F32).T[:, :1].astype(jnp.int32)


def gelu_pair(v):
    sq = v * v
    half = 0.5 + 0.5 * jnp.tanh(v * (GELU_A + GELU_B * sq))
    act = v * half
    return act, half + act * (1.0 - half) * (2.0 * GELU_A + 6.0 * GELU_B * sq)


def layer_kernel(
    owner_ref, gains_ref, table_ref, buckets_ref, sizes_ref, len_ref,
    master_hbm, tokens_hbm, cot_hbm,
    out_hbm, gin_hbm, p_hbm, slot_ref, small_ref, index_ref, spare,
    weights, sib, xin, yin, dain, dbin, zin, ubuf, sendbuf, recvbuf,
    q_ref, k_ref, v_ref, ctx_ref, tokens, hidden, cb_ref, rb_ref, small, gacc,
    idx_row_ref, rel_ref, bucket_ref, weight_ref, pad,
    load_sem, out_sem, p_sem,
    fa_send, fa_recv, fz_send, fz_recv, f_send, fx_recv, fy_recv, fda_recv, fdb_recv, fs_recv,
    r_send, h_recv, da_recv, db_recv, x_recv, y_recv, z_send, z_recv, a2a_send, a2a_recv, half_send, half_recv,
    sm_send, sm_recv,
):
    core, chip, xpos, ypos, zpos, xnbr, ynbr = place()
    other = 1 - core
    ntok, model = tokens.shape
    hid = (weights.shape[0] - 4 * model) // 2
    nchunk = hid // FF_CHUNK
    first_in, first_down = 4 * model, 4 * model + hid
    col = ypos * 2 + xpos
    xcol = ypos * 2 + (1 - xpos)
    ycol = (1 - ypos) * 2 + xpos
    dcol = (1 - ypos) * 2 + (1 - xpos)
    own_cols = pl.ds(pl.multiple_of(core * HALF, TILE), HALF)
    tile = 256
    ntile = ntok // tile

    def units_copy(count, send_sem, recv_sem):
        at = spare.at[pl.ds(0, count * RANGE_ROWS)]
        return remote(at, at, send_sem, recv_sem, (other, chip))

    def pieces_copy(send_sem, recv_sem):
        at = recvbuf.at[0, pl.ds(0, (CHIPS - 1) * PAIR_ROWS)]
        return remote(at, at, send_sem, recv_sem, (other, chip))

    load_tokens = pltpu.make_async_copy(tokens_hbm, tokens, load_sem.at[0])
    load_tokens.start()

    barrier = pltpu.get_barrier_semaphore()
    for step in range(1, CHIPS):
        pl.semaphore_signal(
            barrier, inc=1, device_id=(core, lax.rem(chip + step, CHIPS)), device_id_type=MESH
        )
    pl.semaphore_signal(barrier, inc=1, device_id=(other, chip), device_id_type=MESH)

    def lanes(rows, width):
        return lax.broadcasted_iota(jnp.int32, (rows, width), 1)

    def steps(rows, width):
        return lax.broadcasted_iota(jnp.int32, (rows, width), 0)

    def mark(mask):
        return mask.astype(F32).astype(BF)

    def eight(row):
        return jnp.broadcast_to(row, (8, row.shape[1]))

    owners = owner_ref[...]
    nblock = owners.shape[1]

    def pack_index():
        mine = mark(eight(owners == chip))
        block, low = steps(nblock, 128), lanes(nblock, 128) * RANGE_BLOCKS
        count = dotf(mine, mark(jnp.logical_and(block >= low, block < low + RANGE_BLOCKS)))
        start = dotf(mine, mark(block < low))
        row, low = lanes(128, PACK_ROWS), steps(128, PACK_ROWS) * PAIR_ROWS
        spread = mark(jnp.logical_and(row >= low, row < low + PAIR_ROWS))
        count = dotf(count.astype(BF), spread)
        start = dotf(start.astype(BF), spread)
        rng = dotf(lanes(8, 128).astype(F32).astype(BF), spread)
        inner = lanes(8, PACK_ROWS).astype(F32) - PAIR_ROWS * rng
        turn = jnp.floor(inner * (1.0 / BROWS))
        index = jnp.where(turn < count, start * BROWS + inner, -1.0)
        index_ref[...] = index.astype(jnp.int32)

    def unit_index():
        row, low = lanes(128, RANGE_ROWS), steps(128, RANGE_ROWS) * BROWS
        spread = mark(jnp.logical_and(row >= low, row < low + BROWS))
        inner = lanes(8, RANGE_ROWS).astype(F32) - BROWS * dotf(lanes(8, 128).astype(F32).astype(BF), spread)
        values = eight(owners).astype(F32).astype(BF)
        for rnd in range(ROUNDS):
            rng, _ = unit_place(rnd * CHIPS + chip)
            at = lanes(nblock, 128)
            pick = jnp.logical_and(steps(nblock, 128) == at + rng * RANGE_BLOCKS, at < RANGE_BLOCKS)
            owner = dotf(values, mark(pick))
            same = jnp.logical_and(owner.T[:, :1] == owner[:1], steps(128, 128) < lanes(128, 128))
            rank = jnp.sum(same.astype(F32), axis=0, keepdims=True)
            index = (
                PAIR_ROWS * dotf(owner.astype(BF), spread)
                + BROWS * dotf(eight(rank).astype(BF), spread)
                + inner
            )
            idx_row_ref[rnd : rnd + 1, :] = index[:1].astype(jnp.int32)

    def relative():
        count = buckets_ref.shape[1]
        pad[...] = jnp.full((16, 128), 127.0, F32)
        for i in range(8):
            width = min(128, count - 128 * i)
            pad[i : i + 1, :width] = buckets_ref[:, 128 * i : 128 * i + width].astype(F32)
        turned = dotf(pad[:8].astype(BF), mark(steps(128, 128) + lanes(128, 128) == 127))
        for i in range(8):
            source = 6 - i if i < 7 else 7
            bucket_ref[:, 128 * i : 128 * (i + 1)] = turned[source : source + 1].astype(jnp.int32)
        pad[...] = jnp.zeros((16, 128), F32)
        pad[: table_ref.shape[0], : table_ref.shape[1]] = table_ref[...]
        rel_ref[...] = lax.dot_general(
            pad[...], (steps(128, 1024) == bucket_ref[...]).astype(F32), NN,
            precision=HIGHEST, preferred_element_type=F32,
        )

    def sequence_weights():
        count = sizes_ref.shape[1]
        seqs = ntok // LEN
        pad[...] = jnp.zeros((16, 128), F32)
        pad[:1, :count] = sizes_ref[...].astype(F32)
        sizes = pad[:8]
        ends = dotf(sizes.astype(BF), mark(steps(128, 128) <= lanes(128, 128)))
        for i in range(seqs):
            seq = ((core * CHIPS + chip) * seqs + i).astype(F32)
            inside = jnp.logical_and(ends - sizes <= seq, seq < ends)
            size = jnp.sum(jnp.where(inside, sizes, 0.0)[:1], axis=1, keepdims=True)
            weight = jnp.float32(seqs * 2 * CHIPS) / (jnp.float32(count) * size)
            weight_ref[i : i + 1, :] = jnp.broadcast_to(weight, (1, model))

    def pack(mbuf):
        load = pltpu.make_async_copy(master_hbm.at[:, own_cols], mbuf, load_sem.at[1])
        load.start()
        pack_index()
        load.wait()
        own_half = mbuf[...].astype(BF)
        index = as_column(index_ref[:1, :])
        for part in range(4):
            rows = PACK_ROWS // 4
            onehot = (
                lax.broadcasted_iota(jnp.int32, (rows, mbuf.shape[0]), 1)
                == index[part * rows : (part + 1) * rows, :]
            ).astype(F32).astype(BF)
            packed = dotf(onehot, own_half).astype(BF)
            for til in range(3):
                sendbuf[til, part * rows : (part + 1) * rows, :] = packed[:, til * TILE : (til + 1) * TILE]

    pl.run_scoped(pack, pltpu.VMEM((master_hbm.shape[0], HALF), F32))
    pl.semaphore_wait(barrier, CHIPS)

    def fa_copy(rnd, step):
        dest = lax.rem(chip + step, CHIPS)
        rng, til = unit_place(rnd * CHIPS + dest)
        return remote(
            sendbuf.at[til, piece_rows(rng), :], recvbuf.at[rnd, piece_rows(chip), :],
            fa_send.at[rnd], fa_recv.at[rnd], (core, dest),
        )

    def fa_start(rnd):
        for step in range(1, CHIPS):
            fa_copy(rnd, step).start()
        rng, til = unit_place(rnd * CHIPS + chip)
        recvbuf[rnd, piece_rows(chip), :] = sendbuf[til, piece_rows(rng), :]

    def own_unit(rnd):
        pieces_copy(fa_send.at[rnd], fa_recv.at[rnd]).wait_recv()
        v = rnd * CHIPS + chip
        index = as_column(idx_row_ref[rnd : rnd + 1, :])
        for part in range(2):
            rows = RANGE_ROWS // 2
            onehot = (
                lax.broadcasted_iota(jnp.int32, (rows, PACK_ROWS), 1)
                == index[part * rows : (part + 1) * rows, :]
            ).astype(F32).astype(BF)
            weights[half_slice(v, core, part)] = dotf(onehot, recvbuf[rnd]).astype(BF)

    def nearest(k):
        return (zpos, zpos + 1 - 2 * (zpos % 2), 2 - zpos // 2, 3 - 3 * (zpos // 2))[k]

    def behind(p):
        return nearest(p % 4) if p < 8 else p % 4

    def fwd_unit(p, column):
        return p // 4 * CHIPS + behind(p) * 4 + column

    def fz_copy(rnd, source, up):
        at = unit_slice(rnd * CHIPS + source * 4 + col, core)
        dest = chip + (4 if up else -4)
        return remote(weights.at[at], weights.at[at], fz_send.at[rnd], fz_recv.at[rnd, source], (core, dest))

    def fz_start(rnd):
        @pl.when(zpos < 3)
        def _():
            fz_copy(rnd, zpos, True).start()

        @pl.when(zpos > 0)
        def _():
            fz_copy(rnd, zpos, False).start()

    def fz_relay(rnd, k):
        source = nearest(k)
        units_copy(1, fz_send.at[rnd], fz_recv.at[rnd, source]).wait_recv()

        @pl.when(jnp.logical_and(source < zpos, zpos < 3))
        def _():
            fz_copy(rnd, source, True).start()

        @pl.when(jnp.logical_and(source > zpos, zpos > 0))
        def _():
            fz_copy(rnd, source, False).start()

    def fz_sent(rnd):
        inner = zpos % 3 > 0

        @pl.when(inner)
        def _():
            units_copy(5, fz_send.at[rnd], fz_recv.at[rnd, 0]).wait_send()

        @pl.when(jnp.logical_not(inner))
        def _():
            units_copy(1, fz_send.at[rnd], fz_recv.at[rnd, 0]).wait_send()

    def fx_copy(p):
        at = unit_slice(fwd_unit(p, col), core)
        return remote(weights.at[at], weights.at[at], f_send.at[p], fx_recv.at[p], (core, xnbr))

    def fy_copy(p):
        at = unit_slice(fwd_unit(p, col), core)
        return remote(weights.at[at], weights.at[at], f_send.at[p], fy_recv.at[p], (core, ynbr))

    def fda_copy(p):
        at = half_slice(fwd_unit(p, xcol), core, 0)
        return remote(weights.at[at], weights.at[at], f_send.at[p], fda_recv.at[p], (core, ynbr))

    def fdb_copy(p):
        at = half_slice(fwd_unit(p, ycol), core, 1)
        return remote(weights.at[at], weights.at[at], f_send.at[p], fdb_recv.at[p], (core, xnbr))

    def fs_copy(p, kind):
        at = unit_slice(fwd_unit(p, (col, xcol, ycol, dcol)[kind]), core)
        return remote(weights.at[at], weights.at[at], f_send.at[p], fs_recv.at[p], (other, chip))

    def fwd_a(p):
        if p < 8 and p % 4:
            fz_relay(p // 4, p % 4)
        fx_copy(p).start()
        fy_copy(p).start()
        fs_copy(p, 0).start()

    def fwd_b(p):
        fx_copy(p).wait_recv()
        fda_copy(p).start()
        fs_copy(p, 1).start()
        fy_copy(p).wait_recv()
        fdb_copy(p).start()
        fs_copy(p, 2).start()

    def fwd_c(p):
        fda_copy(p).wait_recv()
        fdb_copy(p).wait_recv()
        fs_copy(p, 3).start()

    def fwd_done(*pairs):
        for p in pairs:
            units_copy(4, f_send.at[p], fs_recv.at[p]).wait_recv()

    def fwd_sent(rounds, pairs):
        for rnd in rounds:
            pieces_copy(fa_send.at[rnd], fa_recv.at[rnd]).wait_send()
            fz_sent(rnd)
        for p in pairs:
            units_copy(7, f_send.at[p], fs_recv.at[p]).wait_send()

    lane_head = lax.broadcasted_iota(jnp.int32, (LEN, 128), 1) // HEAD_DIM

    def forward(base, s_scr, p_scr):
        fa_start(0)
        unit_index()
        relative()
        sequence_weights()
        load_tokens.wait()
        for part in range(ntok // 128):
            rows = slice(part * 128, (part + 1) * 128)
            values = tokens[rows, :].astype(F32)
            inv_rms = lax.rsqrt(jnp.mean(values * values, axis=-1, keepdims=True) + EPS_NORM)
            hidden[rows, :] = (values * inv_rms * gains_ref[0:1, :]).astype(BF)

        def bands(h, _):
            wide = jnp.broadcast_to(rel_ref[pl.ds(h, 1), :], (128, 1024))
            base[pl.ds(h, 1)] = pltpu.roll(wide, 0, 1, stride=1, stride_axis=0)[:, :896][None]
            return 0

        lax.fori_loop(0, HEADS, bands, 0)
        own_unit(0)
        fz_start(0)
        fwd_a(0)
        fwd_a(1)
        fwd_b(0)
        fwd_a(2)
        fwd_b(1)
        fwd_c(0)
        fwd_a(3)
        fa_start(1)
        fwd_b(2)
        fwd_c(1)
        fwd_done(0, 1)

        def third_of(step):
            nearer = jnp.minimum(zpos, 2)
            middle = 1 - zpos % 2 * (1 - zpos // 2)
            turn = step // 4
            return jnp.where(turn == 0, nearer, jnp.where(turn == 1, middle, 3 - nearer - middle))

        def projections(step):
            third = third_of(step)
            near = pl.ds(pl.multiple_of(third * TILE, TILE), TILE)
            far = pl.ds(pl.multiple_of(HALF + third * TILE, TILE), TILE)
            for mat, out_ref in enumerate((q_ref, k_ref, v_ref)):
                mat_rows = slice(mat * model, (mat + 1) * model)
                both = jnp.concatenate([weights[mat_rows, near], weights[mat_rows, far]], axis=1)
                value = dotf(hidden[...], both).astype(BF)
                out_ref[:, near] = value[:, :TILE]
                out_ref[:, far] = value[:, TILE:]

        row_id = lax.broadcasted_iota(jnp.int32, (128, LEN), 0)

        def seq_pair(step):
            return step % 2, third_of(step) + 3 * (step // 2 % 2)

        def p_copy(step, head):
            seq, pair = seq_pair(step)
            return pltpu.make_async_copy(
                p_scr.at[step % 2, head], p_hbm.at[seq * HEADS + pair * 2 + head], p_sem.at[step % 2, head]
            )

        def attend(step):
            seq, pair = seq_pair(step)
            rows = pl.ds(pl.multiple_of(seq * LEN, LEN), LEN)
            lanes = pl.ds(pl.multiple_of(pair * 128, 128), 128)
            length = len_ref[seq]

            @pl.when(step >= 2)
            def _():
                for head in range(2):
                    p_copy(step - 2, head).wait()

            q_two = q_ref[rows, lanes]
            k_two = k_ref[rows, lanes]
            v_two = v_ref[rows, lanes].T
            outs = []
            for head in range(2):
                k_one = jnp.where(lane_head == head, k_two, jnp.zeros_like(k_two))
                top = jnp.full((8, LEN), NEG_FILL, F32)
                for blk in range(4):
                    score = dotf(k_one[blk * 128 : (blk + 1) * 128], q_two, NT)
                    score = score + base[pair * 2 + head, :, 384 - 128 * blk : 896 - 128 * blk]
                    score = jnp.where(row_id + blk * 128 < length, score, NEG_FILL)
                    s_scr[head, blk * 128 : (blk + 1) * 128, :] = score
                    top = jnp.maximum(top, jnp.max(score.reshape(16, 8, LEN), axis=0))
                top = jnp.max(top, axis=0, keepdims=True)
                total = jnp.zeros((8, LEN), F32)
                for blk in range(4):
                    part = jnp.exp(s_scr[head, blk * 128 : (blk + 1) * 128, :] - top)
                    s_scr[head, blk * 128 : (blk + 1) * 128, :] = part
                    total = total + jnp.sum(part.reshape(16, 8, LEN), axis=0)
                inverse = 1.0 / jnp.sum(total, axis=0, keepdims=True)
                for blk in range(4):
                    p_scr[step % 2, head, blk * 128 : (blk + 1) * 128, :] = (
                        s_scr[head, blk * 128 : (blk + 1) * 128, :] * inverse
                    ).astype(BF)
                outs.append(dotf(v_two[head * HEAD_DIM : (head + 1) * HEAD_DIM], p_scr[step % 2, head]))
                p_copy(step, head).start()
            ctx_ref[rows, lanes] = jnp.concatenate(outs, axis=0).T.astype(BF)

        plan = {
            0: (lambda: own_unit(1), lambda: fz_start(1), lambda: fwd_a(4), lambda: fa_start(2), lambda: fwd_c(2)),
            1: (lambda: fwd_b(3),),
            3: (lambda: fwd_c(3), lambda: fwd_a(5), lambda: fwd_done(2)),
            4: (lambda: own_unit(2), lambda: fz_start(2), lambda: fwd_b(4)),
            5: (lambda: fwd_a(6),),
            6: (lambda: fwd_c(4), lambda: fwd_b(5)),
            7: (lambda: fwd_a(7), lambda: fwd_done(3)),
            8: (lambda: fz_relay(2, 1), lambda: fwd_c(5), lambda: fwd_b(6)),
            9: (lambda: fwd_b(7),),
            10: (lambda: fz_relay(2, 2), lambda: fwd_c(6)),
            11: (lambda: fz_relay(2, 3), lambda: fwd_a(8), lambda: fwd_c(7)),
        }

        def attend_step(step, _):
            @pl.when(step % 4 == 0)
            def _():
                projections(step)

            attend(step)
            for at, todo in plan.items():
                @pl.when(step == at)
                def _():
                    for act in todo:
                        act()
            return 0

        lax.fori_loop(0, 12, attend_step, 0)
        for step in (10, 11):
            for head in range(2):
                p_copy(step, head).wait()

    pl.run_scoped(
        forward,
        pltpu.VMEM((HEADS, 128, 896), F32),
        pltpu.VMEM((2, LEN, LEN), F32),
        pltpu.VMEM((2, 2, LEN, LEN), BF),
    )

    def src_of(p, gq):
        return gq if p < 3 else weights

    def unit(p, column):
        return p * 4 + column

    def sib_copy(p, column, gq=None):
        v = unit(p, column)
        return remote(
            src_of(p, gq).at[unit_slice(v, other)], sib.at[unit_slice(v, 0)],
            r_send.at[p], h_recv.at[p], (other, chip),
        )

    def da_copy(p, gq=None):
        at = half_slice(unit(p, dcol), core, 0)
        return remote(src_of(p, gq).at[at], dain.at[p], r_send.at[p], da_recv.at[p], (core, ynbr))

    def db_copy(p, gq=None):
        at = half_slice(unit(p, dcol), core, 1)
        return remote(src_of(p, gq).at[at], dbin.at[p], r_send.at[p], db_recv.at[p], (core, xnbr))

    def x_copy(p, gq=None):
        at = unit_slice(unit(p, xcol), core)
        return remote(src_of(p, gq).at[at], xin.at[p], r_send.at[p], x_recv.at[p], (core, xnbr))

    def y_copy(p, gq=None):
        at = unit_slice(unit(p, ycol), core)
        return remote(src_of(p, gq).at[at], yin.at[p], r_send.at[p], y_recv.at[p], (core, ynbr))

    def z_copy(p, gq=None):
        rnd, zt = p // 4, p % 4
        at = unit_slice(unit(p, col), core)
        return remote(
            src_of(p, gq).at[at], zin.at[rnd, zpos], z_send.at[rnd], z_recv.at[rnd, zpos], (core, zt * 4 + col)
        )

    def z_arrived(rnd, src):
        return remote(zin.at[rnd, src], zin.at[rnd, src], z_send.at[rnd], z_recv.at[rnd, src], (core, xnbr))

    def add(ref, at, incoming):
        ref[at] = (ref[at].astype(F32) + incoming.astype(F32)).astype(BF)

    def red_s(p, gq=None):
        for column in range(4):
            sib_copy(p, column, gq).start()

    def red_0(p, gq=None):
        units_copy(4, r_send.at[p], h_recv.at[p]).wait_recv()
        for column in range(4):
            add(src_of(p, gq), unit_slice(unit(p, column), core), sib[unit_slice(unit(p, column), 0)])
        da_copy(p, gq).start()
        db_copy(p, gq).start()

    def red_1(p, gq=None):
        da_copy(p, gq).wait_recv()
        add(src_of(p, gq), half_slice(unit(p, xcol), core, 0), dain[p])
        x_copy(p, gq).start()
        db_copy(p, gq).wait_recv()
        add(src_of(p, gq), half_slice(unit(p, ycol), core, 1), dbin[p])
        y_copy(p, gq).start()

    def red_2(p, gq=None):
        x_copy(p, gq).wait_recv()
        y_copy(p, gq).wait_recv()
        at = unit_slice(unit(p, col), core)
        total = (src_of(p, gq)[at].astype(F32) + xin[p].astype(F32) + yin[p].astype(F32)).astype(BF)

        @pl.when(zpos == p % 4)
        def _():
            ubuf[p // 4] = total

        @pl.when(zpos != p % 4)
        def _():
            src_of(p, gq)[at] = total
            z_copy(p, gq).start()

    def a2a_copy(rnd, step):
        dest = lax.rem(chip + step, CHIPS)
        rng, til = unit_place(rnd * CHIPS + chip)
        return remote(
            recvbuf.at[rnd, piece_rows(dest), :],
            slot_ref.at[piece_rows(rng), pl.ds(pl.multiple_of(core * HALF + til * TILE, TILE), TILE)],
            a2a_send.at[rnd], a2a_recv.at[rnd], (core, dest),
        )

    def keep_copy(rnd):
        rng, til = unit_place(rnd * CHIPS + chip)
        return pltpu.make_async_copy(
            recvbuf.at[rnd, piece_rows(chip), :],
            slot_ref.at[piece_rows(rng), pl.ds(pl.multiple_of(core * HALF + til * TILE, TILE), TILE)],
            load_sem.at[rnd],
        )

    def red_3(rnd):
        total = ubuf[rnd].astype(F32)
        for off in (1, 2, 3):
            src = lax.rem(zpos + off, 4)
            z_arrived(rnd, src).wait_recv()
            total = total + zin[rnd, src].astype(F32)
        total = total.astype(BF)
        for part in range(4):
            rows = PACK_ROWS // 4
            onehot = (
                lax.broadcasted_iota(jnp.int32, (rows, RANGE_ROWS), 0) + part * rows
                == idx_row_ref[rnd : rnd + 1, :]
            ).astype(F32).astype(BF)
            recvbuf[rnd, part * rows : (part + 1) * rows, :] = dotf(onehot, total).astype(BF)
        for step in range(1, CHIPS):
            a2a_copy(rnd, step).start()
        keep_copy(rnd).start()

    def red_sent(pairs):
        for p in pairs:
            units_copy(7, r_send.at[p], h_recv.at[p]).wait_send()

    def red_3_at(plane):
        @pl.when(zpos == plane)
        def _():
            red_3(0)

    def out_copy(i):
        rows = pl.ds(pl.multiple_of(i * tile, tile), tile)
        return pltpu.make_async_copy(hidden.at[rows], out_hbm.at[rows], out_sem.at[i])

    def feed(cot, down, out_acc, u_acc, act_s, pb_s):
        load_cot = pltpu.make_async_copy(cot_hbm, cot, load_sem.at[2])
        load_cot.start()
        load_cot.wait()
        fwd_a(9)
        fwd_done(4, 5, 6, 7)

        def head(i, _):
            rows = pl.ds(pl.multiple_of(i * tile, tile), tile)
            value = tokens[rows, :].astype(F32) + dotf(ctx_ref[rows, :], weights[3 * model : 4 * model, :])
            rb_ref[rows, :] = value
            inv_rms = lax.rsqrt(jnp.mean(value * value, axis=-1, keepdims=True) + EPS_NORM)
            hidden[rows, :] = (value * inv_rms * gains_ref[1:2, :]).astype(BF)
            down[rows, :] = (cot[rows, :].astype(F32) * weight_ref[pl.ds(i * tile // LEN, 1), :]).astype(BF)
            out_acc[rows, :] = jnp.zeros((tile, model), F32)
            u_acc[rows, :] = jnp.zeros((tile, model), F32)
            return 0

        lax.fori_loop(0, ntile, head, 0)
        fwd_a(10)
        fwd_b(8)

        middle = {
            0: (lambda: fwd_a(11), lambda: fwd_b(9), lambda: fwd_c(8), lambda: fwd_sent((0, 1), range(8))),
            1: (lambda: fwd_b(11), lambda: fwd_c(9), lambda: fwd_c(10), lambda: fwd_sent((2,), (8,))),
            2: (lambda: fwd_c(11),),
            3: (lambda: red_0(6), lambda: fwd_sent((), (9, 10))),
            4: (lambda: red_1(6), lambda: red_0(8), lambda: fwd_sent((), (11,))),
            5: (lambda: red_2(6), lambda: red_0(9), lambda: red_1(8)),
        }
        plan = {
            0: (lambda: fwd_done(8), lambda: fwd_b(10)),
            2: (lambda: red_s(6), lambda: red_s(7), lambda: fwd_done(9, 10)),
            3: (lambda: red_s(8), lambda: red_0(7), lambda: fwd_done(11)),
            4: (lambda: red_s(9), lambda: red_1(7)),
            5: (lambda: red_s(5), lambda: red_s(10), lambda: red_s(11), lambda: red_2(7)),
        }

        def run(what, now):
            for at, todo in what.items():
                @pl.when(now == at)
                def _():
                    for act in todo:
                        act()

        def chunk(c, _):
            rows_in = pl.ds(pl.multiple_of(first_in + c * FF_CHUNK, FF_CHUNK), FF_CHUNK)
            rows_down = pl.ds(pl.multiple_of(first_down + c * FF_CHUNK, FF_CHUNK), FF_CHUNK)
            for i in range(ntile):
                rows = slice(i * tile, (i + 1) * tile)
                pre = dotf(hidden[rows, :], weights[rows_in, :], NT)
                back = dotf(down[rows, :], weights[rows_down, :], NT)
                act, slope = gelu_pair(pre)
                act = act.astype(BF)
                pre_back = (back * slope).astype(BF)
                act_s[rows, :] = act
                pb_s[rows, :] = pre_back
                out_acc[rows, :] += dotf(act, weights[rows_down, :])
                u_acc[rows, :] += dotf(pre_back, weights[rows_in, :])
            run(middle, c)
            weights[rows_down, :] = dotf(act_s[...], down[...], TN).astype(BF)
            weights[rows_in, :] = dotf(pb_s[...], hidden[...], TN).astype(BF)
            run(plan, c)
            return 0

        lax.fori_loop(0, nchunk, chunk, 0)

        tail_plan = {
            0: (lambda: red_0(5),),
            1: (lambda: red_1(9),),
            2: (lambda: red_0(10),),
            3: (lambda: red_2(8),),
        }
        gacc[1] = jnp.zeros((8, model), F32)

        def tail(i, _):
            rows = pl.ds(pl.multiple_of(i * tile, tile), tile)
            value = rb_ref[rows, :]
            out = (value + out_acc[rows, :]).astype(BF)
            inv_rms = lax.rsqrt(jnp.mean(value * value, axis=-1, keepdims=True) + EPS_NORM)
            u = u_acc[rows, :]
            gu = u * gains_ref[1:2, :]
            normal = value * inv_rms
            mean = jnp.mean(gu * normal, axis=-1, keepdims=True)
            back = cot[rows, :].astype(F32) * weight_ref[pl.ds(i * tile // LEN, 1), :] + inv_rms * (gu - normal * mean)
            rb_ref[rows, :] = back
            low = back.astype(BF)
            down[rows, :] = low
            hidden[rows, :] = out
            out_copy(i).start()
            cb_ref[rows, :] = dotf(low, weights[3 * model : 4 * model, :], NT).astype(BF)
            gacc[1] += jnp.sum((u * normal).reshape(tile // 8, 8, model), axis=0)
            run(tail_plan, i)
            return 0

        lax.fori_loop(0, ntile, tail, 0)
        weights[3 * model : 4 * model, :] = dotf(ctx_ref[...], down[...], TN).astype(BF)
        red_s(4)
        red_s(3)
        red_1(5)
        for i in range(ntile):
            out_copy(i).wait()

    pl.run_scoped(
        feed,
        pltpu.VMEM((ntok, model), BF),
        pltpu.VMEM((ntok, model), BF),
        pltpu.VMEM((ntok, model), F32),
        pltpu.VMEM((ntok, model), F32),
        pltpu.VMEM((ntok, FF_CHUNK), BF),
        pltpu.VMEM((ntok, FF_CHUNK), BF),
    )

    def backward(gq, hid_t, diag, drow, p_scr, ds_scr):
        def split(step):
            turn = step // 2
            return step % 2, turn // 2 + 3 * (turn % 2)

        def p_copy(step, head):
            seq, pair = split(step)
            return pltpu.make_async_copy(
                p_hbm.at[seq * HEADS + pair * 2 + head], p_scr.at[step % 2, head], p_sem.at[step % 2, head]
            )

        for head in range(2):
            p_copy(0, head).start()
        diag[...] = jnp.zeros_like(diag)
        for part in range(ntok // 128):
            rows = slice(part * 128, (part + 1) * 128)
            values = tokens[rows, :].astype(F32)
            inv_rms = lax.rsqrt(jnp.mean(values * values, axis=-1, keepdims=True) + EPS_NORM)
            hid_t[:, rows] = (values * inv_rms * gains_ref[0:1, :]).astype(BF).T

        def attend_back(step):
            seq, pair = split(step)
            rows = pl.ds(pl.multiple_of(seq * LEN, LEN), LEN)
            lanes = pl.ds(pl.multiple_of(pair * 128, 128), 128)

            @pl.when(step + 1 < 12)
            def _():
                for head in range(2):
                    p_copy(step + 1, head).start()

            q_two, k_two, v_two, do_two = (
                q_ref[rows, lanes], k_ref[rows, lanes], v_ref[rows, lanes], cb_ref[rows, lanes]
            )
            k_turn = k_two.T
            inner = (do_two.astype(F32) * ctx_ref[rows, lanes].astype(F32)).T
            dv_parts, dk_parts, dq_parts = [], [], []
            for head in range(2):
                p_copy(step, head).wait()
                delta = jnp.sum(inner[head * HEAD_DIM : (head + 1) * HEAD_DIM], axis=0, keepdims=True)
                v_one = jnp.where(lane_head == head, v_two, jnp.zeros_like(v_two))
                for blk in range(4):
                    sub = slice(blk * 128, (blk + 1) * 128)
                    prob_back = dotf(v_one[sub], do_two, NT)
                    score = p_scr[step % 2, head, sub, :].astype(F32) * (prob_back - delta)
                    diag[pair * 2 + head, :, 384 - 128 * blk : 896 - 128 * blk] += score
                    ds_scr[head, sub, :] = score.astype(BF)
                dv_parts.append(dotf(p_scr[step % 2, head], do_two))
                dk_parts.append(dotf(ds_scr[head], q_two))
                dq_parts.append(dotf(k_turn[head * HEAD_DIM : (head + 1) * HEAD_DIM], ds_scr[head]))
            v_ref[rows, lanes] = jnp.where(lane_head == 0, dv_parts[0], dv_parts[1]).astype(BF)
            k_ref[rows, lanes] = jnp.where(lane_head == 0, dk_parts[0], dk_parts[1]).astype(BF)
            q_ref[rows, lanes] = jnp.concatenate(dq_parts, axis=0).T.astype(BF)

        def project(third):
            near = slice(third * TILE, (third + 1) * TILE)
            far = slice(HALF + third * TILE, HALF + (third + 1) * TILE)
            for mat, grad in enumerate((q_ref, k_ref, v_ref)):
                mat_rows = slice(mat * model, (mat + 1) * model)
                both = jnp.concatenate([grad[:, near], grad[:, far]], axis=1)
                value = dotf(hid_t[...], both).astype(BF)
                gq[mat_rows, near] = value[:, :TILE]
                gq[mat_rows, far] = value[:, TILE:]

        plan = {
            0: (lambda: red_0(11), lambda: red_2(9)),
            1: (lambda: red_1(10),),
            2: (lambda: red_0(4), lambda: red_2(5)),
            3: (lambda: project(0), lambda: red_s(0, gq), lambda: red_1(11), lambda: red_0(3)),
            4: (lambda: red_2(10),),
            5: (lambda: red_1(4), lambda: red_0(0, gq)),
            6: (lambda: red_2(11), lambda: red_1(3)),
            7: (lambda: project(1), lambda: red_s(1, gq), lambda: red_2(4)),
            8: (lambda: red_3(2), lambda: red_1(0, gq)),
            9: (lambda: red_0(1, gq), lambda: red_2(3)),
            11: (lambda: project(2), lambda: red_s(2, gq), lambda: red_1(1, gq), lambda: red_2(0, gq)),
        }

        def back_step(step, _):
            attend_back(step)
            for at, todo in plan.items():
                @pl.when(step == at)
                def _():
                    for act in todo:
                        act()
            return 0

        lax.fori_loop(0, 12, back_step, 0)

        gacc[0] = jnp.zeros((8, model), F32)

        def gin_copy(i):
            rows = slice(i * tile, (i + 1) * tile)
            return pltpu.make_async_copy(rb_ref.at[rows], gin_hbm.at[rows], out_sem.at[i])

        def tail(i):
            rows = slice(i * tile, (i + 1) * tile)
            u = (
                dotf(q_ref[rows, :], weights[:model, :], NT)
                + dotf(k_ref[rows, :], weights[model : 2 * model, :], NT)
                + dotf(v_ref[rows, :], weights[2 * model : 3 * model, :], NT)
            )
            value = tokens[rows, :].astype(F32)
            inv_rms = lax.rsqrt(jnp.mean(value * value, axis=-1, keepdims=True) + EPS_NORM)
            gu = u * gains_ref[0:1, :]
            normal = value * inv_rms
            mean = jnp.mean(gu * normal, axis=-1, keepdims=True)
            rb_ref[rows, :] += inv_rms * (gu - normal * mean)
            gin_copy(i).start()
            gacc[0] += jnp.sum((u * normal).reshape(tile // 8, 8, model), axis=0)

        def unskew(g, _):
            accs = [
                jnp.concatenate([diag[g * 4 + h], jnp.zeros((128, 128), F32)], axis=1) for h in range(4)
            ]
            size = 64
            while size >= 1:
                accs = [acc[:size] + pltpu.roll(acc[size:], 1024 - size, 1) for acc in accs]
                size //= 2
            for h in range(4):
                drow[pl.ds(g * 4 + h, 1), :] = accs[h]
            return 0

        drow[...] = jnp.zeros_like(drow)
        lax.fori_loop(0, HEADS // 4, unskew, 0)
        onehot = (lax.broadcasted_iota(jnp.int32, (128, 1024), 0) == bucket_ref[...]).astype(F32)
        table = lax.dot_general(drow[...], onehot, NT, precision=HIGHEST, preferred_element_type=F32)
        small[0, :, :model] = jnp.zeros((16, model), F32)
        small[0, 1:2, :model] = jnp.sum(gacc[1], axis=0, keepdims=True)
        small[0, :, model:] = table
        red_0(2, gq)
        red_3(1)
        red_3_at(3)
        tail(0)
        red_2(1, gq)
        red_1(2, gq)
        tail(1)
        tail(2)
        red_2(2, gq)
        red_3_at(0)
        tail(3)
        small[0, 0:1, :model] = jnp.sum(gacc[0], axis=0, keepdims=True)
        sm_copy(0).start()
        red_3_at(2)
        red_3_at(1)
        sm_next(0)
        sm_copy(1).start()
        sm_next(1)
        sm_copy(2).start()
        for i in range(ntile):
            gin_copy(i).wait()
        red_sent(range(4))
        units_copy(3, z_send.at[0], z_recv.at[0, 0]).wait_send()

    def sm_copy(step):
        device = ((other, chip), (core, xnbr), (core, ynbr))[step]
        return remote(small.at[2 * step], small.at[2 * step + 1], sm_send.at[step], sm_recv.at[step], device)

    def sm_plane(off):
        return remote(
            small.at[6], small.at[7 + zpos], sm_send.at[2 + off], sm_recv.at[2 + off],
            (core, lax.rem(zpos + off, 4) * 4 + col),
        )

    def sm_next(step):
        sm_copy(step).wait_recv()
        small[2 * step + 2] = small[2 * step] + small[2 * step + 1]

    pl.run_scoped(
        backward,
        pltpu.VMEM((3 * model, model), BF),
        pltpu.VMEM((model, ntok), BF),
        pltpu.VMEM((HEADS, 128, 896), F32),
        pltpu.VMEM((16, 1024), F32),
        pltpu.VMEM((2, 2, LEN, LEN), BF),
        pltpu.VMEM((2, LEN, LEN), BF),
    )

    early = 6 * PAIR_ROWS

    def half_copy(part):
        at = (slice(0, early), slice(early, PACK_ROWS))[part]
        return remote(
            slot_ref.at[at, own_cols], slot_ref.at[at, own_cols], half_send.at[part], half_recv.at[part],
            (other, chip),
        )

    sm_next(2)
    for off in (1, 2, 3):
        sm_plane(off).start()
    small[7 + zpos] = small[6]
    for rnd in (2, 1):
        keep_copy(rnd).wait()
        pieces_copy(a2a_send.at[rnd], a2a_recv.at[rnd]).wait_recv()
    half_copy(1).start()
    keep_copy(0).wait()
    pieces_copy(a2a_send.at[0], a2a_recv.at[0]).wait_recv()
    half_copy(0).start()
    for off in (1, 2, 3):
        sm_plane(off).wait_recv()
    small_ref[...] = small[7] + small[8] + small[9] + small[10]
    for step in range(3):
        sm_copy(step).wait_send()
    for off in (1, 2, 3):
        sm_plane(off).wait_send()
    red_sent(range(4, 4 * ROUNDS))
    for rnd in range(ROUNDS):
        pieces_copy(a2a_send.at[rnd], a2a_recv.at[rnd]).wait_send()
        if rnd:
            units_copy(3, z_send.at[rnd], z_recv.at[rnd, 0]).wait_send()
    half_copy(1).wait()
    half_copy(0).wait()


def layer_pass(owners, gains, table, buckets, sizes, lens, master, tokens, cot):
    ntok, model = tokens.shape
    rows = 8 * master.shape[0]
    dma = pltpu.SemaphoreType.DMA
    half = RANGE_ROWS // 2
    pairs = 4 * ROUNDS
    act = pltpu.VMEM((ntok, model), BF)
    return pl.pallas_call(
        layer_kernel,
        name="layer_pass",
        out_shape=(
            jax.ShapeDtypeStruct((ntok, model), BF),
            jax.ShapeDtypeStruct((ntok, model), F32),
            jax.ShapeDtypeStruct((2 * HEADS, LEN, LEN), BF),
            jax.ShapeDtypeStruct((PACK_ROWS, model), BF),
            jax.ShapeDtypeStruct((16, model + 128), F32),
            jax.ShapeDtypeStruct((8, PACK_ROWS), jnp.int32),
            jax.ShapeDtypeStruct((7 * RANGE_ROWS, TILE), BF),
        ),
        in_specs=[VM] * 5 + [SM] + [ANY] * 3,
        out_specs=(ANY, ANY, ANY, ANY, VM, VM, ANY),
        scratch_shapes=[
            pltpu.VMEM((rows, model), BF),
            pltpu.VMEM((rows, HALF), BF),
            pltpu.VMEM((pairs, RANGE_ROWS, TILE), BF),
            pltpu.VMEM((pairs, RANGE_ROWS, TILE), BF),
            pltpu.VMEM((pairs, half, TILE), BF),
            pltpu.VMEM((pairs, half, TILE), BF),
            pltpu.VMEM((ROUNDS, 4, RANGE_ROWS, TILE), BF),
            pltpu.VMEM((ROUNDS, RANGE_ROWS, TILE), BF),
            pltpu.VMEM((3, PACK_ROWS, TILE), BF),
            pltpu.VMEM((ROUNDS, PACK_ROWS, TILE), BF),
            act, act, act, act, act, act, act,
            pltpu.VMEM((ntok, model), F32),
            pltpu.VMEM((11, 16, model + 128), F32),
            pltpu.VMEM((2, 8, model), F32),
            pltpu.VMEM((ROUNDS, RANGE_ROWS), jnp.int32),
            pltpu.VMEM((16, 1024), F32),
            pltpu.VMEM((1, 1024), jnp.int32),
            pltpu.VMEM((8, model), F32),
            pltpu.VMEM((16, 128), F32),
            dma((3,)), dma((4,)), dma((2, 2)),
            dma((ROUNDS,)), dma((ROUNDS,)), dma((ROUNDS,)), dma((ROUNDS, 4)), dma((pairs,)),
            dma((pairs,)), dma((pairs,)), dma((pairs,)), dma((pairs,)), dma((pairs,)),
            dma((pairs,)), dma((pairs,)), dma((pairs,)), dma((pairs,)), dma((pairs,)), dma((pairs,)),
            dma((ROUNDS,)), dma((ROUNDS, 4)), dma((ROUNDS,)), dma((ROUNDS,)), dma((2,)), dma((2,)),
            dma((6,)), dma((6,)),
        ],
        compiler_params=pltpu.CompilerParams(
            collective_id=0, has_side_effects=True, vmem_limit_bytes=62 * 2**20
        ),
    )(owners, gains, table, buckets, sizes, lens, master, tokens, cot)


BETA_ONE = 0.5
BETA_TWO = 0.75
LEARN_RATE = 0.06
SMALL_RATE = 0.4
WEIGHT_DECAY = 0.01
EPS_ADAM = 1e-08
OPT_STEP = 3


def adamw(weight, gradient, first_in, second, rate):
    first_out = BETA_ONE * first_in + (1.0 - BETA_ONE) * gradient
    second_out = BETA_TWO * second + (1.0 - BETA_TWO) * gradient * gradient
    fix_first = 1.0 - BETA_ONE**OPT_STEP
    fix_second = 1.0 - BETA_TWO**OPT_STEP
    update = first_out / fix_first / (jnp.sqrt(second_out / fix_second) + EPS_ADAM)
    return (first_out, second_out, weight - rate * (update + WEIGHT_DECAY * weight))


def adam_kernel(
    idx_ref, packed_ref, small_ref, gains_ref, gains_first_ref, gains_second_ref,
    table_ref, table_first_ref, table_second_ref, master_ref, first_ref, second_ref, out_ref, gin_ref,
    grad_ref, fnew_ref, snew_ref, mnew_ref, copy_ref, out_new_ref, gin_new_ref,
    ggrad_ref, gfnew_ref, gsnew_ref, gnew_ref, tgrad_ref, tfnew_ref, tsnew_ref, tnew_ref,
):
    rows, model = master_ref.shape
    onehot = (
        lax.broadcasted_iota(jnp.int32, (rows, PACK_ROWS), 0) + pl.program_id(0) * rows == idx_ref[:1, :]
    ).astype(F32).astype(BF)
    grad = dotf(onehot, packed_ref[...])
    first_new, second_new, master_new = adamw(
        master_ref[...], grad, first_ref[...], second_ref[...], LEARN_RATE
    )
    grad_ref[...] = grad
    fnew_ref[...] = first_new
    snew_ref[...] = second_new
    mnew_ref[...] = master_new
    copy_ref[...] = master_new.astype(BF)
    out_new_ref[...] = out_ref[...]
    gin_new_ref[...] = gin_ref[...]

    @pl.when(pl.program_id(0) == 0)
    def _():
        heads, buckets = table_ref.shape
        grad = small_ref[:2, :model]
        ggrad_ref[...] = grad
        gfnew_ref[...], gsnew_ref[...], gnew_ref[...] = adamw(
            gains_ref[...], grad, gains_first_ref[...], gains_second_ref[...], SMALL_RATE
        )
        grad = small_ref[:heads, model : model + buckets]
        tgrad_ref[...] = grad
        tfnew_ref[...], tsnew_ref[...], tnew_ref[...] = adamw(
            table_ref[...], grad, table_first_ref[...], table_second_ref[...], SMALL_RATE
        )


ADAM_STEPS = 2


def adam_pass(whole, master, first, second, out, gin):
    rows, model = master.shape
    ntok = out.shape[0]

    def part(total):
        return pl.BlockSpec((total // ADAM_STEPS, model), lambda i: (i, 0))

    def full(a):
        return pl.BlockSpec(a.shape, lambda i: (0, 0))

    def like(a):
        return jax.ShapeDtypeStruct(a.shape, a.dtype)

    wide = like(master)
    gains, table = whole[3], whole[6]
    return pl.pallas_call(
        adam_kernel,
        name="adam_pass",
        grid=(ADAM_STEPS,),
        out_shape=(wide, wide, wide, wide, jax.ShapeDtypeStruct((rows, model), BF), like(out), like(gin))
        + (like(gains),) * 4 + (like(table),) * 4,
        in_specs=[full(a) for a in whole] + [part(rows)] * 3 + [part(ntok)] * 2,
        out_specs=(part(rows),) * 5 + (part(ntok),) * 2 + (full(gains),) * 4 + (full(table),) * 4,
        compiler_params=pltpu.CompilerParams(vmem_limit_bytes=60 * 2**20),
    )(*whole, master, first, second, out, gin)


def fast_body(
    tokens, cotangent, master_slots, first_slots, second_slots, norm_gains, gains_first, gains_second,
    bias_table, table_first, table_second, bucket_ids, valid_len, task_sizes, owner_list,
):
    block_out, grad_input, _, packed, small, index, _ = layer_pass(
        owner_list[None, :], norm_gains, bias_table.T, bucket_ids[None, :], task_sizes[None, :], valid_len,
        master_slots, tokens, cotangent,
    )
    whole = (
        index, packed, small, norm_gains, gains_first, gains_second, bias_table.T, table_first.T, table_second.T
    )
    (
        grad_slots, first_new, second_new, master_new, master_copy, block_out, grad_input,
        grad_gains, gains_first_new, gains_second_new, gains_new,
        grad_table, table_first_new, table_second_new, table_new,
    ) = adam_pass(whole, master_slots, first_slots, second_slots, block_out, grad_input)
    return (
        block_out, grad_input, grad_slots, grad_gains, grad_table.T, first_new, second_new, master_new, master_copy,
        gains_first_new, gains_second_new, gains_new, table_first_new.T, table_second_new.T, table_new.T,
    )


def product(left_side, right_side):
    return jnp.dot(left_side, right_side, preferred_element_type=jnp.float32)


def contract_rows(left_side, right_side):
    return lax.dot_general(
        left_side, right_side, (((0,), (0,)), ((), ())), preferred_element_type=jnp.float32
    )


def contract_cols(left_side, right_side):
    return lax.dot_general(
        left_side, right_side, (((1,), (1,)), ((), ())), preferred_element_type=jnp.float32
    )


def smooth_act(values):
    return jax.nn.gelu(values, approximate=True)


def slot_layout(owner_list, devices, capacity):
    block_count = owner_list.shape[0]
    onehot = (owner_list[:, None] == jnp.arange(devices, dtype=jnp.int32)[None, :]).astype(
        jnp.int32
    )
    rank_in = jnp.sum((jnp.cumsum(onehot, axis=0) - onehot) * onehot, axis=1)
    slot_of = owner_list * capacity + rank_in
    source = (
        jnp.zeros((devices * capacity,), jnp.int32)
        .at[slot_of]
        .set(jnp.arange(block_count, dtype=jnp.int32))
    )
    filled = (
        jnp.zeros((devices * capacity,), jnp.int32)
        .at[slot_of]
        .set(jnp.ones((block_count,), jnp.int32))
    )
    return (slot_of, source, filled, rank_in)


def split_rows(all_rows):
    model_width = all_rows.shape[1]
    hidden = (all_rows.shape[0] - 4 * model_width) // 2
    return (
        all_rows[:model_width],
        all_rows[model_width : 2 * model_width],
        all_rows[2 * model_width : 3 * model_width],
        all_rows[3 * model_width : 4 * model_width],
        all_rows[4 * model_width : 4 * model_width + hidden],
        all_rows[4 * model_width + hidden :],
    )


def norm_raw(values, gain_row):
    inv_rms = lax.rsqrt(jnp.mean(values * values, axis=-1, keepdims=True) + EPS_NORM)
    return values * inv_rms * gain_row


def expand_bias(bias_table, bucket_ids):
    length = (bucket_ids.shape[0] + 1) // 2
    onehot = jax.nn.one_hot(bucket_ids, bias_table.shape[0], dtype=jnp.float32)
    rel_rows = jnp.dot(onehot, bias_table, precision=HIGHEST)
    reverse = rel_rows[::-1].T
    tiled_rows = jnp.tile(reverse, (1, length + 1))[:, : 2 * length * length]
    return tiled_rows.reshape(reverse.shape[0], length, 2 * length)[:, :, :length][:, :, ::-1]


def masked_scores(seq_query, seq_key, rel_bias, length):
    scores = (
        jnp.einsum("qhd,khd->hqk", seq_query, seq_key, preferred_element_type=jnp.float32)
        + rel_bias
    )
    live = jnp.arange(seq_key.shape[0], dtype=jnp.int32)[None, None, :] < length
    return jnp.where(live, scores, NEG_FILL)


def adamw_step(weight, gradient, first_in, second, step_value, rate):
    first_out = BETA_ONE * first_in + (1.0 - BETA_ONE) * gradient
    second_out = BETA_TWO * second + (1.0 - BETA_TWO) * gradient * gradient
    fix_first = 1.0 - jnp.power(jnp.float32(BETA_ONE), step_value)
    fix_second = 1.0 - jnp.power(jnp.float32(BETA_TWO), step_value)
    update = first_out / fix_first / (jnp.sqrt(second_out / fix_second) + EPS_ADAM)
    return (first_out, second_out, weight - rate * (update + WEIGHT_DECAY * weight))


def plain_body(
    tokens,
    cotangent,
    master_slots,
    first_slots,
    second_slots,
    norm_gains,
    gains_first,
    gains_second,
    bias_table,
    table_first,
    table_second,
    bucket_ids,
    valid_len,
    task_sizes,
    owner_list,
):
    devices = lax.axis_size("fsdp")
    replicas = lax.axis_size("dp")
    my_index = lax.axis_index("fsdp")
    capacity = master_slots.shape[0] // BROWS
    model_width = master_slots.shape[1]
    seq_dev = valid_len.shape[0]
    slot_of, source, filled, rank_in = slot_layout(owner_list, devices, capacity)
    sent_shard = master_slots.astype(jnp.bfloat16)

    def rebuild(gathered):
        blocks = gathered.reshape(devices * capacity, BROWS, model_width)[slot_of]
        return split_rows(blocks.reshape(-1, model_width))

    def by_seq(array_in):
        return array_in.reshape(seq_dev, LEN, HEADS, HEAD_DIM)

    def to_rows(array_in):
        return array_in.reshape(-1, model_width).astype(jnp.bfloat16)

    w_query, w_key, w_value, w_out, w_in, w_down = rebuild(
        lax.all_gather(sent_shard, "fsdp", axis=0, tiled=True)
    )
    rel_bias, bias_pull = jax.vjp(lambda table_in: expand_bias(table_in, bucket_ids), bias_table)
    inputs = tokens.astype(jnp.float32)
    hidden_one, norm_one_pull = jax.vjp(norm_raw, inputs, norm_gains[0])
    hidden_one = hidden_one.astype(jnp.bfloat16)
    queries = product(hidden_one, w_query).astype(jnp.bfloat16)
    keys_in = product(hidden_one, w_key).astype(jnp.bfloat16)
    values_in = product(hidden_one, w_value).astype(jnp.bfloat16)

    def attend_one(packed):
        seq_query, seq_key, seq_value, length = packed
        scores = masked_scores(seq_query, seq_key, rel_bias, length)
        row_max = jnp.max(scores, axis=-1, keepdims=True)
        exp_scores = jnp.exp(scores - row_max)
        totals = jnp.sum(exp_scores, axis=-1, keepdims=True)
        attn_probs = (exp_scores / totals).astype(jnp.bfloat16)
        context = jnp.einsum(
            "hqk,khd->qhd", attn_probs, seq_value, preferred_element_type=jnp.float32
        )
        return (context, row_max + jnp.log(totals))

    context, log_sums = lax.map(
        attend_one, (by_seq(queries), by_seq(keys_in), by_seq(values_in), valid_len)
    )
    context = to_rows(context)
    resid = inputs + product(context, w_out)
    hidden_two, norm_two_pull = jax.vjp(norm_raw, resid, norm_gains[1])
    hidden_two = hidden_two.astype(jnp.bfloat16)
    pre_act = contract_cols(hidden_two, w_in)
    active_full, act_pull = jax.vjp(smooth_act, pre_act)
    active = active_full.astype(jnp.bfloat16)
    block_out = (resid + product(active, w_down)).astype(jnp.bfloat16)
    first_seq = (lax.axis_index("dp") * devices + my_index) * seq_dev
    seq_ids = first_seq + jnp.arange(seq_dev, dtype=jnp.int32)
    task_ends = jnp.cumsum(task_sizes)
    task_count = task_sizes.shape[0]
    task_of = jnp.sum((task_ends[None, :] <= seq_ids[:, None]).astype(jnp.int32), axis=1)
    size_of = jnp.sum(
        jnp.where(
            task_of[:, None] == jnp.arange(task_count, dtype=jnp.int32)[None, :],
            task_sizes[None, :],
            0,
        ),
        axis=1,
    )
    seq_weight = jnp.float32(seq_dev * replicas * devices) / (
        jnp.float32(task_count) * size_of.astype(jnp.float32)
    )
    back_out = (
        cotangent.astype(jnp.float32).reshape(seq_dev, LEN, model_width) * seq_weight[:, None, None]
    ).reshape(-1, model_width)
    w_query, w_key, w_value, w_out, w_in, w_down = rebuild(
        lax.all_gather(sent_shard, "fsdp", axis=0, tiled=True)
    )
    down_back = back_out.astype(jnp.bfloat16)
    grad_down = contract_rows(active, down_back)
    act_back = contract_cols(down_back, w_down)
    (pre_full,) = act_pull(act_back)
    pre_back = pre_full.astype(jnp.bfloat16)
    grad_in = contract_rows(pre_back, hidden_two)
    resid_part, gain_two = norm_two_pull(product(pre_back, w_in))
    resid_back = back_out + resid_part
    out_back = resid_back.astype(jnp.bfloat16)
    grad_out = contract_rows(context, out_back)
    context_back = contract_cols(out_back, w_out).astype(jnp.bfloat16)

    def attend_back(score_sum, packed):
        seq_query, seq_key, seq_value, seq_back, length, log_sum = packed
        scores = masked_scores(seq_query, seq_key, rel_bias, length)
        attn_probs = jnp.exp(scores - log_sum)
        value_grad = jnp.einsum(
            "hqk,qhd->khd",
            attn_probs.astype(jnp.bfloat16),
            seq_back,
            preferred_element_type=jnp.float32,
        )
        prob_grad = jnp.einsum(
            "qhd,khd->hqk", seq_back, seq_value, preferred_element_type=jnp.float32
        )
        score_back = (
            attn_probs * (prob_grad - jnp.sum(attn_probs * prob_grad, axis=-1, keepdims=True))
        ).astype(jnp.bfloat16)
        query_grad = jnp.einsum(
            "hqk,khd->qhd", score_back, seq_key, preferred_element_type=jnp.float32
        )
        key_grad = jnp.einsum(
            "hqk,qhd->khd", score_back, seq_query, preferred_element_type=jnp.float32
        )
        return (score_sum + score_back.astype(jnp.float32), (query_grad, key_grad, value_grad))

    score_sum, (query_grad, key_grad, value_grad) = lax.scan(
        attend_back,
        jnp.zeros_like(rel_bias),
        (
            by_seq(queries),
            by_seq(keys_in),
            by_seq(values_in),
            by_seq(context_back),
            valid_len,
            log_sums,
        ),
    )
    query_back = to_rows(query_grad)
    key_back = to_rows(key_grad)
    value_back = to_rows(value_grad)
    grad_query = contract_rows(hidden_one, query_back)
    grad_key = contract_rows(hidden_one, key_back)
    grad_value = contract_rows(hidden_one, value_back)
    hidden_back = (
        contract_cols(query_back, w_query)
        + contract_cols(key_back, w_key)
        + contract_cols(value_back, w_value)
    )
    input_part, gain_one = norm_one_pull(hidden_back)
    grad_input = resid_back + input_part
    (table_grad,) = bias_pull(score_sum)
    grad_rows = jnp.concatenate(
        [grad_query, grad_key, grad_value, grad_out, grad_in, grad_down], axis=0
    )
    slotted = jnp.where(
        filled[:, None, None] > 0, grad_rows.reshape(-1, BROWS, model_width)[source], 0.0
    ).reshape(-1, model_width)
    owned_grads = lax.psum_scatter(slotted, "fsdp", scatter_dimension=0, tiled=True)
    grad_slots = lax.psum(owned_grads, "dp")
    grad_gains, grad_table = lax.psum((jnp.stack([gain_one, gain_two]), table_grad), ("dp", "fsdp"))
    step_value = jnp.float32(OPT_STEP)
    first_new, second_new, master_new = adamw_step(
        master_slots, grad_slots, first_slots, second_slots, step_value, LEARN_RATE
    )
    gains_first_new, gains_second_new, gains_new = adamw_step(
        norm_gains, grad_gains, gains_first, gains_second, step_value, SMALL_RATE
    )
    table_first_new, table_second_new, table_new = adamw_step(
        bias_table, grad_table, table_first, table_second, step_value, SMALL_RATE
    )
    return (
        block_out,
        grad_input,
        grad_slots,
        grad_gains,
        grad_table,
        first_new,
        second_new,
        master_new,
        master_new.astype(jnp.bfloat16),
        gains_first_new,
        gains_second_new,
        gains_new,
        table_first_new,
        table_second_new,
        table_new,
    )


def solution(mesh):
    in_specs = (
        P(("dp", "fsdp"), None),
        P(("dp", "fsdp"), None),
        P("fsdp", None),
        P("fsdp", None),
        P("fsdp", None),
        P(),
        P(),
        P(),
        P(),
        P(),
        P(),
        P(),
        P(("dp", "fsdp")),
        P(),
        P(),
    )
    out_specs = (
        P(("dp", "fsdp"), None),
        P(("dp", "fsdp"), None),
        P("fsdp", None),
        P(),
        P(),
        P("fsdp", None),
        P("fsdp", None),
        P("fsdp", None),
        P("fsdp", None),
        P(),
        P(),
        P(),
        P(),
        P(),
        P(),
    )
    fast = dict(mesh.shape) == {"dp": 2, "fsdp": CHIPS}
    body = fast_body if fast else plain_body
    return jax.shard_map(
        body, mesh=mesh, in_specs=in_specs, out_specs=out_specs, check_vma=False)
```
